128 devices in a mesh: shell: 16 (over y, x), order: 8 (over z, core).
Axes of the slice: x: 4, y: 4, z: 4, core: 2. Of those that a mesh axis runs over, the one named last changes fastest.
Arguments:
- velocity: bfloat16 [3, 32, 2, 512, 512], P(None, 'shell', None, 'order'), may hold values from -6 to 6
- vorticity: bfloat16 [3, 32, 2, 512, 512], P(None, 'shell', None, 'order'), may hold values from -6 to 6
- magnetic: bfloat16 [3, 32, 2, 512, 512], P(None, 'shell', None, 'order'), may hold values from -6 to 6
- current: bfloat16 [3, 32, 2, 512, 512], P(None, 'shell', None, 'order'), may hold values from -6 to 6
- potential: bfloat16 [3, 32, 2, 512, 512], P(None, 'shell', None, 'order'), may hold values from -6 to 6
- order_slots: int32 [512], replicated, may hold values from 0 to 511, as said below
- legendre_values: bfloat16 [256, 513, 256], P('order'), as said below
- block_lengths: int32 [4], replicated, may hold values from 1 to 16, 32 in all
- coupling: float32 [2, 32], P(None, 'shell'), may hold values from 50 to 500
- angular: float32 [2, 32], P(None, 'shell'), may hold values from 3.8146973e-05 to 0.00038146973
Outputs:
- velocity_next: float32 [3, 32, 2, 512, 512], P(None, 'shell', None, 'order')
- potential_next: float32 [3, 32, 2, 512, 512], P(None, 'shell', None, 'order')
The draws below stay inside these ranges and needn't reach their ends.
Inputs may be any that keep to these rules, and one draw needn't show every extreme that they name: `order_slots`: slots 2 i and 2 i + 1 hold an order m < 256 and 511 - m; every order from 0 to 511 is held once. `legendre_values`: the orthonormal associated Legendre functions (the squared harmonic integrates to 1 over the sphere), without Condon-Shortley phase, of the orders in order_slots, at cos(theta_j), packed as the first step says; entries beyond a slot's degrees are unused. `block_lengths`: the 4 lengths sum to 32; the largest is exactly 16.
All inputs are finite; a program needn't handle non-finite values.
Results may differ from the reference program's by a relative error of at most 0.004.
Values may be sent and summed in bfloat16 or wider, within the bound.
No kernel may reach another device: no remote copies, remote signals or barrier semaphores. Data moves between devices by JAX's collectives and lax.ppermute only.
A program may use at most 128 MiB of HBM per device.

```python
import math
import jax
import jax.numpy as jnp
import numpy as np
from jax import lax

L = 512
NLAT = 512
NPHI = 1024
NBLK = 4
R = 32
NH = 256


def shared_orders(key):
    first_half = jax.random.permutation(jax.random.fold_in(key, 7), L // 2).astype(jnp.int32)
    return jnp.stack([first_half, L - 1 - first_half], axis=1).reshape(L).astype(jnp.int32)


def legendre_full(orders, degrees_count, lat_count):
    half_rows = lat_count // 2
    colatitude = math.pi * (jnp.arange(half_rows, dtype=jnp.float32) + 0.5) / lat_count
    cosines = jnp.cos(colatitude)[None, :]
    sines = jnp.sin(colatitude)[None, :]
    order_real = orders.astype(jnp.float32)[:, None]
    order_int = orders.astype(jnp.int32)[:, None]
    log_start = 0.5 * (jnp.log((2.0 * order_real + 1.0) / (4.0 * math.pi)) + lax.lgamma(order_real + 0.5) - lax.lgamma(order_real + 1.0) - 0.5 * math.log(math.pi)) + order_real * jnp.log(sines)
    start_value = jnp.exp(log_start)
    second = jnp.sqrt(2.0 * order_real + 3.0) * cosines * start_value

    def advance(carry, degree):
        previous, before_last = carry
        degree_real = degree.astype(jnp.float32)
        raise_factor = jnp.sqrt((4.0 * degree_real * degree_real - 1.0) / jnp.maximum(degree_real * degree_real - order_real * order_real, 1.0))
        drop_factor = jnp.sqrt(jnp.maximum((degree_real - 1.0) ** 2 - order_real * order_real, 0.0) / jnp.maximum(4.0 * (degree_real - 1.0) ** 2 - 1.0, 1.0))
        general = raise_factor * (cosines * previous - drop_factor * before_last)
        result = jnp.where(degree < order_int, 0.0, jnp.where(degree == order_int, start_value, jnp.where(degree == order_int + 1, second, general)))
        return ((result, previous), result)
    zero_rows = jnp.zeros((orders.shape[0], half_rows), jnp.float32)
    _, legendre = lax.scan(advance, (zero_rows, zero_rows), jnp.arange(degrees_count, dtype=jnp.int32))
    return legendre


def draw_order_slots(key, part):
    return shared_orders(key)


def draw_legendre_values(key, part):
    orders = shared_orders(key)
    full = jnp.transpose(legendre_full(orders, L, NLAT), (1, 0, 2))
    pair_rows = full.reshape(L // 2, 2, L, NLAT // 2)
    lower = orders.reshape(L // 2, 2)[:, 0]
    packed_ids = jnp.arange(L + 1, dtype=jnp.int32)[None, :]
    even_index = jnp.clip(lower[:, None] + packed_ids, 0, L - 1)
    odd_index = jnp.clip(packed_ids - 1, 0, L - 1)
    even_vals = jnp.take_along_axis(pair_rows[:, 0], even_index[:, :, None], axis=1)
    odd_vals = jnp.take_along_axis(pair_rows[:, 1], odd_index[:, :, None], axis=1)
    use_even = packed_ids[:, :, None] < (L - lower)[:, None, None]
    return jnp.where(use_even, even_vals, odd_vals).astype(jnp.float32).astype(jnp.bfloat16)


def degree_envelope(base_level, low_gain, length):
    degree_real = jnp.arange(L, dtype=jnp.float32)
    return base_level + low_gain * jnp.exp(-degree_real / length)


def spectral_values(key):
    envelope = degree_envelope(0.8, 1.6, 8.0)
    values = jax.random.truncated_normal(key, -2.5, 2.5, (3, R, 2, L, L), jnp.float32) * envelope
    return values.astype(jnp.bfloat16)


def draw_velocity(key, part):
    key = jax.random.fold_in(key, 21)
    return spectral_values(key)


def draw_vorticity(key, part):
    key = jax.random.fold_in(key, 22)
    return spectral_values(key)


def draw_magnetic(key, part):
    key = jax.random.fold_in(key, 23)
    return spectral_values(key)


def draw_current(key, part):
    key = jax.random.fold_in(key, 24)
    return spectral_values(key)


def draw_potential(key, part):
    key = jax.random.fold_in(key, 25)
    return spectral_values(key)


def levels(rng, extent, shards, smallest, largest):
    loudness, own = 1.0, jax.random.fold_in(rng, 6)
    for axis_at, parts in shards:
        heights = jnp.exp(jax.random.uniform(jax.random.fold_in(own, axis_at), (parts,), jnp.float32, smallest / len(shards), largest / len(shards)))
        loudness = loudness * jnp.repeat(heights, extent[axis_at] // parts).reshape([-1 if axis == axis_at else 1 for axis in range(len(extent))])
    return loudness


def split_up(amount, total, limit, skew):
    weights = [(1 << 20) // math.isqrt(grade ** skew) + 1 for grade in range(2, amount + 1)]
    rest, given = total - limit - (amount - 1), [1] * (amount - 1)
    while rest > 0:
        movable = [i for i in range(amount - 1) if given[i] < limit]
        mass, remaining = sum([weights[i] for i in movable]), rest
        for i in movable:
            more = min(limit - given[i], max(1, remaining * weights[i] // mass), rest)
            given[i] = given[i] + more
            rest = rest - more
    return np.array([limit] + given)


def ragged_sizes(stream_key, number_of, total, limit, lean):
    if number_of == 2:
        one = jax.random.randint(stream_key, (), max(1, total - limit), min(limit, total - 1) + 1)
        return jnp.stack([one, total - one])
    tallies = jnp.asarray(split_up(number_of, total, limit, lean), jnp.int32)
    couples = (number_of - 1) // 2
    donor, receiver = tallies[1:1 + 2 * couples:2], tallies[2:2 + 2 * couples:2]
    room = jnp.minimum(donor - 1, limit - receiver)
    shifted = jax.random.randint(jax.random.fold_in(stream_key, 1), (couples,), 0, 1 << 20) % (room + 1)
    tallies = tallies.at[1:1 + 2 * couples:2].set(donor - shifted).at[2:2 + 2 * couples:2].set(receiver + shifted)
    return tallies[jax.random.permutation(jax.random.fold_in(stream_key, 2), number_of)]


def setup_inputs(seed: int = 0) -> dict:
    arg_keys = jax.random.split(jax.random.key(seed), 11)
    return {
        "velocity": draw_velocity(jax.random.fold_in(arg_keys[10], 71), 0),
        "vorticity": draw_vorticity(jax.random.fold_in(arg_keys[10], 71), 0),
        "magnetic": draw_magnetic(jax.random.fold_in(arg_keys[10], 71), 0),
        "current": draw_current(jax.random.fold_in(arg_keys[10], 71), 0),
        "potential": draw_potential(jax.random.fold_in(arg_keys[10], 71), 0),
        "order_slots": draw_order_slots(jax.random.fold_in(arg_keys[10], 71), 0),
        "legendre_values": draw_legendre_values(jax.random.fold_in(arg_keys[10], 71), 0),
        "block_lengths": ragged_sizes(arg_keys[7], NBLK, R, R // 2, 1).astype(jnp.int32),
        "coupling": jnp.clip(jnp.exp(math.log(500.0) - 2.3025851 * jax.random.uniform(arg_keys[8], (2, R), jnp.float32) ** levels(arg_keys[8], (2, R), ((1, 16),), -0.2, 0.2)), 50.0, 500.0),
        "angular": jnp.clip(jnp.exp(math.log(0.00038146973) - 2.3025851 * jax.random.uniform(arg_keys[9], (2, R), jnp.float32) ** levels(arg_keys[9], (2, R), ((1, 16),), -0.2, 0.2)), 3.814697265625e-05, 0.00038146973),
    }


time_step = 0.5
rotation_rate = 2.0

def unpack_table(packed, orders):
    pair_count = packed.shape[0]
    degree_count = packed.shape[1] - 1
    lower = orders.astype(jnp.int32).reshape(pair_count, 2)[:, 0]
    padded = jnp.concatenate([jnp.zeros((pair_count, degree_count, packed.shape[2]), packed.dtype), packed], axis=1)
    starts = (degree_count - lower).astype(jnp.int32)
    even_rows = jax.vmap(lambda row, begin: lax.dynamic_slice_in_dim(row, begin, degree_count, 0))(padded, starts)
    degree_ids = jnp.arange(degree_count, dtype=jnp.int32)
    odd_rows = jnp.where(degree_ids[None, :, None] >= (degree_count - 1 - lower)[:, None, None], packed[:, 1:, :], jnp.zeros_like(packed[:, 1:, :]))
    table = jnp.stack([even_rows, odd_rows], axis=1).reshape(2 * pair_count, degree_count, packed.shape[2])
    return jnp.transpose(table, (1, 0, 2))

def parity_sign(orders, degrees_count):
    parity = (jnp.arange(degrees_count, dtype=jnp.int32)[None, :] + orders.astype(jnp.int32)[:, None]) % 2
    return 1.0 - 2.0 * parity.astype(jnp.float32)

def latitude_weight(row_ids, lat_count, degrees_count):
    colatitude = math.pi * (row_ids.astype(jnp.float32) + 0.5) / lat_count
    return math.sqrt(2.0 * math.pi) * degrees_count * math.pi / lat_count * jnp.sin(colatitude)

def cross_product(first, second):
    return jnp.stack([first[1] * second[2] - first[2] * second[1], first[2] * second[0] - first[0] * second[2], first[0] * second[1] - first[1] * second[0]])

def nonlinear_terms(field_grid):
    flow_grid = field_grid[0:3]
    vorticity_grid = field_grid[3:6]
    magnetic_grid = field_grid[6:9]
    current_grid = field_grid[9:12]
    rotation = jnp.stack([rotation_rate * flow_grid[1], -rotation_rate * flow_grid[0], jnp.zeros_like(flow_grid[0])])
    momentum = cross_product(flow_grid, vorticity_grid) + cross_product(current_grid, magnetic_grid) + rotation
    induction = cross_product(flow_grid, magnetic_grid)
    return jnp.concatenate([momentum, induction], axis=0)

def round_trip(values):
    return lax.optimization_barrier(values.astype(jnp.bfloat16)).astype(jnp.float32)

def reference(velocity, vorticity, magnetic, current, potential, order_slots, legendre_values, block_lengths, coupling, angular):
    legendre = unpack_table(legendre_values, order_slots)
    legendre_wide = legendre.astype(jnp.float32)
    parity = parity_sign(order_slots, L)
    weight = latitude_weight(jnp.arange(NH, dtype=jnp.int32), NLAT, L)
    spectral = jnp.concatenate([velocity, vorticity, magnetic, current], axis=0)

    def one_shell(shell_spec):
        zero_block = jnp.zeros_like(shell_spec)
        even_part = jnp.where(parity > 0, shell_spec, zero_block).astype(jnp.float32)
        odd_part = jnp.where(parity > 0, zero_block, shell_spec).astype(jnp.float32)
        even_sum = jnp.einsum('cpkl,lkj->cpkj', even_part, legendre_wide)
        odd_sum = jnp.einsum('cpkl,lkj->cpkj', odd_part, legendre_wide)
        hemispheres = round_trip(jnp.stack([even_sum + odd_sum, even_sum - odd_sum], axis=1))
        real_rows = jnp.zeros((12, 2, NH, NPHI // 2 + 1), jnp.float32).at[:, :, :, order_slots].set(jnp.swapaxes(hemispheres[:, :, 0], 2, 3))
        imag_rows = jnp.zeros((12, 2, NH, NPHI // 2 + 1), jnp.float32).at[:, :, :, order_slots].set(jnp.swapaxes(hemispheres[:, :, 1], 2, 3))
        field_grid = jnp.fft.irfft(lax.complex(real_rows, imag_rows), n=NPHI, axis=-1) * (NPHI * math.sqrt(2.0 * math.pi) / L)
        products = nonlinear_terms(field_grid)
        spectrum = jnp.fft.rfft(products, axis=-1)[..., order_slots]
        scaling = (weight / NPHI)[:, None]
        real_part = round_trip(jnp.real(spectrum) * scaling)
        imag_part = round_trip(jnp.imag(spectrum) * scaling)
        northern = jnp.einsum('pcjk,lkj->cpkl', jnp.stack([real_part[:, 0], imag_part[:, 0]]), legendre_wide)
        southern = jnp.einsum('pcjk,lkj->cpkl', jnp.stack([real_part[:, 1], imag_part[:, 1]]), legendre_wide)
        return northern + parity * southern
    analysed = lax.map(one_shell, jnp.moveaxis(spectral, 1, 0))
    shell_ids = jnp.arange(R, dtype=jnp.int32)
    starts = (jnp.cumsum(block_lengths) - block_lengths).astype(jnp.int32)
    is_start = jnp.any(shell_ids[:, None] == starts[None, :], axis=1)
    below = jnp.where(is_start[None, :], 0.0, coupling)
    above = jnp.concatenate([below[:, 1:], jnp.zeros((2, 1), below.dtype)], axis=1)
    degree_real = jnp.arange(L, dtype=jnp.float32)
    degree_term = degree_real * (degree_real + 1.0)
    diagonal = 1.0 + below[:, :, None] + above[:, :, None] + angular[:, :, None] * degree_term
    states = (velocity, potential)
    results = []
    for field_index in range(2):
        state_rows = jnp.moveaxis(states[field_index], 1, 0)
        term_rows = analysed[:, 3 * field_index:3 * field_index + 3]

        def forward(carry, inputs):
            carried, running = carry
            state_row, term_row, below_row, above_row, diagonal_row = inputs
            values = state_row.astype(jnp.float32) + time_step * term_row
            denominator = diagonal_row - below_row * carried
            slopes = above_row / denominator
            running = (values + below_row * running) / denominator
            return ((slopes, running), (slopes, running))
        initial = (jnp.zeros((L,), jnp.float32), jnp.zeros(term_rows.shape[1:], jnp.float32))
        _, (slope_rows, reduced) = lax.scan(forward, initial, (state_rows, term_rows, below[field_index], above[field_index], diagonal[field_index]))

        def backward(carried, inputs):
            slope_row, reduced_row = inputs
            carried = reduced_row + slope_row * carried
            return (carried, carried)
        _, solved = lax.scan(backward, jnp.zeros(term_rows.shape[1:], jnp.float32), (slope_rows, reduced), reverse=True)
        results.append(jnp.moveaxis(solved, 0, 1))
    return (results[0], results[1])
```

```python
import math

import jax
import jax.numpy as jnp
import numpy as np
from jax import lax
from jax.experimental import pallas as pl
from jax.experimental.pallas import tpu as pltpu
from jax.sharding import PartitionSpec as P

L = 512
NLAT = 512
NPHI = 1024
NH = 256
f32 = jnp.float32
bf16 = jnp.bfloat16
MIB = 1 << 20


def natural_tables():
    phases = (np.arange(L)[:, None] * np.arange(NPHI)[None, :]) % NPHI
    angles = 2.0 * np.pi * phases / NPHI
    rows = np.stack([np.cos(angles), -np.sin(angles)], axis=1)
    weight = np.where(np.arange(L) == 0, 1.0, 2.0) * (math.sqrt(2.0 * math.pi) / L)
    synthesis = (rows * weight[:, None, None]).reshape(2 * L, NPHI)
    analysis = (rows / NPHI).reshape(2 * L, NPHI)
    return synthesis.T.astype(jnp.bfloat16), analysis.astype(jnp.bfloat16)


def load(ref, rows):
    return jnp.concatenate([ref[q, rows, :] for q in range(ref.shape[0])], axis=1)


def store(ref, rows, value):
    for q in range(ref.shape[0]):
        ref[q, rows, :] = value[:, q * 128 : q * 128 + 128]


def synthesis_kernel(lower, vel, vor, mag, cur, table, out, xs, ys):
    step = pl.program_id(0)
    for a, ref in enumerate((vel, vor, mag, cur)):
        for c in range(3):
            for s in range(2):
                for p in range(2):
                    row = (s * 24 + (a * 3 + c) * 2 + p) * 16
                    store(xs, pl.ds(row, 16), ref[c, s, p].astype(f32))
    r = lax.broadcasted_iota(jnp.int32, (1, L), 1)
    sign_a = (1 - 2 * (r & 1)).astype(f32)

    def one_pair(i, _):
        m = lower[step * 8 + i]
        a = load(xs, pl.ds(2 * i, 48, stride=16))
        b = load(xs, pl.ds(2 * i + 1, 48, stride=16))
        a = pltpu.roll(a, (L - m) & (L - 1), 1)
        b_last = b[:, L - 1 : L]
        b = pltpu.roll(b, 1, 1)
        is_a = r < L - m
        sign_b = (1 - 2 * ((r + m) & 1)).astype(f32)
        a = jnp.where(is_a, a, 0.0)
        b = jnp.where(is_a, 0.0, b)
        lhs = jnp.concatenate([a, a * sign_a, b, b * sign_b], axis=0).astype(bf16)
        res = jnp.dot(lhs, table[i, 0:L, :], preferred_element_type=f32)
        last = b_last * table[i, L : L + 1, :].astype(f32)
        last_sign = (1 - 2 * (m & 1)).astype(f32)
        b_n = res[96:144] + last
        b_s = res[144:192] + last * last_sign
        for k, parts in ((2 * i, (res[0:48], res[48:96])), (2 * i + 1, (b_n, b_s))):
            for h in range(2):
                for s in range(2):
                    rows = pl.ds((s * 2 + h) * 384 + k, 24, stride=16)
                    store(ys, rows, parts[h][s * 24 : s * 24 + 24])
        return 0

    lax.fori_loop(0, 8, one_pair, 0)
    for sh in range(4):
        for jh in range(2):
            piece = ys[jh, sh * 384 : sh * 384 + 384, :]
            out[sh * 2 + jh] = piece.reshape(24, 16, 128).astype(bf16)


def legendre_synthesis(lower, velocity, vorticity, magnetic, current, table):
    field = pl.BlockSpec((3, 2, 2, 16, L), lambda g, low: (0, 0, 0, g, 0))
    return pl.pallas_call(
        synthesis_kernel,
        grid_spec=pltpu.PrefetchScalarGridSpec(
            num_scalar_prefetch=1,
            grid=(4,),
            in_specs=[field] * 4 + [pl.BlockSpec((8, L + 1, NH), lambda g, low: (g, 0, 0))],
            out_specs=pl.BlockSpec((8, 24, 16, 128), lambda g, low: (0, 0, g, 0)),
            scratch_shapes=[pltpu.VMEM((4, 768, 128), f32), pltpu.VMEM((2, 1536, 128), f32)],
        ),
        out_shape=jax.ShapeDtypeStruct((8, 24, 64, 128), bf16),
        compiler_params=pltpu.CompilerParams(vmem_limit_bytes=40 * MIB),
        cost_estimate=pl.CostEstimate(flops=int(1.6e9), bytes_accessed=15 * MIB, transcendentals=0),
        name="legendre_synthesis",
    )(lower, velocity, vorticity, magnetic, current, table)


def state_kernel(kappa, angular, vel, pot, out, scr):
    for f, ref in enumerate((vel, pot)):
        for c in range(3):
            for s in range(2):
                for p in range(2):
                    x = ref[c, s, p].astype(f32)
                    row = s * 48 + ((f * 3 + c) * 2 + p) * 4
                    for d in range(4):
                        scr[d, row : row + 4, :] = x[4 * d : 4 * d + 4]
    lane = lax.broadcasted_iota(jnp.int32, (1, L), 1)
    for kind, ref in enumerate((kappa, angular)):
        for f in range(2):
            for s in range(2):
                value = jnp.full((1, L), ref[f, s], f32)
                high = value.astype(bf16).astype(f32)
                rest = value - high
                mid = rest.astype(bf16).astype(f32)
                low = rest - mid
                line = jnp.where(lane < 128, high, jnp.where(lane < 256, mid, low))
                row = 96 + (kind * 2 + f) * 2 + s
                for d in range(4):
                    scr[d, row : row + 1, :] = line
    scr[:, 104:112, :] = jnp.zeros((4, 8, L), f32)
    out[...] = scr[...].astype(bf16)


def state_to_send(kappa, angular, velocity, potential):
    field = pl.BlockSpec((3, 2, 2, 16, L), lambda g: (0, 0, 0, g, 0))
    small = pl.BlockSpec(memory_space=pltpu.SMEM)
    return pl.pallas_call(
        state_kernel,
        grid=(4,),
        in_specs=[small, small, field, field],
        out_specs=pl.BlockSpec((4, 112, L), lambda g: (g, 0, 0)),
        out_shape=jax.ShapeDtypeStruct((16, 112, L), bf16),
        scratch_shapes=[pltpu.VMEM((4, 112, L), f32)],
        compiler_params=pltpu.CompilerParams(vmem_limit_bytes=24 * MIB),
        cost_estimate=pl.CostEstimate(flops=10**6, bytes_accessed=4 * MIB, transcendentals=0),
        name="state_to_send",
    )(kappa, angular, velocity, potential)


def grid_kernel(lat, syn, ana, weight, out, wide, prod, acc):
    step = pl.program_id(0)

    @pl.when(step == 0)
    def _():
        for c in range(12):
            wide[:, c * 128 : c * 128 + 128] = lat[:, 2 * c : 2 * c + 2].reshape(1024, 128)

    g = jnp.dot(syn[...], wide[...], preferred_element_type=f32)
    x = [g[:, c * 128 : c * 128 + 128] for c in range(12)]
    u, w, b, j = x[0:3], x[3:6], x[6:9], x[9:12]

    def cross(p, q):
        return [
            p[1] * q[2] - p[2] * q[1],
            p[2] * q[0] - p[0] * q[2],
            p[0] * q[1] - p[1] * q[0],
        ]

    uw, jb, ub = cross(u, w), cross(j, b), cross(u, b)
    terms = [uw[0] + jb[0] + 2.0 * u[1], uw[1] + jb[1] - 2.0 * u[0], uw[2] + jb[2]] + ub
    for c in range(6):
        prod[:, c * 128 : c * 128 + 128] = terms[c].astype(bf16)
    part = jnp.dot(ana[...], prod[...], preferred_element_type=f32)

    @pl.when(step == 0)
    def _():
        acc[...] = part

    @pl.when(step > 0)
    def _():
        acc[...] += part

    @pl.when(step == pl.num_programs(0) - 1)
    def _():
        wt = weight[...]
        for c in range(6):
            out[:, c * 128 : c * 128 + 128] = (acc[:, c * 128 : c * 128 + 128] * wt).astype(bf16)


def grid_stage(lat, syn, ana, weight):
    rows = 256
    return pl.pallas_call(
        grid_kernel,
        grid=(NPHI // rows,),
        in_specs=[
            pl.BlockSpec((8, 24, 64, 128), lambda i: (0, 0, 0, 0)),
            pl.BlockSpec((rows, 1024), lambda i: (i, 0)),
            pl.BlockSpec((1024, rows), lambda i: (0, i)),
            pl.BlockSpec((1, 128), lambda i: (0, 0)),
        ],
        out_specs=pl.BlockSpec((1024, 768), lambda i: (0, 0)),
        out_shape=jax.ShapeDtypeStruct((1024, 768), bf16),
        scratch_shapes=[
            pltpu.VMEM((1024, 1536), bf16),
            pltpu.VMEM((rows, 768), bf16),
            pltpu.VMEM((1024, 768), f32),
        ],
        compiler_params=pltpu.CompilerParams(vmem_limit_bytes=48 * MIB),
        cost_estimate=pl.CostEstimate(flops=int(4.8e9), bytes_accessed=9 * MIB, transcendentals=0),
        name="grid_stage",
    )(lat, syn, ana, weight)


def prepare_kernel(place, lower, table, extra, table_out, factors, scr):
    l_row = lax.broadcasted_iota(jnp.int32, (1, L), 1)
    for i in range(2):
        m = lower[place[0] * 2 + i]
        scr[...] = table[i].astype(f32)
        a = jnp.transpose(scr[0:L, :])
        a = pltpu.roll(a, m, 1)
        table_out[2 * i] = jnp.where(l_row >= m, a, 0.0).astype(bf16)
        b = jnp.transpose(scr[1 : L + 1, :])
        table_out[2 * i + 1] = jnp.where(l_row >= L - 1 - m, b, 0.0).astype(bf16)
    degree = l_row.astype(f32)
    degree_term = degree * (degree + 1.0)
    below, angle = [[], []], [[], []]
    for d in range(16):
        x = extra[d].astype(f32)
        value = (x[0:8, 0:128] + x[0:8, 128:256]) + x[0:8, 256:384]
        value = jnp.concatenate([value] * 4, axis=1)
        for f in range(2):
            for s in range(2):
                below[f].append(value[f * 2 + s : f * 2 + s + 1])
                angle[f].append(value[4 + f * 2 + s : 4 + f * 2 + s + 1])
    for f in range(2):
        carried = jnp.zeros((1, L), f32)
        for s in range(32):
            under = below[f][s]
            above = below[f][s + 1] if s < 31 else jnp.zeros((1, L), f32)
            diagonal = 1.0 + under + above + angle[f][s] * degree_term
            inverse = 1.0 / (diagonal - under * carried)
            carried = above * inverse
            row = f * 32 + s
            factors[0, row : row + 1, :] = inverse
            factors[1, row : row + 1, :] = under * inverse
            factors[2, row : row + 1, :] = carried


def prepare_solve(place, lower, table, state):
    return pl.pallas_call(
        prepare_kernel,
        grid_spec=pltpu.PrefetchScalarGridSpec(
            num_scalar_prefetch=2,
            grid=(1,),
            in_specs=[
                pl.BlockSpec((2, L + 1, NH), lambda g, place, low: (place[0], 0, 0)),
                pl.BlockSpec((16, 16, L), lambda g, place, low: (0, 6, 0)),
            ],
            out_specs=[
                pl.BlockSpec((4, NH, L), lambda g, place, low: (0, 0, 0)),
                pl.BlockSpec((3, 64, L), lambda g, place, low: (0, 0, 0)),
            ],
            scratch_shapes=[pltpu.VMEM((L + 1, NH), f32)],
        ),
        out_shape=[
            jax.ShapeDtypeStruct((4, NH, L), bf16),
            jax.ShapeDtypeStruct((3, 64, L), f32),
        ],
        compiler_params=pltpu.CompilerParams(vmem_limit_bytes=24 * MIB),
        cost_estimate=pl.CostEstimate(flops=10**7, bytes_accessed=3 * MIB, transcendentals=0),
        name="prepare_solve",
    )(place, lower, table, state)


def solve_kernel(place, lower, coef, state, table, factors, out, cs, lhs, rhs):
    for c in range(6):
        cs[c] = coef[:, c * 128 : c * 128 + 128].astype(f32)
    l_row = lax.broadcasted_iota(jnp.int32, (1, L), 1)
    for k in range(4):
        m = lower[place[0] * 2 + k // 2]
        order = m if k % 2 == 0 else L - 1 - m
        half_sign = 0.5 * (1 - 2 * ((l_row + order) & 1)).astype(f32)
        for h in range(2):
            for c in range(6):
                for p in range(2):
                    row = ((h * 6 + c) * 2 + p) * 32
                    for jh in range(2):
                        start = h * 16 + jh * 8 + k * 2 + p
                        lhs[k % 2, row : row + 32, jh * 128 : jh * 128 + 128] = cs[
                            c, pl.ds(start, 32, stride=32), :
                        ].astype(bf16)
        res = jnp.dot(lhs[k % 2], table[k], preferred_element_type=f32)
        half = 0.5 * res[0:384] + half_sign * res[384:768]
        for cp in range(12):
            store(rhs, pl.ds(cp * 4 + k, 32, stride=48), half[cp * 32 : cp * 32 + 32])

    def factor(kind, f, s):
        return factors[kind, pl.ds(f * 32 + s, 1), :]

    def forward(d, running):
        running = list(running)
        block = state[d].astype(f32)
        for s2 in range(2):
            s = 2 * d + s2
            for f in range(2):
                base = s * 48 + f * 24
                value = load(rhs, pl.ds(base, 24)) + block[s2 * 48 + f * 24 : s2 * 48 + f * 24 + 24]
                running[f] = factor(0, f, s) * value + factor(1, f, s) * running[f]
                store(rhs, pl.ds(base, 24), running[f])
        return tuple(running)

    zero = jnp.zeros((24, L), f32)
    lax.fori_loop(0, 16, forward, (zero, zero))

    def backward(step, carried):
        d = 15 - step
        carried = list(carried)
        pieces = [None] * 4
        for s2 in (1, 0):
            s = 2 * d + s2
            for f in range(2):
                value = load(rhs, pl.ds(s * 48 + f * 24, 24))
                carried[f] = value + factor(2, f, s) * carried[f]
                pieces[s2 * 2 + f] = carried[f]
        out[d] = jnp.concatenate(pieces, axis=0).astype(bf16)
        return tuple(carried)

    lax.fori_loop(0, 16, backward, (zero, zero))


def analysis_and_solve(place, lower, coef, state, table, factors):
    return pl.pallas_call(
        solve_kernel,
        grid_spec=pltpu.PrefetchScalarGridSpec(
            num_scalar_prefetch=2,
            grid=(1,),
            in_specs=[
                pl.BlockSpec((1024, 768), lambda g, place, low: (0, 0)),
                pl.BlockSpec((16, 96, L), lambda g, place, low: (0, 0, 0)),
                pl.BlockSpec((4, NH, L), lambda g, place, low: (0, 0, 0)),
                pl.BlockSpec((3, 64, L), lambda g, place, low: (0, 0, 0)),
            ],
            out_specs=pl.BlockSpec((16, 96, L), lambda g, place, low: (0, 0, 0)),
            scratch_shapes=[
                pltpu.VMEM((6, 1024, 128), f32),
                pltpu.VMEM((2, 768, NH), bf16),
                pltpu.VMEM((4, 32 * 48, 128), f32),
            ],
        ),
        out_shape=jax.ShapeDtypeStruct((16, 96, L), bf16),
        compiler_params=pltpu.CompilerParams(vmem_limit_bytes=48 * MIB),
        cost_estimate=pl.CostEstimate(flops=int(0.9e9), bytes_accessed=6 * MIB, transcendentals=0),
        name="analysis_and_solve",
    )(place, lower, coef, state, table, factors)


def unpack_kernel(got, out_v, out_p, scr, tmp):
    store(scr, pl.ds(0, 768), got[...].astype(f32).reshape(768, L))
    for f, ref in enumerate((out_v, out_p)):
        for c in range(3):
            for p in range(2):
                for k in range(4):
                    row = ((f * 3 + c) * 2 + p) * 4 + k
                    store(tmp, pl.ds(k, 16, stride=4), load(scr, pl.ds(row, 16, stride=48)))
                ref[c, 0, p] = load(tmp, pl.ds(0, 64))


def unpack_solution(got):
    shape = jax.ShapeDtypeStruct((3, 2, 2, 64, L), f32)
    field = pl.BlockSpec((3, 1, 2, 64, L), lambda s: (0, s, 0, 0, 0))
    return pl.pallas_call(
        unpack_kernel,
        grid=(2,),
        in_specs=[pl.BlockSpec((16, 48, L), lambda s: (0, s, 0))],
        out_specs=[field, field],
        out_shape=[shape, shape],
        scratch_shapes=[pltpu.VMEM((4, 768, 128), f32), pltpu.VMEM((4, 64, 128), f32)],
        compiler_params=pltpu.CompilerParams(vmem_limit_bytes=24 * MIB),
        cost_estimate=pl.CostEstimate(flops=10**6, bytes_accessed=5 * MIB, transcendentals=0),
        name="unpack_solution",
    )(got)


def fourier_tables(order_slots):
    natural_s, natural_a = natural_tables()
    ids = jnp.arange(2 * L, dtype=jnp.int32)
    part = jnp.arange(2, dtype=jnp.int32)
    by_source = order_slots.reshape(8, 1, 64) * 2 + part[None, :, None]
    pick_s = (ids[:, None] == by_source.reshape(1, -1)).astype(bf16)
    syn = jnp.dot(jnp.asarray(natural_s), pick_s, preferred_element_type=f32).astype(bf16)
    slots = order_slots.reshape(8, 16, 4).transpose(1, 0, 2)
    by_target = slots[..., None] * 2 + part
    pick_a = (by_target.reshape(-1, 1) == ids[None, :]).astype(bf16)
    ana = jnp.dot(pick_a, jnp.asarray(natural_a), preferred_element_type=f32).astype(bf16)
    return syn, ana


def body(
    velocity,
    vorticity,
    magnetic,
    current,
    potential,
    order_slots,
    legendre_values,
    block_lengths,
    coupling,
    angular,
):
    order_rank = lax.axis_index("order")
    shell_rank = lax.axis_index("shell")
    lower = lax.dynamic_slice_in_dim(order_slots, order_rank * 64, 64).reshape(32, 2)[:, 0]
    place = shell_rank.reshape(1)
    shell_ids = shell_rank * 2 + jnp.arange(2, dtype=jnp.int32)
    starts = jnp.cumsum(block_lengths) - block_lengths
    is_start = jnp.any(shell_ids[:, None] == starts[None, :], axis=1)
    kappa = jnp.where(is_start[None, :], 0.0, coupling)
    rows = (order_rank & 1) * 128 + jnp.arange(128, dtype=jnp.int32)
    colatitude = math.pi * (rows.astype(f32) + 0.5) / NLAT
    weight = (math.sqrt(2.0 * math.pi) * L * math.pi / NLAT * jnp.sin(colatitude))[None, :]

    latitude = legendre_synthesis(
        lower, velocity, vorticity, magnetic, current, legendre_values
    )
    incoming = lax.all_to_all(latitude, "order", 0, 0, tiled=True)

    order_after, vel_after, pot_after, _ = lax.optimization_barrier(
        (order_slots, velocity, potential, latitude)
    )
    state = state_to_send(kappa, angular, vel_after, pot_after)
    state = lax.all_to_all(state, "shell", 0, 0, tiled=True)
    syn, ana = fourier_tables(order_after)
    table, factors = prepare_solve(place, lower, legendre_values, state)

    coefs = grid_stage(incoming, syn, ana, weight)
    coefs = lax.all_to_all(
        coefs.reshape(128, 8, 768), ("shell", "order"), 0, 0, tiled=True
    ).reshape(1024, 768)
    solved = analysis_and_solve(place, lower, coefs, state, table, factors)
    solved = lax.all_to_all(solved, "shell", 0, 0, tiled=True)
    return tuple(unpack_solution(solved))


def solution(mesh):
    spectral = P(None, "shell", None, "order", None)
    in_specs = (
        spectral,
        spectral,
        spectral,
        spectral,
        spectral,
        P(),
        P("order", None, None),
        P(),
        P(None, "shell"),
        P(None, "shell"),
    )
    return jax.shard_map(
        body, mesh=mesh, in_specs=in_specs, out_specs=(spectral, spectral), check_vma=False
    )
```

```python
import math

import jax
import jax.numpy as jnp
import numpy as np
from jax import lax
from jax.experimental import pallas as pl
from jax.experimental.pallas import tpu as pltpu
from jax.sharding import PartitionSpec as P

L = 512
NLAT = 512
NPHI = 1024
NH = 256
f32 = jnp.float32
bf16 = jnp.bfloat16
MIB = 1 << 20


def natural_tables():
    phases = (np.arange(L)[:, None] * np.arange(NPHI)[None, :]) % NPHI
    angles = 2.0 * np.pi * phases / NPHI
    rows = np.stack([np.cos(angles), -np.sin(angles)], axis=1)
    weight = np.where(np.arange(L) == 0, 1.0, 2.0) * (math.sqrt(2.0 * math.pi) / L)
    synthesis = (rows * weight[:, None, None]).reshape(2 * L, NPHI)
    analysis = (rows / NPHI).reshape(2 * L, NPHI)
    return synthesis.T.astype(jnp.bfloat16), analysis.astype(jnp.bfloat16)


def load(ref, rows):
    return jnp.concatenate([ref[q, rows, :] for q in range(ref.shape[0])], axis=1)


def store(ref, rows, value):
    for q in range(ref.shape[0]):
        ref[q, rows, :] = value[:, q * 128 : q * 128 + 128]


def synthesis_kernel(lower, vel, vor, mag, cur, table, out, xs, ys):
    step = pl.program_id(0)
    for a, ref in enumerate((vel, vor, mag, cur)):
        for c in range(3):
            for s in range(2):
                for p in range(2):
                    row = (s * 24 + (a * 3 + c) * 2 + p) * 16
                    store(xs, pl.ds(row, 16), ref[c, s, p].astype(f32))
    r = lax.broadcasted_iota(jnp.int32, (1, L), 1)
    sign_a = (1 - 2 * (r & 1)).astype(f32)

    def one_pair(i, _):
        m = lower[step * 8 + i]
        a = load(xs, pl.ds(2 * i, 48, stride=16))
        b = load(xs, pl.ds(2 * i + 1, 48, stride=16))
        a = pltpu.roll(a, (L - m) & (L - 1), 1)
        b_last = b[:, L - 1 : L]
        b = pltpu.roll(b, 1, 1)
        is_a = r < L - m
        sign_b = (1 - 2 * ((r + m) & 1)).astype(f32)
        a = jnp.where(is_a, a, 0.0)
        b = jnp.where(is_a, 0.0, b)
        lhs = jnp.concatenate([a, a * sign_a, b, b * sign_b], axis=0).astype(bf16)
        res = jnp.dot(lhs, table[i, 0:L, :], preferred_element_type=f32)
        last = b_last * table[i, L : L + 1, :].astype(f32)
        last_sign = (1 - 2 * (m & 1)).astype(f32)
        b_n = res[96:144] + last
        b_s = res[144:192] + last * last_sign
        for k, parts in ((2 * i, (res[0:48], res[48:96])), (2 * i + 1, (b_n, b_s))):
            for h in range(2):
                for s in range(2):
                    rows = pl.ds((s * 2 + h) * 384 + k, 24, stride=16)
                    store(ys, rows, parts[h][s * 24 : s * 24 + 24])
        return 0

    lax.fori_loop(0, 8, one_pair, 0)
    for sh in range(4):
        for jh in range(2):
            piece = ys[jh, sh * 384 : sh * 384 + 384, :]
            out[sh * 2 + jh] = piece.reshape(24, 16, 128).astype(bf16)


def legendre_synthesis(lower, velocity, vorticity, magnetic, current, table):
    field = pl.BlockSpec((3, 2, 2, 16, L), lambda g, low: (0, 0, 0, g, 0))
    return pl.pallas_call(
        synthesis_kernel,
        grid_spec=pltpu.PrefetchScalarGridSpec(
            num_scalar_prefetch=1,
            grid=(4,),
            in_specs=[field] * 4 + [pl.BlockSpec((8, L + 1, NH), lambda g, low: (g, 0, 0))],
            out_specs=pl.BlockSpec((8, 24, 16, 128), lambda g, low: (0, 0, g, 0)),
            scratch_shapes=[pltpu.VMEM((4, 768, 128), f32), pltpu.VMEM((2, 1536, 128), f32)],
        ),
        out_shape=jax.ShapeDtypeStruct((8, 24, 64, 128), bf16),
        compiler_params=pltpu.CompilerParams(vmem_limit_bytes=40 * MIB),
        cost_estimate=pl.CostEstimate(flops=int(1.6e9), bytes_accessed=15 * MIB, transcendentals=0),
        name="legendre_synthesis",
    )(lower, velocity, vorticity, magnetic, current, table)


def state_kernel(place, kappa, angular, vel, pot, *refs):
    outs, scr = refs[:16], refs[16]
    for f, ref in enumerate((vel, pot)):
        for c in range(3):
            for s in range(2):
                for p in range(2):
                    x = ref[c, s, p].astype(f32)
                    row = s * 48 + ((f * 3 + c) * 2 + p) * 4
                    for d in range(16):
                        scr[d, row : row + 4, :] = x[4 * d : 4 * d + 4]
    lane = lax.broadcasted_iota(jnp.int32, (1, L), 1)
    lines = []
    for ref in (kappa, angular):
        for f in range(2):
            for s in range(2):
                value = jnp.full((1, L), ref[f, s], f32)
                high = value.astype(bf16).astype(f32)
                rest = value - high
                mid = rest.astype(bf16).astype(f32)
                low = rest - mid
                lines.append(jnp.where(lane < 128, high, jnp.where(lane < 256, mid, low)))
    extra = jnp.concatenate(lines + [jnp.zeros((8, L), f32)], axis=0).astype(bf16)
    for r in range(16):
        outs[r][0:96, :] = scr[place[0] ^ r].astype(bf16)
        outs[r][96:112, :] = extra


def state_to_send(place, kappa, angular, velocity, potential):
    field = pl.BlockSpec((3, 2, 2, 64, L), lambda g: (0, 0, 0, 0, 0))
    small = pl.BlockSpec(memory_space=pltpu.SMEM)
    return pl.pallas_call(
        state_kernel,
        grid=(1,),
        in_specs=[small, small, small, field, field],
        out_specs=[pl.BlockSpec((112, L), lambda g: (0, 0))] * 16,
        out_shape=[jax.ShapeDtypeStruct((112, L), bf16)] * 16,
        scratch_shapes=[pltpu.VMEM((16, 96, L), f32)],
        compiler_params=pltpu.CompilerParams(vmem_limit_bytes=32 * MIB),
        cost_estimate=pl.CostEstimate(flops=10**6, bytes_accessed=4 * MIB, transcendentals=0),
        name="state_to_send",
    )(place, kappa, angular, velocity, potential)


def grid_kernel(lat, syn, ana, weight, out, wide, prod, acc):
    step = pl.program_id(0)

    @pl.when(step == 0)
    def _():
        for c in range(12):
            wide[:, c * 128 : c * 128 + 128] = lat[:, 2 * c : 2 * c + 2].reshape(1024, 128)

    g = jnp.dot(syn[...], wide[...], preferred_element_type=f32)
    x = [g[:, c * 128 : c * 128 + 128] for c in range(12)]
    u, w, b, j = x[0:3], x[3:6], x[6:9], x[9:12]

    def cross(p, q):
        return [
            p[1] * q[2] - p[2] * q[1],
            p[2] * q[0] - p[0] * q[2],
            p[0] * q[1] - p[1] * q[0],
        ]

    uw, jb, ub = cross(u, w), cross(j, b), cross(u, b)
    terms = [uw[0] + jb[0] + 2.0 * u[1], uw[1] + jb[1] - 2.0 * u[0], uw[2] + jb[2]] + ub
    for c in range(6):
        prod[:, c * 128 : c * 128 + 128] = terms[c].astype(bf16)
    part = jnp.dot(ana[...], prod[...], preferred_element_type=f32)

    @pl.when(step == 0)
    def _():
        acc[...] = part

    @pl.when(step > 0)
    def _():
        acc[...] += part

    @pl.when(step == pl.num_programs(0) - 1)
    def _():
        wt = weight[...]
        for c in range(6):
            out[:, c * 128 : c * 128 + 128] = (acc[:, c * 128 : c * 128 + 128] * wt).astype(bf16)


def grid_stage(lat, syn, ana, weight):
    rows = 256
    return pl.pallas_call(
        grid_kernel,
        grid=(NPHI // rows,),
        in_specs=[
            pl.BlockSpec((8, 24, 64, 128), lambda i: (0, 0, 0, 0)),
            pl.BlockSpec((rows, 1024), lambda i: (i, 0)),
            pl.BlockSpec((1024, rows), lambda i: (0, i)),
            pl.BlockSpec((1, 128), lambda i: (0, 0)),
        ],
        out_specs=pl.BlockSpec((1024, 768), lambda i: (0, 0)),
        out_shape=jax.ShapeDtypeStruct((1024, 768), bf16),
        scratch_shapes=[
            pltpu.VMEM((1024, 1536), bf16),
            pltpu.VMEM((rows, 768), bf16),
            pltpu.VMEM((1024, 768), f32),
        ],
        compiler_params=pltpu.CompilerParams(vmem_limit_bytes=48 * MIB),
        cost_estimate=pl.CostEstimate(flops=int(4.8e9), bytes_accessed=9 * MIB, transcendentals=0),
        name="grid_stage",
    )(lat, syn, ana, weight)


def prepare_kernel(place, lower, table, *refs):
    parts, (state_out, table_out, factors, scr, extra) = refs[:16], refs[16:]
    for r in range(16):
        state_out[place[0] ^ r] = parts[r][0:96, :]
        extra[place[0] ^ r] = parts[r][96:112, :].astype(f32)
    l_row = lax.broadcasted_iota(jnp.int32, (1, L), 1)
    for i in range(2):
        m = lower[place[0] * 2 + i]
        scr[...] = table[i].astype(f32)
        a = jnp.transpose(scr[0:L, :])
        a = pltpu.roll(a, m, 1)
        table_out[2 * i] = jnp.where(l_row >= m, a, 0.0).astype(bf16)
        b = jnp.transpose(scr[1 : L + 1, :])
        table_out[2 * i + 1] = jnp.where(l_row >= L - 1 - m, b, 0.0).astype(bf16)
    degree = l_row.astype(f32)
    degree_term = degree * (degree + 1.0)
    below, angle = [[], []], [[], []]
    for d in range(16):
        x = extra[d]
        value = (x[0:8, 0:128] + x[0:8, 128:256]) + x[0:8, 256:384]
        value = jnp.concatenate([value] * 4, axis=1)
        for f in range(2):
            for s in range(2):
                below[f].append(value[f * 2 + s : f * 2 + s + 1])
                angle[f].append(value[4 + f * 2 + s : 4 + f * 2 + s + 1])
    for f in range(2):
        carried = jnp.zeros((1, L), f32)
        for s in range(32):
            under = below[f][s]
            above = below[f][s + 1] if s < 31 else jnp.zeros((1, L), f32)
            diagonal = 1.0 + under + above + angle[f][s] * degree_term
            inverse = 1.0 / (diagonal - under * carried)
            carried = above * inverse
            row = f * 32 + s
            factors[0, row : row + 1, :] = inverse
            factors[1, row : row + 1, :] = under * inverse
            factors[2, row : row + 1, :] = carried


def prepare_solve(place, lower, table, parts):
    return pl.pallas_call(
        prepare_kernel,
        grid_spec=pltpu.PrefetchScalarGridSpec(
            num_scalar_prefetch=2,
            grid=(1,),
            in_specs=[
                pl.BlockSpec((2, L + 1, NH), lambda g, place, low: (place[0], 0, 0)),
            ]
            + [pl.BlockSpec((112, L), lambda g, place, low: (0, 0))] * 16,
            out_specs=[
                pl.BlockSpec((16, 96, L), lambda g, place, low: (0, 0, 0)),
                pl.BlockSpec((4, NH, L), lambda g, place, low: (0, 0, 0)),
                pl.BlockSpec((3, 64, L), lambda g, place, low: (0, 0, 0)),
            ],
            scratch_shapes=[pltpu.VMEM((L + 1, NH), f32), pltpu.VMEM((16, 16, L), f32)],
        ),
        out_shape=[
            jax.ShapeDtypeStruct((16, 96, L), bf16),
            jax.ShapeDtypeStruct((4, NH, L), bf16),
            jax.ShapeDtypeStruct((3, 64, L), f32),
        ],
        compiler_params=pltpu.CompilerParams(vmem_limit_bytes=24 * MIB),
        cost_estimate=pl.CostEstimate(flops=10**7, bytes_accessed=3 * MIB, transcendentals=0),
        name="prepare_solve",
    )(place, lower, table, *parts)


def solve_kernel(place, lower, coef, state, table, factors, out, cs, lhs, rhs):
    for c in range(6):
        cs[c] = coef[:, c * 128 : c * 128 + 128].astype(f32)
    l_row = lax.broadcasted_iota(jnp.int32, (1, L), 1)
    for k in range(4):
        m = lower[place[0] * 2 + k // 2]
        order = m if k % 2 == 0 else L - 1 - m
        half_sign = 0.5 * (1 - 2 * ((l_row + order) & 1)).astype(f32)
        for h in range(2):
            for c in range(6):
                for p in range(2):
                    row = ((h * 6 + c) * 2 + p) * 32
                    for jh in range(2):
                        start = h * 16 + jh * 8 + k * 2 + p
                        lhs[k % 2, row : row + 32, jh * 128 : jh * 128 + 128] = cs[
                            c, pl.ds(start, 32, stride=32), :
                        ].astype(bf16)
        res = jnp.dot(lhs[k % 2], table[k], preferred_element_type=f32)
        half = 0.5 * res[0:384] + half_sign * res[384:768]
        for cp in range(12):
            store(rhs, pl.ds(cp * 4 + k, 32, stride=48), half[cp * 32 : cp * 32 + 32])

    def factor(kind, f, s):
        return factors[kind, pl.ds(f * 32 + s, 1), :]

    def forward(d, running):
        running = list(running)
        block = state[d].astype(f32)
        for s2 in range(2):
            s = 2 * d + s2
            for f in range(2):
                base = s * 48 + f * 24
                value = load(rhs, pl.ds(base, 24)) + block[s2 * 48 + f * 24 : s2 * 48 + f * 24 + 24]
                running[f] = factor(0, f, s) * value + factor(1, f, s) * running[f]
                store(rhs, pl.ds(base, 24), running[f])
        return tuple(running)

    zero = jnp.zeros((24, L), f32)
    lax.fori_loop(0, 16, forward, (zero, zero))

    def backward(step, carried):
        d = 15 - step
        carried = list(carried)
        pieces = [None] * 4
        for s2 in (1, 0):
            s = 2 * d + s2
            for f in range(2):
                value = load(rhs, pl.ds(s * 48 + f * 24, 24))
                carried[f] = value + factor(2, f, s) * carried[f]
                pieces[s2 * 2 + f] = carried[f]
        out[d] = jnp.concatenate(pieces, axis=0).astype(bf16)
        return tuple(carried)

    lax.fori_loop(0, 16, backward, (zero, zero))


def analysis_and_solve(place, lower, coef, state, table, factors):
    return pl.pallas_call(
        solve_kernel,
        grid_spec=pltpu.PrefetchScalarGridSpec(
            num_scalar_prefetch=2,
            grid=(1,),
            in_specs=[
                pl.BlockSpec((1024, 768), lambda g, place, low: (0, 0)),
                pl.BlockSpec((16, 96, L), lambda g, place, low: (0, 0, 0)),
                pl.BlockSpec((4, NH, L), lambda g, place, low: (0, 0, 0)),
                pl.BlockSpec((3, 64, L), lambda g, place, low: (0, 0, 0)),
            ],
            out_specs=pl.BlockSpec((16, 96, L), lambda g, place, low: (0, 0, 0)),
            scratch_shapes=[
                pltpu.VMEM((6, 1024, 128), f32),
                pltpu.VMEM((2, 768, NH), bf16),
                pltpu.VMEM((4, 32 * 48, 128), f32),
            ],
        ),
        out_shape=jax.ShapeDtypeStruct((16, 96, L), bf16),
        compiler_params=pltpu.CompilerParams(vmem_limit_bytes=48 * MIB),
        cost_estimate=pl.CostEstimate(flops=int(0.9e9), bytes_accessed=6 * MIB, transcendentals=0),
        name="analysis_and_solve",
    )(place, lower, coef, state, table, factors)


def unpack_kernel(got, out_v, out_p, scr, tmp):
    store(scr, pl.ds(0, 768), got[...].astype(f32).reshape(768, L))
    for f, ref in enumerate((out_v, out_p)):
        for c in range(3):
            for p in range(2):
                for k in range(4):
                    row = ((f * 3 + c) * 2 + p) * 4 + k
                    store(tmp, pl.ds(k, 16, stride=4), load(scr, pl.ds(row, 16, stride=48)))
                ref[c, 0, p] = load(tmp, pl.ds(0, 64))


def unpack_solution(got):
    shape = jax.ShapeDtypeStruct((3, 2, 2, 64, L), f32)
    field = pl.BlockSpec((3, 1, 2, 64, L), lambda s: (0, s, 0, 0, 0))
    return pl.pallas_call(
        unpack_kernel,
        grid=(2,),
        in_specs=[pl.BlockSpec((16, 48, L), lambda s: (0, s, 0))],
        out_specs=[field, field],
        out_shape=[shape, shape],
        scratch_shapes=[pltpu.VMEM((4, 768, 128), f32), pltpu.VMEM((4, 64, 128), f32)],
        compiler_params=pltpu.CompilerParams(vmem_limit_bytes=24 * MIB),
        cost_estimate=pl.CostEstimate(flops=10**6, bytes_accessed=5 * MIB, transcendentals=0),
        name="unpack_solution",
    )(got)


def fourier_tables(order_slots):
    natural_s, natural_a = natural_tables()
    ids = jnp.arange(2 * L, dtype=jnp.int32)
    part = jnp.arange(2, dtype=jnp.int32)
    by_source = order_slots.reshape(8, 1, 64) * 2 + part[None, :, None]
    pick_s = (ids[:, None] == by_source.reshape(1, -1)).astype(bf16)
    syn = jnp.dot(jnp.asarray(natural_s), pick_s, preferred_element_type=f32).astype(bf16)
    slots = order_slots.reshape(8, 16, 4).transpose(1, 0, 2)
    by_target = slots[..., None] * 2 + part
    pick_a = (by_target.reshape(-1, 1) == ids[None, :]).astype(bf16)
    ana = jnp.dot(pick_a, jnp.asarray(natural_a), preferred_element_type=f32).astype(bf16)
    return syn, ana


def body(
    velocity,
    vorticity,
    magnetic,
    current,
    potential,
    order_slots,
    legendre_values,
    block_lengths,
    coupling,
    angular,
):
    order_rank = lax.axis_index("order")
    shell_rank = lax.axis_index("shell")
    lower = lax.dynamic_slice_in_dim(order_slots, order_rank * 64, 64).reshape(32, 2)[:, 0]
    place = shell_rank.reshape(1)
    shell_ids = shell_rank * 2 + jnp.arange(2, dtype=jnp.int32)
    starts = jnp.cumsum(block_lengths) - block_lengths
    is_start = jnp.any(shell_ids[:, None] == starts[None, :], axis=1)
    kappa = jnp.where(is_start[None, :], 0.0, coupling)
    rows = (order_rank & 1) * 128 + jnp.arange(128, dtype=jnp.int32)
    colatitude = math.pi * (rows.astype(f32) + 0.5) / NLAT
    weight = (math.sqrt(2.0 * math.pi) * L * math.pi / NLAT * jnp.sin(colatitude))[None, :]

    latitude = legendre_synthesis(
        lower, velocity, vorticity, magnetic, current, legendre_values
    )
    incoming = lax.all_to_all(latitude, "order", 0, 0, tiled=True)

    order_after, vel_after, pot_after, _ = lax.optimization_barrier(
        (order_slots, velocity, potential, latitude)
    )
    parts = state_to_send(place, kappa, angular, vel_after, pot_after)
    parts = [parts[0]] + [
        lax.ppermute(parts[r], "shell", [(i, i ^ r) for i in range(16)]) for r in range(1, 16)
    ]
    syn, ana = fourier_tables(order_after)
    early = 12
    incoming, parts[1:early] = lax.optimization_barrier((incoming, parts[1:early]))
    coefs = grid_stage(incoming, syn, ana, weight)
    coefs = lax.all_to_all(
        coefs.reshape(128, 8, 768), ("shell", "order"), 0, 0, tiled=True
    ).reshape(1024, 768)
    state, table, factors = prepare_solve(place, lower, legendre_values, parts)
    solved = analysis_and_solve(place, lower, coefs, state, table, factors)
    solved = lax.all_to_all(solved, "shell", 0, 0, tiled=True)
    return tuple(unpack_solution(solved))


def solution(mesh):
    spectral = P(None, "shell", None, "order", None)
    in_specs = (
        spectral,
        spectral,
        spectral,
        spectral,
        spectral,
        P(),
        P("order", None, None),
        P(),
        P(None, "shell"),
        P(None, "shell"),
    )
    return jax.shard_map(
        body, mesh=mesh, in_specs=in_specs, out_specs=(spectral, spectral), check_vma=False
    )
```

```python
import math

import jax
import jax.numpy as jnp
import numpy as np
from jax import lax
from jax.experimental import pallas as pl
from jax.experimental.pallas import tpu as pltpu
from jax.sharding import PartitionSpec as P

L = 512
NLAT = 512
NPHI = 1024
NH = 256
f32 = jnp.float32
bf16 = jnp.bfloat16
MIB = 1 << 20


def natural_tables():
    phases = (np.arange(L)[:, None] * np.arange(NPHI)[None, :]) % NPHI
    angles = 2.0 * np.pi * phases / NPHI
    rows = np.stack([np.cos(angles), -np.sin(angles)], axis=1)
    weight = np.where(np.arange(L) == 0, 1.0, 2.0) * (math.sqrt(2.0 * math.pi) / L)
    synthesis = (rows * weight[:, None, None]).reshape(2 * L, NPHI)
    analysis = (rows / NPHI).reshape(2 * L, NPHI)
    return synthesis.T.astype(jnp.bfloat16), analysis.astype(jnp.bfloat16)


def load(ref, rows):
    return jnp.concatenate([ref[q, rows, :] for q in range(ref.shape[0])], axis=1)


def store(ref, rows, value):
    for q in range(ref.shape[0]):
        ref[q, rows, :] = value[:, q * 128 : q * 128 + 128]


PITCH = 33
TABLE_PITCH = 17
CHUNK = 171


def synthesis_kernel(place, lower, vel, vor, mag, cur, table, out, pairs, xs, ys, ts):
    step = pl.program_id(0)
    chunk = pl.program_id(1)

    @pl.when(chunk == 0)
    def _():
        for a, ref in enumerate((vel, vor, mag, cur)):
            for c in range(3):
                for s in range(2):
                    for p in range(2):
                        row = (s * 24 + (a * 3 + c) * 2 + p) * PITCH
                        store(xs, pl.ds(row, 32), ref[c, s, p].astype(f32))

    for q in range(3):

        @pl.when(chunk == q)
        def _():
            for d in range(CHUNK):
                store(ts, pl.ds((q * CHUNK + d) * TABLE_PITCH, 16), table[d].astype(f32))

    r = lax.broadcasted_iota(jnp.int32, (1, L), 1)
    sign_a = (1 - 2 * (r & 1)).astype(f32)

    def one_pair(i, _):
        m = lower[step * 16 + i]
        a = load(xs, pl.ds(2 * i, 48, stride=PITCH))
        b = load(xs, pl.ds(2 * i + 1, 48, stride=PITCH))
        rows = load(ts, pl.ds(i, L, stride=TABLE_PITCH)).astype(bf16)
        a = pltpu.roll(a, (L - m) & (L - 1), 1)
        b_last = b[:, L - 1 : L]
        b = pltpu.roll(b, 1, 1)
        is_a = r < L - m
        sign_b = (1 - 2 * ((r + m) & 1)).astype(f32)
        a = jnp.where(is_a, a, 0.0)
        b = jnp.where(is_a, 0.0, b)
        lhs = jnp.concatenate([a, a * sign_a, b, b * sign_b], axis=0).astype(bf16)
        res = jnp.dot(lhs, rows, preferred_element_type=f32)
        last = b_last * load(ts, pl.ds(L * TABLE_PITCH + i, 1))
        last_sign = (1 - 2 * (m & 1)).astype(f32)
        b_n = res[96:144] + last
        b_s = res[144:192] + last * last_sign
        for k, parts in ((2 * i, (res[0:48], res[48:96])), (2 * i + 1, (b_n, b_s))):
            for h in range(2):
                for s in range(2):
                    at = pl.ds((s * 2 + h) * 24 * PITCH + k, 24, stride=PITCH)
                    store(ys, at, parts[h][s * 24 : s * 24 + 24])
        return 0

    @pl.when(chunk == 2)
    def _():
        lax.fori_loop(0, 16, one_pair, 0, unroll=8)
        for sh in range(4):
            for jh in range(2):
                for cp in range(24):
                    row = (sh * 24 + cp) * PITCH
                    out[sh * 2 + jh, cp] = ys[jh, row : row + 32, :].astype(bf16)

    @pl.when((chunk == 2) & (step == place[0] // 8))
    def _():
        for i in range(2):
            at = (place[0] & 7) * 2 + i
            pairs[i, 0:L, :] = load(ts, pl.ds(at, L, stride=TABLE_PITCH)).astype(bf16)
            last = load(ts, pl.ds(L * TABLE_PITCH + at, 1))
            pairs[i, L : L + 16, :] = jnp.broadcast_to(last, (16, NH)).astype(bf16)


def legendre_synthesis(place, lower, velocity, vorticity, magnetic, current, table):
    field = pl.BlockSpec((3, 2, 2, 32, L), lambda g, q, place, low: (0, 0, 0, g, 0))
    return pl.pallas_call(
        synthesis_kernel,
        grid_spec=pltpu.PrefetchScalarGridSpec(
            num_scalar_prefetch=2,
            grid=(2, 3),
            in_specs=[field] * 4
            + [pl.BlockSpec((CHUNK, 16, NH), lambda g, q, place, low: (q, g, 0))],
            out_specs=[
                pl.BlockSpec((8, 24, 32, 128), lambda g, q, place, low: (0, 0, g, 0)),
                pl.BlockSpec((2, L + 16, NH), lambda g, q, place, low: (0, 0, 0)),
            ],
            scratch_shapes=[
                pltpu.VMEM((4, 48 * PITCH, 128), f32),
                pltpu.VMEM((2, 96 * PITCH, 128), f32),
                pltpu.VMEM((2, (L + 1) * TABLE_PITCH + 7, 128), f32),
            ],
        ),
        out_shape=[
            jax.ShapeDtypeStruct((8, 24, 64, 128), bf16),
            jax.ShapeDtypeStruct((2, L + 16, NH), bf16),
        ],
        compiler_params=pltpu.CompilerParams(vmem_limit_bytes=52 * MIB),
        cost_estimate=pl.CostEstimate(flops=int(1.6e9), bytes_accessed=15 * MIB, transcendentals=0),
        name="legendre_synthesis",
    )(place, lower, velocity, vorticity, magnetic, current, table)


def state_kernel(place, kappa, angular, vel, pot, *refs):
    outs, scr = refs[:16], refs[16]
    for f, ref in enumerate((vel, pot)):
        for c in range(3):
            for s in range(2):
                for p in range(2):
                    x = ref[c, s, p].astype(f32)
                    row = s * 48 + ((f * 3 + c) * 2 + p) * 4
                    for d in range(16):
                        scr[d, row : row + 4, :] = x[4 * d : 4 * d + 4]
    lane = lax.broadcasted_iota(jnp.int32, (1, L), 1)
    lines = []
    for ref in (kappa, angular):
        for f in range(2):
            for s in range(2):
                value = jnp.full((1, L), ref[f, s], f32)
                high = value.astype(bf16).astype(f32)
                rest = value - high
                mid = rest.astype(bf16).astype(f32)
                low = rest - mid
                lines.append(jnp.where(lane < 128, high, jnp.where(lane < 256, mid, low)))
    extra = jnp.concatenate(lines + [jnp.zeros((8, L), f32)], axis=0).astype(bf16)
    for r in range(16):
        outs[r][0:96, :] = scr[place[0] ^ r].astype(bf16)
        outs[r][96:112, :] = extra


def state_to_send(place, kappa, angular, velocity, potential):
    field = pl.BlockSpec((3, 2, 2, 64, L), lambda g: (0, 0, 0, 0, 0))
    small = pl.BlockSpec(memory_space=pltpu.SMEM)
    return pl.pallas_call(
        state_kernel,
        grid=(1,),
        in_specs=[small, small, small, field, field],
        out_specs=[pl.BlockSpec((112, L), lambda g: (0, 0))] * 16,
        out_shape=[jax.ShapeDtypeStruct((112, L), bf16)] * 16,
        scratch_shapes=[pltpu.VMEM((16, 96, L), f32)],
        compiler_params=pltpu.CompilerParams(vmem_limit_bytes=32 * MIB),
        cost_estimate=pl.CostEstimate(flops=10**6, bytes_accessed=4 * MIB, transcendentals=0),
        name="state_to_send",
    )(place, kappa, angular, velocity, potential)


def grid_kernel(lat, syn, ana, weight, out, wide, prod):
    step = pl.program_id(0)
    rows = 512

    @pl.when(step == 0)
    def _():
        for c in range(12):
            wide[:, c * 128 : c * 128 + 128] = lat[:, 2 * c : 2 * c + 2].reshape(1024, 128)

    @pl.when(step < 2)
    def _():
        g = jnp.dot(syn[...], wide[...], preferred_element_type=f32)
        x = [g[:, c * 128 : c * 128 + 128] for c in range(12)]
        u, w, b, j = x[0:3], x[3:6], x[6:9], x[9:12]

        def cross(p, q):
            return [
                p[1] * q[2] - p[2] * q[1],
                p[2] * q[0] - p[0] * q[2],
                p[0] * q[1] - p[1] * q[0],
            ]

        uw, jb, ub = cross(u, w), cross(j, b), cross(u, b)
        terms = [uw[0] + jb[0] + 2.0 * u[1], uw[1] + jb[1] - 2.0 * u[0], uw[2] + jb[2]] + ub
        at = pl.ds(pl.multiple_of(step * rows, rows), rows)
        for c in range(6):
            prod[at, c * 128 : c * 128 + 128] = terms[c].astype(bf16)

    @pl.when(step >= 2)
    def _():
        sums = jnp.dot(ana[...], prod[...], preferred_element_type=f32)
        for c in range(6):
            part = sums[:, c * 128 : c * 128 + 128] * weight[...]
            out[:, c * 128 : c * 128 + 128] = part.astype(bf16)


def grid_stage(lat, syn, ana, weight):
    rows = 512
    return pl.pallas_call(
        grid_kernel,
        grid=(4,),
        in_specs=[
            pl.BlockSpec((8, 24, 64, 128), lambda i: (0, 0, 0, 0)),
            pl.BlockSpec((rows, 1024), lambda i: (jnp.minimum(i, 1), 0)),
            pl.BlockSpec((rows, 1024), lambda i: (jnp.maximum(i - 2, 0), 0)),
            pl.BlockSpec((1, 128), lambda i: (0, 0)),
        ],
        out_specs=pl.BlockSpec((rows, 768), lambda i: (jnp.maximum(i - 2, 0), 0)),
        out_shape=jax.ShapeDtypeStruct((1024, 768), bf16),
        scratch_shapes=[pltpu.VMEM((1024, 1536), bf16), pltpu.VMEM((1024, 768), bf16)],
        compiler_params=pltpu.CompilerParams(vmem_limit_bytes=32 * MIB),
        cost_estimate=pl.CostEstimate(flops=int(4.8e9), bytes_accessed=9 * MIB, transcendentals=0),
        name="grid_stage",
    )(lat, syn, ana, weight)


def prepare_kernel(place, lower, table, *refs):
    parts, (state_out, table_out, factors, scr, extra) = refs[:16], refs[16:]
    for r in range(16):
        state_out[place[0] ^ r] = parts[r][0:96, :]
        extra[place[0] ^ r] = parts[r][96:112, :].astype(f32)
    l_row = lax.broadcasted_iota(jnp.int32, (1, L), 1)
    for i in range(2):
        m = lower[place[0] * 2 + i]
        scr[...] = table[i].astype(f32)
        a = jnp.transpose(scr[0:L, :])
        a = pltpu.roll(a, m, 1)
        table_out[2 * i] = jnp.where(l_row >= m, a, 0.0).astype(bf16)
        b = jnp.transpose(scr[1 : L + 1, :])
        table_out[2 * i + 1] = jnp.where(l_row >= L - 1 - m, b, 0.0).astype(bf16)
    degree = l_row.astype(f32)
    degree_term = degree * (degree + 1.0)
    below, angle = [[], []], [[], []]
    for d in range(16):
        x = extra[d]
        value = (x[0:8, 0:128] + x[0:8, 128:256]) + x[0:8, 256:384]
        value = jnp.concatenate([value] * 4, axis=1)
        for f in range(2):
            for s in range(2):
                below[f].append(value[f * 2 + s : f * 2 + s + 1])
                angle[f].append(value[4 + f * 2 + s : 4 + f * 2 + s + 1])
    for f in range(2):
        carried = jnp.zeros((1, L), f32)
        for s in range(32):
            under = below[f][s]
            above = below[f][s + 1] if s < 31 else jnp.zeros((1, L), f32)
            diagonal = 1.0 + under + above + angle[f][s] * degree_term
            inverse = 1.0 / (diagonal - under * carried)
            carried = above * inverse
            row = f * 32 + s
            factors[0, row : row + 1, :] = inverse
            factors[1, row : row + 1, :] = under * inverse
            factors[2, row : row + 1, :] = carried


def prepare_solve(place, lower, table, parts):
    return pl.pallas_call(
        prepare_kernel,
        grid_spec=pltpu.PrefetchScalarGridSpec(
            num_scalar_prefetch=2,
            grid=(1,),
            in_specs=[
                pl.BlockSpec((2, L + 16, NH), lambda g, place, low: (0, 0, 0)),
            ]
            + [pl.BlockSpec((112, L), lambda g, place, low: (0, 0))] * 16,
            out_specs=[
                pl.BlockSpec((16, 96, L), lambda g, place, low: (0, 0, 0)),
                pl.BlockSpec((4, NH, L), lambda g, place, low: (0, 0, 0)),
                pl.BlockSpec((3, 64, L), lambda g, place, low: (0, 0, 0)),
            ],
            scratch_shapes=[pltpu.VMEM((L + 16, NH), f32), pltpu.VMEM((16, 16, L), f32)],
        ),
        out_shape=[
            jax.ShapeDtypeStruct((16, 96, L), bf16),
            jax.ShapeDtypeStruct((4, NH, L), bf16),
            jax.ShapeDtypeStruct((3, 64, L), f32),
        ],
        compiler_params=pltpu.CompilerParams(vmem_limit_bytes=60 * MIB),
        cost_estimate=pl.CostEstimate(flops=10**7, bytes_accessed=3 * MIB, transcendentals=0),
        name="prepare_solve",
    )(place, lower, table, *parts)


def solve_kernel(place, lower, coef, state, table, factors, out, cs, lhs, rhs):
    for c in range(6):
        cs[c] = coef[:, c * 128 : c * 128 + 128].astype(f32)
    l_row = lax.broadcasted_iota(jnp.int32, (1, L), 1)
    for k in range(4):
        m = lower[place[0] * 2 + k // 2]
        order = m if k % 2 == 0 else L - 1 - m
        half_sign = 0.5 * (1 - 2 * ((l_row + order) & 1)).astype(f32)
        for h in range(2):
            for c in range(6):
                for p in range(2):
                    row = ((h * 6 + c) * 2 + p) * 32
                    for jh in range(2):
                        start = h * 16 + jh * 8 + k * 2 + p
                        lhs[k % 2, row : row + 32, jh * 128 : jh * 128 + 128] = cs[
                            c, pl.ds(start, 32, stride=32), :
                        ].astype(bf16)
        res = jnp.dot(lhs[k % 2], table[k], preferred_element_type=f32)
        half = 0.5 * res[0:384] + half_sign * res[384:768]
        for cp in range(12):
            store(rhs, pl.ds(cp * 4 + k, 32, stride=48), half[cp * 32 : cp * 32 + 32])

    def factor(kind, f, s):
        return factors[kind, pl.ds(f * 32 + s, 1), :]

    def forward(d, running):
        running = list(running)
        block = state[d].astype(f32)
        for s2 in range(2):
            s = 2 * d + s2
            for f in range(2):
                base = s * 48 + f * 24
                value = load(rhs, pl.ds(base, 24)) + block[s2 * 48 + f * 24 : s2 * 48 + f * 24 + 24]
                running[f] = factor(0, f, s) * value + factor(1, f, s) * running[f]
                store(rhs, pl.ds(base, 24), running[f])
        return tuple(running)

    zero = jnp.zeros((24, L), f32)
    lax.fori_loop(0, 16, forward, (zero, zero))

    def backward(step, carried):
        d = 15 - step
        carried = list(carried)
        pieces = [None] * 4
        for s2 in (1, 0):
            s = 2 * d + s2
            for f in range(2):
                value = load(rhs, pl.ds(s * 48 + f * 24, 24))
                carried[f] = value + factor(2, f, s) * carried[f]
                pieces[s2 * 2 + f] = carried[f]
        out[d] = jnp.concatenate(pieces, axis=0).astype(bf16)
        return tuple(carried)

    lax.fori_loop(0, 16, backward, (zero, zero))


def analysis_and_solve(place, lower, coef, state, table, factors):
    return pl.pallas_call(
        solve_kernel,
        grid_spec=pltpu.PrefetchScalarGridSpec(
            num_scalar_prefetch=2,
            grid=(1,),
            in_specs=[
                pl.BlockSpec((1024, 768), lambda g, place, low: (0, 0)),
                pl.BlockSpec((16, 96, L), lambda g, place, low: (0, 0, 0)),
                pl.BlockSpec((4, NH, L), lambda g, place, low: (0, 0, 0)),
                pl.BlockSpec((3, 64, L), lambda g, place, low: (0, 0, 0)),
            ],
            out_specs=pl.BlockSpec((16, 96, L), lambda g, place, low: (0, 0, 0)),
            scratch_shapes=[
                pltpu.VMEM((6, 1024, 128), f32),
                pltpu.VMEM((2, 768, NH), bf16),
                pltpu.VMEM((4, 32 * 48, 128), f32),
            ],
        ),
        out_shape=jax.ShapeDtypeStruct((16, 96, L), bf16),
        compiler_params=pltpu.CompilerParams(vmem_limit_bytes=32 * MIB),
        cost_estimate=pl.CostEstimate(flops=int(0.9e9), bytes_accessed=6 * MIB, transcendentals=0),
        name="analysis_and_solve",
    )(place, lower, coef, state, table, factors)


def unpack_kernel(got, out_v, out_p, scr, tmp):
    store(scr, pl.ds(0, 768), got[...].astype(f32).reshape(768, L))
    for f, ref in enumerate((out_v, out_p)):
        for c in range(3):
            for p in range(2):
                for k in range(4):
                    row = ((f * 3 + c) * 2 + p) * 4 + k
                    store(tmp, pl.ds(k, 16, stride=4), load(scr, pl.ds(row, 16, stride=48)))
                ref[c, 0, p] = load(tmp, pl.ds(0, 64))


def unpack_solution(got):
    shape = jax.ShapeDtypeStruct((3, 2, 2, 64, L), f32)
    field = pl.BlockSpec((3, 1, 2, 64, L), lambda s: (0, s, 0, 0, 0))
    return pl.pallas_call(
        unpack_kernel,
        grid=(2,),
        in_specs=[pl.BlockSpec((16, 48, L), lambda s: (0, s, 0))],
        out_specs=[field, field],
        out_shape=[shape, shape],
        scratch_shapes=[pltpu.VMEM((4, 768, 128), f32), pltpu.VMEM((4, 64, 128), f32)],
        compiler_params=pltpu.CompilerParams(vmem_limit_bytes=24 * MIB),
        cost_estimate=pl.CostEstimate(flops=10**6, bytes_accessed=5 * MIB, transcendentals=0),
        name="unpack_solution",
    )(got)


def fourier_tables(order_slots):
    natural_s, natural_a = natural_tables()
    ids = jnp.arange(2 * L, dtype=jnp.int32)
    part = jnp.arange(2, dtype=jnp.int32)
    by_source = order_slots.reshape(8, 1, 64) * 2 + part[None, :, None]
    pick_s = (ids[:, None] == by_source.reshape(1, -1)).astype(bf16)
    syn = jnp.dot(jnp.asarray(natural_s), pick_s, preferred_element_type=f32).astype(bf16)
    slots = order_slots.reshape(8, 16, 4).transpose(1, 0, 2)
    by_target = slots[..., None] * 2 + part
    pick_a = (by_target.reshape(-1, 1) == ids[None, :]).astype(bf16)
    ana = jnp.dot(pick_a, jnp.asarray(natural_a), preferred_element_type=f32).astype(bf16)
    return syn, ana


def body(
    velocity,
    vorticity,
    magnetic,
    current,
    potential,
    order_slots,
    legendre_values,
    block_lengths,
    coupling,
    angular,
):
    order_rank = lax.axis_index("order")
    shell_rank = lax.axis_index("shell")
    lower = lax.dynamic_slice_in_dim(order_slots, order_rank * 64, 64).reshape(32, 2)[:, 0]
    place = shell_rank.reshape(1)
    shell_ids = shell_rank * 2 + jnp.arange(2, dtype=jnp.int32)
    starts = jnp.cumsum(block_lengths) - block_lengths
    is_start = jnp.any(shell_ids[:, None] == starts[None, :], axis=1)
    kappa = jnp.where(is_start[None, :], 0.0, coupling)
    rows = (order_rank & 1) * 128 + jnp.arange(128, dtype=jnp.int32)
    colatitude = math.pi * (rows.astype(f32) + 0.5) / NLAT
    weight = (math.sqrt(2.0 * math.pi) * L * math.pi / NLAT * jnp.sin(colatitude))[None, :]

    latitude, pairs = legendre_synthesis(
        place,
        lower,
        velocity,
        vorticity,
        magnetic,
        current,
        jnp.transpose(legendre_values, (1, 0, 2)),
    )
    incoming = lax.all_to_all(latitude, "order", 0, 0, tiled=True)

    order_after, vel_after, pot_after, _ = lax.optimization_barrier(
        (order_slots, velocity, potential, latitude)
    )
    parts = state_to_send(place, kappa, angular, vel_after, pot_after)
    parts = [parts[0]] + [
        lax.ppermute(parts[r], "shell", [(i, i ^ r) for i in range(16)]) for r in range(1, 16)
    ]
    syn, ana = fourier_tables(order_after)
    state, table, factors = prepare_solve(place, lower, pairs, parts)
    incoming, state, table, factors = lax.optimization_barrier((incoming, state, table, factors))

    coefs = grid_stage(incoming, syn, ana, weight)
    coefs = lax.all_to_all(
        coefs.reshape(128, 8, 768), ("shell", "order"), 0, 0, tiled=True
    ).reshape(1024, 768)
    solved = analysis_and_solve(place, lower, coefs, state, table, factors)
    solved = lax.all_to_all(solved, "shell", 0, 0, tiled=True)
    return tuple(unpack_solution(solved))


def solution(mesh):
    spectral = P(None, "shell", None, "order", None)
    in_specs = (
        spectral,
        spectral,
        spectral,
        spectral,
        spectral,
        P(),
        P("order", None, None),
        P(),
        P(None, "shell"),
        P(None, "shell"),
    )
    return jax.shard_map(
        body, mesh=mesh, in_specs=in_specs, out_specs=(spectral, spectral), check_vma=False
    )
```

```python
import math

import jax
import jax.numpy as jnp
import numpy as np
from jax import lax
from jax.experimental import pallas as pl
from jax.experimental.pallas import tpu as pltpu
from jax.sharding import PartitionSpec as P

L = 512
NLAT = 512
NPHI = 1024
NH = 256
f32 = jnp.float32
bf16 = jnp.bfloat16
MIB = 1 << 20


def natural_tables():
    phases = (np.arange(L)[:, None] * np.arange(NPHI)[None, :]) % NPHI
    angles = 2.0 * np.pi * phases / NPHI
    rows = np.stack([np.cos(angles), -np.sin(angles)], axis=0)
    weight = np.where(np.arange(L) == 0, 1.0, 2.0) * (math.sqrt(2.0 * math.pi) / L)
    synthesis = (rows * weight[None, :, None]).reshape(2 * L, NPHI)
    analysis = (rows / NPHI).reshape(2 * L, NPHI)
    return synthesis.T.astype(jnp.bfloat16), analysis.astype(jnp.bfloat16)


def partner(place, odd, r):
    swapped = (r & 3) * 4 + r // 4
    return place ^ jnp.where(odd == 1, swapped, r)


def load(ref, rows):
    return jnp.concatenate([ref[q, rows, :] for q in range(ref.shape[0])], axis=1)


def store(ref, rows, value):
    for q in range(ref.shape[0]):
        ref[q, rows, :] = value[:, q * 128 : q * 128 + 128]


PITCH = 33
TABLE_PITCH = 17
CHUNK = 171


def synthesis_kernel(place, lower, vel, vor, mag, cur, table, out, pairs, xs, ys, ts):
    step = pl.program_id(0)
    chunk = pl.program_id(1)

    @pl.when(chunk == 0)
    def _():
        for a, ref in enumerate((vel, vor, mag, cur)):
            for c in range(3):
                for s in range(2):
                    for p in range(2):
                        row = (s * 24 + (a * 3 + c) * 2 + p) * PITCH
                        store(xs, pl.ds(row, 32), ref[c, s, p].astype(f32))

    for q in range(3):

        @pl.when(chunk == q)
        def _():
            for d in range(CHUNK):
                store(ts, pl.ds((q * CHUNK + d) * TABLE_PITCH, 16), table[d].astype(f32))

    r = lax.broadcasted_iota(jnp.int32, (1, L), 1)
    sign_a = (1 - 2 * (r & 1)).astype(f32)

    def one_pair(i, _):
        m = lower[step * 16 + i]
        a = load(xs, pl.ds(2 * i, 48, stride=PITCH))
        b = load(xs, pl.ds(2 * i + 1, 48, stride=PITCH))
        rows = load(ts, pl.ds(i, L, stride=TABLE_PITCH)).astype(bf16)
        a = pltpu.roll(a, (L - m) & (L - 1), 1)
        b_last = b[:, L - 1 : L]
        b = pltpu.roll(b, 1, 1)
        is_a = r < L - m
        sign_b = (1 - 2 * ((r + m) & 1)).astype(f32)
        a = jnp.where(is_a, a, 0.0)
        b = jnp.where(is_a, 0.0, b)
        lhs = jnp.concatenate([a, a * sign_a, b, b * sign_b], axis=0).astype(bf16)
        res = jnp.dot(lhs, rows, preferred_element_type=f32)
        last = b_last * load(ts, pl.ds(L * TABLE_PITCH + i, 1))
        last_sign = (1 - 2 * (m & 1)).astype(f32)
        b_n = res[96:144] + last
        b_s = res[144:192] + last * last_sign
        for k, parts in ((2 * i, (res[0:48], res[48:96])), (2 * i + 1, (b_n, b_s))):
            for h in range(2):
                for s in range(2):
                    at = pl.ds((s * 2 + h) * 24 * PITCH + k, 24, stride=PITCH)
                    store(ys, at, parts[h][s * 24 : s * 24 + 24])
        return 0

    @pl.when(chunk == 2)
    def _():
        lax.fori_loop(0, 16, one_pair, 0, unroll=8)
        for sh in range(4):
            for jh in range(2):
                for cp in range(24):
                    row = (sh * 24 + cp) * PITCH
                    out[sh * 2 + jh, cp] = ys[jh, row : row + 32, :].astype(bf16)

    @pl.when((chunk == 2) & (step == place[0] // 8))
    def _():
        for i in range(2):
            at = (place[0] & 7) * 2 + i
            pairs[i, 0:L, :] = load(ts, pl.ds(at, L, stride=TABLE_PITCH)).astype(bf16)
            last = load(ts, pl.ds(L * TABLE_PITCH + at, 1))
            pairs[i, L : L + 16, :] = jnp.broadcast_to(last, (16, NH)).astype(bf16)


def legendre_synthesis(place, lower, velocity, vorticity, magnetic, current, table):
    field = pl.BlockSpec((3, 2, 2, 32, L), lambda g, q, place, low: (0, 0, 0, g, 0))
    return pl.pallas_call(
        synthesis_kernel,
        grid_spec=pltpu.PrefetchScalarGridSpec(
            num_scalar_prefetch=2,
            grid=(2, 3),
            in_specs=[field] * 4
            + [pl.BlockSpec((CHUNK, 16, NH), lambda g, q, place, low: (q, g, 0))],
            out_specs=[
                pl.BlockSpec((8, 24, 32, 128), lambda g, q, place, low: (0, 0, g, 0)),
                pl.BlockSpec((2, L + 16, NH), lambda g, q, place, low: (0, 0, 0)),
            ],
            scratch_shapes=[
                pltpu.VMEM((4, 48 * PITCH, 128), f32),
                pltpu.VMEM((2, 96 * PITCH, 128), f32),
                pltpu.VMEM((2, (L + 1) * TABLE_PITCH + 7, 128), f32),
            ],
        ),
        out_shape=[
            jax.ShapeDtypeStruct((8, 24, 64, 128), bf16),
            jax.ShapeDtypeStruct((2, L + 16, NH), bf16),
        ],
        compiler_params=pltpu.CompilerParams(vmem_limit_bytes=52 * MIB),
        cost_estimate=pl.CostEstimate(flops=int(1.6e9), bytes_accessed=15 * MIB, transcendentals=0),
        name="legendre_synthesis",
    )(place, lower, velocity, vorticity, magnetic, current, table)


def state_kernel(place, kappa, angular, vel, pot, *refs):
    outs, scr = refs[:16], refs[16]
    for f, ref in enumerate((vel, pot)):
        for c in range(3):
            for s in range(2):
                for p in range(2):
                    x = ref[c, s, p].astype(f32)
                    row = s * 48 + ((f * 3 + c) * 2 + p) * 4
                    for d in range(16):
                        scr[d, row : row + 4, :] = x[4 * d : 4 * d + 4]
    lane = lax.broadcasted_iota(jnp.int32, (1, L), 1)
    lines = []
    for ref in (kappa, angular):
        for f in range(2):
            for s in range(2):
                value = jnp.full((1, L), ref[f, s], f32)
                high = value.astype(bf16).astype(f32)
                rest = value - high
                mid = rest.astype(bf16).astype(f32)
                low = rest - mid
                lines.append(jnp.where(lane < 128, high, jnp.where(lane < 256, mid, low)))
    extra = jnp.concatenate(lines + [jnp.zeros((8, L), f32)], axis=0).astype(bf16)
    for r in range(16):
        outs[r][0:96, :] = scr[partner(place[0], place[1], r)].astype(bf16)
        outs[r][96:112, :] = extra


def state_to_send(place, kappa, angular, velocity, potential):
    field = pl.BlockSpec((3, 2, 2, 64, L), lambda g: (0, 0, 0, 0, 0))
    small = pl.BlockSpec(memory_space=pltpu.SMEM)
    return pl.pallas_call(
        state_kernel,
        grid=(1,),
        in_specs=[small, small, small, field, field],
        out_specs=[pl.BlockSpec((112, L), lambda g: (0, 0))] * 16,
        out_shape=[jax.ShapeDtypeStruct((112, L), bf16)] * 16,
        scratch_shapes=[pltpu.VMEM((16, 96, L), f32)],
        compiler_params=pltpu.CompilerParams(vmem_limit_bytes=32 * MIB),
        cost_estimate=pl.CostEstimate(flops=10**6, bytes_accessed=4 * MIB, transcendentals=0),
        name="state_to_send",
    )(place, kappa, angular, velocity, potential)


def grid_kernel(lat, syn, ana, weight, out, wide, prod):
    step = pl.program_id(0)
    rows = 512

    @pl.when(step == 0)
    def _():
        for c in range(12):
            for p in range(2):
                rows_p = lat[:, 2 * c + p].reshape(512, 128)
                wide[p * 512 : p * 512 + 512, c * 128 : c * 128 + 128] = rows_p

    @pl.when(step < 2)
    def _():
        g = jnp.dot(syn[...], wide[...], preferred_element_type=f32)
        x = [g[:, c * 128 : c * 128 + 128] for c in range(12)]
        u, w, b, j = x[0:3], x[3:6], x[6:9], x[9:12]

        def cross(p, q):
            return [
                p[1] * q[2] - p[2] * q[1],
                p[2] * q[0] - p[0] * q[2],
                p[0] * q[1] - p[1] * q[0],
            ]

        uw, jb, ub = cross(u, w), cross(j, b), cross(u, b)
        terms = [uw[0] + jb[0] + 2.0 * u[1], uw[1] + jb[1] - 2.0 * u[0], uw[2] + jb[2]] + ub
        at = pl.ds(pl.multiple_of(step * rows, rows), rows)
        for c in range(6):
            prod[at, c * 128 : c * 128 + 128] = terms[c].astype(bf16)

    @pl.when(step >= 2)
    def _():
        sums = jnp.dot(ana[...], prod[...], preferred_element_type=f32)
        for c in range(6):
            part = sums[:, c * 128 : c * 128 + 128] * weight[...]
            out[:, c * 128 : c * 128 + 128] = part.astype(bf16)


def grid_stage(lat, syn, ana, weight):
    rows = 512
    return pl.pallas_call(
        grid_kernel,
        grid=(4,),
        in_specs=[
            pl.BlockSpec((8, 24, 64, 128), lambda i: (0, 0, 0, 0)),
            pl.BlockSpec((rows, 1024), lambda i: (jnp.minimum(i, 1), 0)),
            pl.BlockSpec((rows, 1024), lambda i: (jnp.maximum(i - 2, 0), 0)),
            pl.BlockSpec((1, 128), lambda i: (0, 0)),
        ],
        out_specs=pl.BlockSpec((rows, 768), lambda i: (jnp.maximum(i - 2, 0), 0)),
        out_shape=jax.ShapeDtypeStruct((1024, 768), bf16),
        scratch_shapes=[pltpu.VMEM((1024, 1536), bf16), pltpu.VMEM((1024, 768), bf16)],
        compiler_params=pltpu.CompilerParams(vmem_limit_bytes=32 * MIB),
        cost_estimate=pl.CostEstimate(flops=int(4.8e9), bytes_accessed=9 * MIB, transcendentals=0),
        name="grid_stage",
    )(lat, syn, ana, weight)


def tables_kernel(lower, slots, targets, natural_s, natural_a, pairs, syn, ana, table_out, scr):
    ids = lax.broadcasted_iota(jnp.int32, (L, L), 0)
    pick = jnp.where(ids == slots[...], 1.0, 0.0).astype(bf16)
    for p in range(2):
        at = slice(p * L, p * L + L)
        syn[:, at] = jnp.dot(natural_s[:, at], pick, preferred_element_type=f32).astype(bf16)
    ids = lax.broadcasted_iota(jnp.int32, (2 * L, 2 * L), 0)
    pick = jnp.where(ids == targets[...], 1.0, 0.0).astype(bf16)
    ana[...] = lax.dot_general(
        pick, natural_a[...], (((0,), (0,)), ((), ())), preferred_element_type=f32
    ).astype(bf16)
    l_row = lax.broadcasted_iota(jnp.int32, (1, L), 1)
    for i in range(2):
        m = lower[i]
        scr[...] = pairs[i].astype(f32)
        a = jnp.transpose(scr[0:L, :])
        a = pltpu.roll(a, m, 1)
        table_out[2 * i] = jnp.where(l_row >= m, a, 0.0).astype(bf16)
        b = jnp.transpose(scr[1 : L + 1, :])
        table_out[2 * i + 1] = jnp.where(l_row >= L - 1 - m, b, 0.0).astype(bf16)


def make_tables(own_lower, order_slots, pairs):
    natural_s, natural_a = natural_tables()
    slots = order_slots.reshape(8, 16, 4).transpose(1, 0, 2)[..., None]
    targets = (slots + jnp.arange(2, dtype=jnp.int32) * L).reshape(1, 2 * L)
    whole = lambda *shape: pl.BlockSpec(shape, lambda g: (0,) * len(shape))
    return pl.pallas_call(
        tables_kernel,
        grid=(1,),
        in_specs=[
            pl.BlockSpec(memory_space=pltpu.SMEM),
            whole(1, L),
            whole(1, 2 * L),
            whole(NPHI, 2 * L),
            whole(2 * L, NPHI),
            whole(2, L + 16, NH),
        ],
        out_specs=[whole(NPHI, 2 * L), whole(2 * L, NPHI), whole(4, NH, L)],
        out_shape=[
            jax.ShapeDtypeStruct((NPHI, 2 * L), bf16),
            jax.ShapeDtypeStruct((2 * L, NPHI), bf16),
            jax.ShapeDtypeStruct((4, NH, L), bf16),
        ],
        scratch_shapes=[pltpu.VMEM((L + 16, NH), f32)],
        compiler_params=pltpu.CompilerParams(vmem_limit_bytes=40 * MIB),
        cost_estimate=pl.CostEstimate(flops=int(4e9), bytes_accessed=12 * MIB, transcendentals=0),
        name="make_tables",
    )(own_lower, order_slots.reshape(1, L), targets, jnp.asarray(natural_s), jnp.asarray(natural_a), pairs)


def factors_kernel(place, *refs):
    parts, (factors, extra) = refs[:16], refs[16:]
    for r in range(16):
        extra[partner(place[0], place[1], r)] = parts[r][...].astype(f32)
    l_row = lax.broadcasted_iota(jnp.int32, (1, L), 1)
    degree = l_row.astype(f32)
    degree_term = degree * (degree + 1.0)
    below, angle = [[], []], [[], []]
    for d in range(16):
        x = extra[d]
        value = (x[0:8, 0:128] + x[0:8, 128:256]) + x[0:8, 256:384]
        value = jnp.concatenate([value] * 4, axis=1)
        for f in range(2):
            for s in range(2):
                below[f].append(value[f * 2 + s : f * 2 + s + 1])
                angle[f].append(value[4 + f * 2 + s : 4 + f * 2 + s + 1])
    for f in range(2):
        carried = jnp.zeros((1, L), f32)
        for s in range(32):
            under = below[f][s]
            above = below[f][s + 1] if s < 31 else jnp.zeros((1, L), f32)
            diagonal = 1.0 + under + above + angle[f][s] * degree_term
            inverse = 1.0 / (diagonal - under * carried)
            carried = above * inverse
            row = f * 32 + s
            factors[0, row : row + 1, :] = inverse
            factors[1, row : row + 1, :] = under * inverse
            factors[2, row : row + 1, :] = carried


def solve_factors(place, parts):
    return pl.pallas_call(
        factors_kernel,
        grid=(1,),
        in_specs=[pl.BlockSpec(memory_space=pltpu.SMEM)]
        + [pl.BlockSpec((16, L), lambda g: (6, 0))] * 16,
        out_specs=pl.BlockSpec((3, 64, L), lambda g: (0, 0, 0)),
        out_shape=jax.ShapeDtypeStruct((3, 64, L), f32),
        scratch_shapes=[pltpu.VMEM((16, 16, L), f32)],
        compiler_params=pltpu.CompilerParams(vmem_limit_bytes=60 * MIB),
        cost_estimate=pl.CostEstimate(flops=10**6, bytes_accessed=MIB, transcendentals=0),
        name="solve_factors",
    )(place, *parts)


def solve_kernel(place, lower, coef, table, factors, *refs):
    parts, (out, cs, lhs, rhs, state) = refs[:16], refs[16:]
    for r in range(16):
        state[partner(place[0], place[1], r)] = parts[r][...]
    for c in range(6):
        cs[c] = coef[:, c * 128 : c * 128 + 128].astype(f32)
    l_row = lax.broadcasted_iota(jnp.int32, (1, L), 1)
    for k in range(4):
        m = lower[k // 2]
        order = m if k % 2 == 0 else L - 1 - m
        half_sign = 0.5 * (1 - 2 * ((l_row + order) & 1)).astype(f32)
        for h in range(2):
            for c in range(6):
                for p in range(2):
                    row = ((h * 6 + c) * 2 + p) * 32
                    for jh in range(2):
                        start = h * 16 + jh * 8 + k * 2 + p
                        lhs[k % 2, row : row + 32, jh * 128 : jh * 128 + 128] = cs[
                            c, pl.ds(start, 32, stride=32), :
                        ].astype(bf16)
        res = jnp.dot(lhs[k % 2], table[k], preferred_element_type=f32)
        half = 0.5 * res[0:384] + half_sign * res[384:768]
        for cp in range(12):
            store(rhs, pl.ds(cp * 4 + k, 32, stride=48), half[cp * 32 : cp * 32 + 32])

    def factor(kind, f, s):
        return factors[kind, pl.ds(f * 32 + s, 1), :]

    def forward(d, running):
        running = list(running)
        block = state[d].astype(f32)
        for s2 in range(2):
            s = 2 * d + s2
            for f in range(2):
                base = s * 48 + f * 24
                value = load(rhs, pl.ds(base, 24)) + block[s2 * 48 + f * 24 : s2 * 48 + f * 24 + 24]
                running[f] = factor(0, f, s) * value + factor(1, f, s) * running[f]
                store(rhs, pl.ds(base, 24), running[f])
        return tuple(running)

    zero = jnp.zeros((24, L), f32)
    lax.fori_loop(0, 16, forward, (zero, zero))

    def backward(step, carried):
        d = 15 - step
        carried = list(carried)
        pieces = [None] * 4
        for s2 in (1, 0):
            s = 2 * d + s2
            for f in range(2):
                value = load(rhs, pl.ds(s * 48 + f * 24, 24))
                carried[f] = value + factor(2, f, s) * carried[f]
                pieces[s2 * 2 + f] = carried[f]
        out[d] = jnp.concatenate(pieces, axis=0).astype(bf16)
        return tuple(carried)

    lax.fori_loop(0, 16, backward, (zero, zero))


def analysis_and_solve(place, own_lower, coef, table, factors, parts):
    small = pl.BlockSpec(memory_space=pltpu.SMEM)
    return pl.pallas_call(
        solve_kernel,
        grid=(1,),
        in_specs=[
            small,
            small,
            pl.BlockSpec((1024, 768), lambda g: (0, 0)),
            pl.BlockSpec((4, NH, L), lambda g: (0, 0, 0)),
            pl.BlockSpec((3, 64, L), lambda g: (0, 0, 0)),
        ]
        + [pl.BlockSpec((96, L), lambda g: (0, 0))] * 16,
        out_specs=pl.BlockSpec((16, 96, L), lambda g: (0, 0, 0)),
        out_shape=jax.ShapeDtypeStruct((16, 96, L), bf16),
        scratch_shapes=[
            pltpu.VMEM((6, 1024, 128), f32),
            pltpu.VMEM((2, 768, NH), bf16),
            pltpu.VMEM((4, 32 * 48, 128), f32),
            pltpu.VMEM((16, 96, L), bf16),
        ],
        compiler_params=pltpu.CompilerParams(vmem_limit_bytes=32 * MIB),
        cost_estimate=pl.CostEstimate(flops=int(0.9e9), bytes_accessed=6 * MIB, transcendentals=0),
        name="analysis_and_solve",
    )(place, own_lower, coef, table, factors, *parts)


def unpack_kernel(got, out_v, out_p, scr, tmp):
    store(scr, pl.ds(0, 768), got[...].astype(f32).reshape(768, L))
    for f, ref in enumerate((out_v, out_p)):
        for c in range(3):
            for p in range(2):
                for k in range(4):
                    row = ((f * 3 + c) * 2 + p) * 4 + k
                    store(tmp, pl.ds(k, 16, stride=4), load(scr, pl.ds(row, 16, stride=48)))
                ref[c, 0, p] = load(tmp, pl.ds(0, 64))


def unpack_solution(got):
    shape = jax.ShapeDtypeStruct((3, 2, 2, 64, L), f32)
    field = pl.BlockSpec((3, 1, 2, 64, L), lambda s: (0, s, 0, 0, 0))
    return pl.pallas_call(
        unpack_kernel,
        grid=(2,),
        in_specs=[pl.BlockSpec((16, 48, L), lambda s: (0, s, 0))],
        out_specs=[field, field],
        out_shape=[shape, shape],
        scratch_shapes=[pltpu.VMEM((4, 768, 128), f32), pltpu.VMEM((4, 64, 128), f32)],
        compiler_params=pltpu.CompilerParams(vmem_limit_bytes=24 * MIB),
        cost_estimate=pl.CostEstimate(flops=10**6, bytes_accessed=5 * MIB, transcendentals=0),
        name="unpack_solution",
    )(got)


def body(
    velocity,
    vorticity,
    magnetic,
    current,
    potential,
    order_slots,
    legendre_values,
    block_lengths,
    coupling,
    angular,
):
    order_rank = lax.axis_index("order")
    shell_rank = lax.axis_index("shell")
    lower = lax.dynamic_slice_in_dim(order_slots, order_rank * 64, 64).reshape(32, 2)[:, 0]
    place = jnp.stack([shell_rank, order_rank & 1]).astype(jnp.int32)
    own_lower = lax.dynamic_slice_in_dim(lower, shell_rank * 2, 2)
    shell_ids = shell_rank * 2 + jnp.arange(2, dtype=jnp.int32)
    starts = jnp.cumsum(block_lengths) - block_lengths
    is_start = jnp.any(shell_ids[:, None] == starts[None, :], axis=1)
    kappa = jnp.where(is_start[None, :], 0.0, coupling)
    rows = (order_rank & 1) * 128 + jnp.arange(128, dtype=jnp.int32)
    colatitude = math.pi * (rows.astype(f32) + 0.5) / NLAT
    weight = (math.sqrt(2.0 * math.pi) * L * math.pi / NLAT * jnp.sin(colatitude))[None, :]

    latitude, pairs = legendre_synthesis(
        place,
        lower,
        velocity,
        vorticity,
        magnetic,
        current,
        jnp.transpose(legendre_values, (1, 0, 2)),
    )
    incoming = lax.all_to_all(latitude, "order", 0, 0, tiled=True)

    order_after, vel_after, pot_after, _ = lax.optimization_barrier(
        (order_slots, velocity, potential, latitude)
    )
    parts = state_to_send(place, kappa, angular, vel_after, pot_after)
    received = [parts[0]]
    for r in range(1, 16):
        swapped = (r & 3) * 4 + r // 4
        pairs_r = [
            (i * 8 + o, (i ^ (swapped if o & 1 else r)) * 8 + o) for i in range(16) for o in range(8)
        ]
        received.append(lax.ppermute(parts[r], ("shell", "order"), pairs_r))
    syn, ana, table = make_tables(own_lower, order_after, pairs)
    factors = solve_factors(place, received)
    incoming, factors, table, received = lax.optimization_barrier(
        (incoming, factors, table, received)
    )

    coefs = grid_stage(incoming, syn, ana, weight)
    coefs = lax.all_to_all(
        coefs.reshape(128, 8, 768), ("shell", "order"), 0, 0, tiled=True
    ).reshape(1024, 768)
    solved = analysis_and_solve(place, own_lower, coefs, table, factors, received)
    solved = lax.all_to_all(solved, "shell", 0, 0, tiled=True)
    return tuple(unpack_solution(solved))


def solution(mesh):
    spectral = P(None, "shell", None, "order", None)
    in_specs = (
        spectral,
        spectral,
        spectral,
        spectral,
        spectral,
        P(),
        P("order", None, None),
        P(),
        P(None, "shell"),
        P(None, "shell"),
    )
    return jax.shard_map(
        body, mesh=mesh, in_specs=in_specs, out_specs=(spectral, spectral), check_vma=False
    )
```

```python
import math

import jax
import jax.numpy as jnp
import numpy as np
from jax import lax
from jax.experimental import pallas as pl
from jax.experimental.pallas import tpu as pltpu
from jax.sharding import PartitionSpec as P

L = 512
NLAT = 512
NPHI = 1024
NH = 256
f32 = jnp.float32
bf16 = jnp.bfloat16
MIB = 1 << 20


def natural_tables():
    phases = (np.arange(L)[:, None] * np.arange(NPHI)[None, :]) % NPHI
    angles = 2.0 * np.pi * phases / NPHI
    rows = np.stack([np.cos(angles), -np.sin(angles)], axis=0)
    weight = np.where(np.arange(L) == 0, 1.0, 2.0) * (math.sqrt(2.0 * math.pi) / L)
    synthesis = (rows * weight[None, :, None]).reshape(2 * L, NPHI)
    analysis = (rows / NPHI).reshape(2 * L, NPHI)
    return synthesis.T.astype(jnp.bfloat16), analysis.astype(jnp.bfloat16)


def partner(place, r):
    swapped = (r & 3) * 4 + r // 4
    return place[0] ^ jnp.where((place[1] & 1) == 1, swapped, r)


def load(ref, rows):
    return jnp.concatenate([ref[q, rows, :] for q in range(ref.shape[0])], axis=1)


def store(ref, rows, value):
    for q in range(ref.shape[0]):
        ref[q, rows, :] = value[:, q * 128 : q * 128 + 128]


PITCH = 33
TABLE_PITCH = 17
CHUNK = 171


def synthesis_kernel(place, orders, vel, vor, mag, cur, table, out, pairs, xs, ys, ts):
    step = pl.program_id(0)
    chunk = pl.program_id(1)

    @pl.when(chunk == 0)
    def _():
        for a, ref in enumerate((vel, vor, mag, cur)):
            for c in range(3):
                for s in range(2):
                    for p in range(2):
                        row = (s * 24 + (a * 3 + c) * 2 + p) * PITCH
                        store(xs, pl.ds(row, 32), ref[c, s, p].astype(f32))

    for q in range(3):

        @pl.when(chunk == q)
        def _():
            for d in range(CHUNK):
                store(ts, pl.ds((q * CHUNK + d) * TABLE_PITCH, 16), table[d].astype(f32))

    r = lax.broadcasted_iota(jnp.int32, (1, L), 1)
    sign_a = (1 - 2 * (r & 1)).astype(f32)

    def one_pair(i, _):
        m = orders[place[1] * 64 + step * 32 + 2 * i]
        a = load(xs, pl.ds(2 * i, 48, stride=PITCH))
        b = load(xs, pl.ds(2 * i + 1, 48, stride=PITCH))
        rows = load(ts, pl.ds(i, L, stride=TABLE_PITCH)).astype(bf16)
        a = pltpu.roll(a, (L - m) & (L - 1), 1)
        b_last = b[:, L - 1 : L]
        b = pltpu.roll(b, 1, 1)
        is_a = r < L - m
        sign_b = (1 - 2 * ((r + m) & 1)).astype(f32)
        a = jnp.where(is_a, a, 0.0)
        b = jnp.where(is_a, 0.0, b)
        lhs = jnp.concatenate([a, a * sign_a, b, b * sign_b], axis=0).astype(bf16)
        res = jnp.dot(lhs, rows, preferred_element_type=f32)
        last = b_last * load(ts, pl.ds(L * TABLE_PITCH + i, 1))
        last_sign = (1 - 2 * (m & 1)).astype(f32)
        b_n = res[96:144] + last
        b_s = res[144:192] + last * last_sign
        for k, parts in ((2 * i, (res[0:48], res[48:96])), (2 * i + 1, (b_n, b_s))):
            for h in range(2):
                for s in range(2):
                    at = pl.ds((s * 2 + h) * 24 * PITCH + k, 24, stride=PITCH)
                    store(ys, at, parts[h][s * 24 : s * 24 + 24])
        return 0

    @pl.when(chunk == 2)
    def _():
        lax.fori_loop(0, 16, one_pair, 0, unroll=8)
        for sh in range(4):
            for jh in range(2):
                for cp in range(24):
                    row = (sh * 24 + cp) * PITCH
                    out[sh * 2 + jh, cp] = ys[jh, row : row + 32, :].astype(bf16)

    @pl.when((chunk == 2) & (step == place[0] // 8))
    def _():
        for i in range(2):
            at = (place[0] & 7) * 2 + i
            pairs[i, 0:L, :] = load(ts, pl.ds(at, L, stride=TABLE_PITCH)).astype(bf16)
            last = load(ts, pl.ds(L * TABLE_PITCH + at, 1))
            pairs[i, L : L + 16, :] = jnp.broadcast_to(last, (16, NH)).astype(bf16)


def legendre_synthesis(place, orders, velocity, vorticity, magnetic, current, table):
    field = pl.BlockSpec((3, 2, 2, 32, L), lambda g, q, place, low: (0, 0, 0, g, 0))
    return pl.pallas_call(
        synthesis_kernel,
        grid_spec=pltpu.PrefetchScalarGridSpec(
            num_scalar_prefetch=2,
            grid=(2, 3),
            in_specs=[field] * 4
            + [pl.BlockSpec((CHUNK, 16, NH), lambda g, q, place, low: (q, g, 0))],
            out_specs=[
                pl.BlockSpec((8, 24, 32, 128), lambda g, q, place, low: (0, 0, g, 0)),
                pl.BlockSpec((2, L + 16, NH), lambda g, q, place, low: (0, 0, 0)),
            ],
            scratch_shapes=[
                pltpu.VMEM((4, 48 * PITCH, 128), f32),
                pltpu.VMEM((2, 96 * PITCH, 128), f32),
                pltpu.VMEM((2, (L + 1) * TABLE_PITCH + 7, 128), f32),
            ],
        ),
        out_shape=[
            jax.ShapeDtypeStruct((8, 24, 64, 128), bf16),
            jax.ShapeDtypeStruct((2, L + 16, NH), bf16),
        ],
        compiler_params=pltpu.CompilerParams(vmem_limit_bytes=60 * MIB),
        cost_estimate=pl.CostEstimate(flops=int(1.6e9), bytes_accessed=15 * MIB, transcendentals=0),
        name="legendre_synthesis",
    )(place, orders, velocity, vorticity, magnetic, current, table)


def state_kernel(place, kappa, angular, vel, pot, *refs):
    outs, scr = refs[:16], refs[16]
    for f, ref in enumerate((vel, pot)):
        for c in range(3):
            for s in range(2):
                for p in range(2):
                    x = ref[c, s, p].astype(f32)
                    row = s * 48 + ((f * 3 + c) * 2 + p) * 4
                    for d in range(16):
                        scr[d, row : row + 4, :] = x[4 * d : 4 * d + 4]
    lane = lax.broadcasted_iota(jnp.int32, (1, L), 1)
    lines = []
    for ref in (kappa, angular):
        for f in range(2):
            for s in range(2):
                value = jnp.full((1, L), ref[f, s], f32)
                high = value.astype(bf16).astype(f32)
                rest = value - high
                mid = rest.astype(bf16).astype(f32)
                low = rest - mid
                lines.append(jnp.where(lane < 128, high, jnp.where(lane < 256, mid, low)))
    extra = jnp.concatenate(lines + [jnp.zeros((8, L), f32)], axis=0).astype(bf16)
    for r in range(16):
        outs[r][0:96, :] = scr[partner(place, r)].astype(bf16)
        outs[r][96:112, :] = extra


def state_to_send(place, kappa, angular, velocity, potential):
    field = pl.BlockSpec((3, 2, 2, 64, L), lambda g: (0, 0, 0, 0, 0))
    small = pl.BlockSpec(memory_space=pltpu.SMEM)
    return pl.pallas_call(
        state_kernel,
        grid=(1,),
        in_specs=[small, small, small, field, field],
        out_specs=[pl.BlockSpec((112, L), lambda g: (0, 0))] * 16,
        out_shape=[jax.ShapeDtypeStruct((112, L), bf16)] * 16,
        scratch_shapes=[pltpu.VMEM((16, 96, L), f32)],
        compiler_params=pltpu.CompilerParams(vmem_limit_bytes=32 * MIB),
        cost_estimate=pl.CostEstimate(flops=10**6, bytes_accessed=4 * MIB, transcendentals=0),
        name="state_to_send",
    )(place, kappa, angular, velocity, potential)


def grid_kernel(lat, syn, ana, weight, out, wide, prod):
    step = pl.program_id(0)
    rows = 512

    @pl.when(step == 0)
    def _():
        for c in range(12):
            for p in range(2):
                rows_p = lat[:, 2 * c + p].reshape(512, 128)
                wide[p * 512 : p * 512 + 512, c * 128 : c * 128 + 128] = rows_p

    @pl.when(step < 2)
    def _():
        g = jnp.dot(syn[...], wide[...], preferred_element_type=f32)
        x = [g[:, c * 128 : c * 128 + 128] for c in range(12)]
        u, w, b, j = x[0:3], x[3:6], x[6:9], x[9:12]

        def cross(p, q):
            return [
                p[1] * q[2] - p[2] * q[1],
                p[2] * q[0] - p[0] * q[2],
                p[0] * q[1] - p[1] * q[0],
            ]

        uw, jb, ub = cross(u, w), cross(j, b), cross(u, b)
        terms = [uw[0] + jb[0] + 2.0 * u[1], uw[1] + jb[1] - 2.0 * u[0], uw[2] + jb[2]] + ub
        at = pl.ds(pl.multiple_of(step * rows, rows), rows)
        for c in range(6):
            prod[at, c * 128 : c * 128 + 128] = terms[c].astype(bf16)

    @pl.when(step >= 2)
    def _():
        sums = jnp.dot(ana[...], prod[...], preferred_element_type=f32)
        for c in range(6):
            part = sums[:, c * 128 : c * 128 + 128] * weight[...]
            out[:, c * 128 : c * 128 + 128] = part.astype(bf16)


def grid_stage(lat, syn, ana, weight):
    rows = 512
    return pl.pallas_call(
        grid_kernel,
        grid=(4,),
        in_specs=[
            pl.BlockSpec((8, 24, 64, 128), lambda i: (0, 0, 0, 0)),
            pl.BlockSpec((rows, 1024), lambda i: (jnp.minimum(i, 1), 0)),
            pl.BlockSpec((rows, 1024), lambda i: (jnp.maximum(i - 2, 0), 0)),
            pl.BlockSpec((1, 128), lambda i: (0, 0)),
        ],
        out_specs=pl.BlockSpec((rows, 768), lambda i: (jnp.maximum(i - 2, 0), 0)),
        out_shape=jax.ShapeDtypeStruct((1024, 768), bf16),
        scratch_shapes=[pltpu.VMEM((1024, 1536), bf16), pltpu.VMEM((1024, 768), bf16)],
        compiler_params=pltpu.CompilerParams(vmem_limit_bytes=60 * MIB),
        cost_estimate=pl.CostEstimate(flops=int(4.8e9), bytes_accessed=9 * MIB, transcendentals=0),
        name="grid_stage",
    )(lat, syn, ana, weight)


def tables_kernel(place, orders, slots, targets, natural_s, natural_a, pairs, syn, ana, table_out, scr):
    ids = lax.broadcasted_iota(jnp.int32, (L, L), 0)
    pick = jnp.where(ids == slots[...], 1.0, 0.0).astype(bf16)
    for p in range(2):
        at = slice(p * L, p * L + L)
        syn[:, at] = jnp.dot(natural_s[:, at], pick, preferred_element_type=f32).astype(bf16)
    ids = lax.broadcasted_iota(jnp.int32, (2 * L, 2 * L), 0)
    pick = jnp.where(ids == targets[...], 1.0, 0.0).astype(bf16)
    ana[...] = lax.dot_general(
        pick, natural_a[...], (((0,), (0,)), ((), ())), preferred_element_type=f32
    ).astype(bf16)
    l_row = lax.broadcasted_iota(jnp.int32, (1, L), 1)
    for i in range(2):
        m = orders[place[1] * 64 + place[0] * 4 + 2 * i]
        scr[...] = pairs[i].astype(f32)
        a = jnp.transpose(scr[0:L, :])
        a = pltpu.roll(a, m, 1)
        table_out[2 * i] = jnp.where(l_row >= m, a, 0.0).astype(bf16)
        b = jnp.transpose(scr[1 : L + 1, :])
        table_out[2 * i + 1] = jnp.where(l_row >= L - 1 - m, b, 0.0).astype(bf16)


def make_tables(place, order_slots, pairs):
    natural_s, natural_a = natural_tables()
    slots = order_slots.reshape(8, 16, 4).transpose(1, 0, 2)[..., None]
    targets = (slots + jnp.arange(2, dtype=jnp.int32) * L).reshape(1, 2 * L)
    whole = lambda *shape: pl.BlockSpec(shape, lambda g: (0,) * len(shape))
    return pl.pallas_call(
        tables_kernel,
        grid=(1,),
        in_specs=[
            pl.BlockSpec(memory_space=pltpu.SMEM),
            pl.BlockSpec(memory_space=pltpu.SMEM),
            whole(1, L),
            whole(1, 2 * L),
            whole(NPHI, 2 * L),
            whole(2 * L, NPHI),
            whole(2, L + 16, NH),
        ],
        out_specs=[whole(NPHI, 2 * L), whole(2 * L, NPHI), whole(4, NH, L)],
        out_shape=[
            jax.ShapeDtypeStruct((NPHI, 2 * L), bf16),
            jax.ShapeDtypeStruct((2 * L, NPHI), bf16),
            jax.ShapeDtypeStruct((4, NH, L), bf16),
        ],
        scratch_shapes=[pltpu.VMEM((L + 16, NH), f32)],
        compiler_params=pltpu.CompilerParams(vmem_limit_bytes=60 * MIB),
        cost_estimate=pl.CostEstimate(flops=int(4e9), bytes_accessed=12 * MIB, transcendentals=0),
        name="make_tables",
    )(
        place,
        order_slots,
        order_slots.reshape(1, L),
        targets,
        jnp.asarray(natural_s),
        jnp.asarray(natural_a),
        pairs,
    )


def factors_kernel(place, *refs):
    parts, (factors, extra) = refs[:16], refs[16:]
    for r in range(16):
        extra[partner(place, r)] = parts[r][...].astype(f32)
    l_row = lax.broadcasted_iota(jnp.int32, (1, L), 1)
    degree = l_row.astype(f32)
    degree_term = degree * (degree + 1.0)
    below, angle = [[], []], [[], []]
    for d in range(16):
        x = extra[d]
        value = (x[0:8, 0:128] + x[0:8, 128:256]) + x[0:8, 256:384]
        value = jnp.concatenate([value] * 4, axis=1)
        for f in range(2):
            for s in range(2):
                below[f].append(value[f * 2 + s : f * 2 + s + 1])
                angle[f].append(value[4 + f * 2 + s : 4 + f * 2 + s + 1])
    for f in range(2):
        carried = jnp.zeros((1, L), f32)
        for s in range(32):
            under = below[f][s]
            above = below[f][s + 1] if s < 31 else jnp.zeros((1, L), f32)
            diagonal = 1.0 + under + above + angle[f][s] * degree_term
            inverse = 1.0 / (diagonal - under * carried)
            carried = above * inverse
            row = f * 32 + s
            factors[0, row : row + 1, :] = inverse
            factors[1, row : row + 1, :] = under * inverse
            factors[2, row : row + 1, :] = carried


def solve_factors(place, parts):
    return pl.pallas_call(
        factors_kernel,
        grid=(1,),
        in_specs=[pl.BlockSpec(memory_space=pltpu.SMEM)]
        + [pl.BlockSpec((16, L), lambda g: (6, 0))] * 16,
        out_specs=pl.BlockSpec((3, 64, L), lambda g: (0, 0, 0)),
        out_shape=jax.ShapeDtypeStruct((3, 64, L), f32),
        scratch_shapes=[pltpu.VMEM((16, 16, L), f32)],
        compiler_params=pltpu.CompilerParams(vmem_limit_bytes=60 * MIB),
        cost_estimate=pl.CostEstimate(flops=10**6, bytes_accessed=MIB, transcendentals=0),
        name="solve_factors",
    )(place, *parts)


def solve_kernel(place, orders, coef, table, factors_hbm, *refs):
    parts, (out, cs, lhs, rhs, state, factors, sems) = refs[:16], refs[16:]
    copies = [pltpu.make_async_copy(factors_hbm, factors, sems.at[16])]
    for r in range(16):
        source = parts[r].at[pl.ds(0, 96)]
        copies.append(pltpu.make_async_copy(source, state.at[partner(place, r)], sems.at[r]))
    for copy in copies:
        copy.start()
    for c in range(6):
        cs[c] = coef[:, c * 128 : c * 128 + 128].astype(f32)
    l_row = lax.broadcasted_iota(jnp.int32, (1, L), 1)
    for k in range(4):
        m = orders[place[1] * 64 + place[0] * 4 + k // 2 * 2]
        order = m if k % 2 == 0 else L - 1 - m
        half_sign = 0.5 * (1 - 2 * ((l_row + order) & 1)).astype(f32)
        for h in range(2):
            for c in range(6):
                for p in range(2):
                    row = ((h * 6 + c) * 2 + p) * 32
                    for jh in range(2):
                        start = h * 16 + jh * 8 + k * 2 + p
                        lhs[k % 2, row : row + 32, jh * 128 : jh * 128 + 128] = cs[
                            c, pl.ds(start, 32, stride=32), :
                        ].astype(bf16)
        res = jnp.dot(lhs[k % 2], table[k], preferred_element_type=f32)
        half = 0.5 * res[0:384] + half_sign * res[384:768]
        for cp in range(12):
            store(rhs, pl.ds(cp * 4 + k, 32, stride=48), half[cp * 32 : cp * 32 + 32])

    for copy in copies:
        copy.wait()

    def factor(kind, f, s):
        return factors[kind, pl.ds(f * 32 + s, 1), :]

    def forward(d, running):
        running = list(running)
        block = state[d].astype(f32)
        for s2 in range(2):
            s = 2 * d + s2
            for f in range(2):
                base = s * 48 + f * 24
                value = load(rhs, pl.ds(base, 24)) + block[s2 * 48 + f * 24 : s2 * 48 + f * 24 + 24]
                running[f] = factor(0, f, s) * value + factor(1, f, s) * running[f]
                store(rhs, pl.ds(base, 24), running[f])
        return tuple(running)

    zero = jnp.zeros((24, L), f32)
    lax.fori_loop(0, 16, forward, (zero, zero))

    def backward(step, carried):
        d = 15 - step
        carried = list(carried)
        pieces = [None] * 4
        for s2 in (1, 0):
            s = 2 * d + s2
            for f in range(2):
                value = load(rhs, pl.ds(s * 48 + f * 24, 24))
                carried[f] = value + factor(2, f, s) * carried[f]
                pieces[s2 * 2 + f] = carried[f]
        out[d] = jnp.concatenate(pieces, axis=0).astype(bf16)
        return tuple(carried)

    lax.fori_loop(0, 16, backward, (zero, zero))


def analysis_and_solve(place, orders, coef, table, factors, parts):
    small = pl.BlockSpec(memory_space=pltpu.SMEM)
    return pl.pallas_call(
        solve_kernel,
        grid=(1,),
        in_specs=[
            small,
            small,
            pl.BlockSpec((1024, 768), lambda g: (0, 0)),
            pl.BlockSpec((4, NH, L), lambda g: (0, 0, 0)),
        ]
        + [pl.BlockSpec(memory_space=pltpu.HBM)] * 17,
        out_specs=pl.BlockSpec((16, 96, L), lambda g: (0, 0, 0)),
        out_shape=jax.ShapeDtypeStruct((16, 96, L), bf16),
        scratch_shapes=[
            pltpu.VMEM((6, 1024, 128), f32),
            pltpu.VMEM((2, 768, NH), bf16),
            pltpu.VMEM((4, 32 * 48, 128), f32),
            pltpu.VMEM((16, 96, L), bf16),
            pltpu.VMEM((3, 64, L), f32),
            pltpu.SemaphoreType.DMA((17,)),
        ],
        compiler_params=pltpu.CompilerParams(vmem_limit_bytes=60 * MIB),
        cost_estimate=pl.CostEstimate(flops=int(0.9e9), bytes_accessed=6 * MIB, transcendentals=0),
        name="analysis_and_solve",
    )(place, orders, coef, table, factors, *parts)


def unpack_kernel(got, out_v, out_p, scr, tmp):
    store(scr, pl.ds(0, 768), got[...].astype(f32).reshape(768, L))
    for f, ref in enumerate((out_v, out_p)):
        for c in range(3):
            for p in range(2):
                for k in range(4):
                    row = ((f * 3 + c) * 2 + p) * 4 + k
                    store(tmp, pl.ds(k, 16, stride=4), load(scr, pl.ds(row, 16, stride=48)))
                ref[c, 0, p] = load(tmp, pl.ds(0, 64))


def unpack_solution(got):
    shape = jax.ShapeDtypeStruct((3, 2, 2, 64, L), f32)
    field = pl.BlockSpec((3, 1, 2, 64, L), lambda s: (0, s, 0, 0, 0))
    return pl.pallas_call(
        unpack_kernel,
        grid=(2,),
        in_specs=[pl.BlockSpec((16, 48, L), lambda s: (0, s, 0))],
        out_specs=[field, field],
        out_shape=[shape, shape],
        scratch_shapes=[pltpu.VMEM((4, 768, 128), f32), pltpu.VMEM((4, 64, 128), f32)],
        compiler_params=pltpu.CompilerParams(vmem_limit_bytes=24 * MIB),
        cost_estimate=pl.CostEstimate(flops=10**6, bytes_accessed=5 * MIB, transcendentals=0),
        name="unpack_solution",
    )(got)


def body(
    velocity,
    vorticity,
    magnetic,
    current,
    potential,
    order_slots,
    legendre_values,
    block_lengths,
    coupling,
    angular,
):
    order_rank = lax.axis_index("order")
    shell_rank = lax.axis_index("shell")
    place = jnp.stack([shell_rank, order_rank]).astype(jnp.int32)
    shell_ids = shell_rank * 2 + jnp.arange(2, dtype=jnp.int32)
    starts = jnp.cumsum(block_lengths) - block_lengths
    is_start = jnp.any(shell_ids[:, None] == starts[None, :], axis=1)
    kappa = jnp.where(is_start[None, :], 0.0, coupling)
    rows = (order_rank & 1) * 128 + jnp.arange(128, dtype=jnp.int32)
    colatitude = math.pi * (rows.astype(f32) + 0.5) / NLAT
    weight = (math.sqrt(2.0 * math.pi) * L * math.pi / NLAT * jnp.sin(colatitude))[None, :]

    latitude, pairs = legendre_synthesis(
        place,
        order_slots,
        velocity,
        vorticity,
        magnetic,
        current,
        jnp.transpose(legendre_values, (1, 0, 2)),
    )
    incoming = lax.all_to_all(latitude, "order", 0, 0, tiled=True)

    order_after, vel_after, pot_after, _ = lax.optimization_barrier(
        (order_slots, velocity, potential, latitude)
    )
    parts = state_to_send(place, kappa, angular, vel_after, pot_after)
    received = [parts[0]]
    for r in range(1, 16):
        swapped = (r & 3) * 4 + r // 4
        pairs_r = [
            (i * 8 + o, (i ^ (swapped if o & 1 else r)) * 8 + o) for i in range(16) for o in range(8)
        ]
        received.append(lax.ppermute(parts[r], ("shell", "order"), pairs_r))
    syn, ana, table = make_tables(place, order_after, pairs)
    incoming, table, received = lax.optimization_barrier((incoming, table, received))

    coefs = grid_stage(incoming, syn, ana, weight)
    received, _ = lax.optimization_barrier((received, coefs))
    factors = solve_factors(place, received)
    coefs = lax.all_to_all(
        coefs.reshape(128, 8, 768), ("shell", "order"), 0, 0, tiled=True
    ).reshape(1024, 768)
    solved = analysis_and_solve(place, order_slots, coefs, table, factors, received)
    solved = lax.all_to_all(solved, "shell", 0, 0, tiled=True)
    return tuple(unpack_solution(solved))


def solution(mesh):
    spectral = P(None, "shell", None, "order", None)
    in_specs = (
        spectral,
        spectral,
        spectral,
        spectral,
        spectral,
        P(),
        P("order", None, None),
        P(),
        P(None, "shell"),
        P(None, "shell"),
    )
    return jax.shard_map(
        body, mesh=mesh, in_specs=in_specs, out_specs=(spectral, spectral), check_vma=False
    )
```

```python
import math

import jax
import jax.numpy as jnp
import numpy as np
from jax import lax
from jax.experimental import pallas as pl
from jax.experimental.pallas import tpu as pltpu
from jax.sharding import PartitionSpec as P

L = 512
NLAT = 512
NPHI = 1024
NH = 256
f32 = jnp.float32
bf16 = jnp.bfloat16
MIB = 1 << 20


def natural_tables():
    phases = (np.arange(L)[:, None] * np.arange(NPHI)[None, :]) % NPHI
    angles = 2.0 * np.pi * phases / NPHI
    rows = np.stack([np.cos(angles), -np.sin(angles)], axis=0)
    weight = np.where(np.arange(L) == 0, 1.0, 2.0) * (math.sqrt(2.0 * math.pi) / L)
    synthesis = (rows * weight[None, :, None]).reshape(2 * L, NPHI)
    analysis = (rows / NPHI).reshape(2 * L, NPHI)
    return synthesis.T.astype(jnp.bfloat16), analysis.astype(jnp.bfloat16)


def partner(place, r):
    swapped = (r & 3) * 4 + r // 4
    return place[0] ^ jnp.where((place[1] & 1) == 1, swapped, r)


def load(ref, rows):
    return jnp.concatenate([ref[q, rows, :] for q in range(ref.shape[0])], axis=1)


def store(ref, rows, value):
    for q in range(ref.shape[0]):
        ref[q, rows, :] = value[:, q * 128 : q * 128 + 128]


PITCH = 33
TABLE_PITCH = 17
CHUNK = 171


def synthesis_kernel(place, orders, vel, vor, mag, cur, table, out, pairs, xs, ys, ts):
    step = pl.program_id(0)
    chunk = pl.program_id(1)

    @pl.when(chunk == 0)
    def _():
        for a, ref in enumerate((vel, vor, mag, cur)):
            for c in range(3):
                for s in range(2):
                    for p in range(2):
                        row = (s * 24 + (a * 3 + c) * 2 + p) * PITCH
                        store(xs, pl.ds(row, 32), ref[c, s, p].astype(f32))

    for q in range(3):

        @pl.when(chunk == q)
        def _():
            for d in range(CHUNK):
                store(ts, pl.ds((q * CHUNK + d) * TABLE_PITCH, 16), table[d].astype(f32))

    r = lax.broadcasted_iota(jnp.int32, (1, L), 1)
    sign_a = (1 - 2 * (r & 1)).astype(f32)

    def one_pair(i, _):
        m = orders[place[1] * 64 + step * 32 + 2 * i]
        a = load(xs, pl.ds(2 * i, 48, stride=PITCH))
        b = load(xs, pl.ds(2 * i + 1, 48, stride=PITCH))
        rows = load(ts, pl.ds(i, L, stride=TABLE_PITCH)).astype(bf16)
        a = pltpu.roll(a, (L - m) & (L - 1), 1)
        b_last = b[:, L - 1 : L]
        b = pltpu.roll(b, 1, 1)
        is_a = r < L - m
        sign_b = (1 - 2 * ((r + m) & 1)).astype(f32)
        a = jnp.where(is_a, a, 0.0)
        b = jnp.where(is_a, 0.0, b)
        lhs = jnp.concatenate([a, a * sign_a, b, b * sign_b], axis=0).astype(bf16)
        res = jnp.dot(lhs, rows, preferred_element_type=f32)
        last = b_last * load(ts, pl.ds(L * TABLE_PITCH + i, 1))
        last_sign = (1 - 2 * (m & 1)).astype(f32)
        b_n = res[96:144] + last
        b_s = res[144:192] + last * last_sign
        for k, parts in ((2 * i, (res[0:48], res[48:96])), (2 * i + 1, (b_n, b_s))):
            for h in range(2):
                for s in range(2):
                    at = pl.ds((s * 2 + h) * 24 * PITCH + k, 24, stride=PITCH)
                    store(ys, at, parts[h][s * 24 : s * 24 + 24])
        return 0

    @pl.when(chunk == 2)
    def _():
        lax.fori_loop(0, 16, one_pair, 0, unroll=8)
        for sh in range(4):
            for jh in range(2):
                for cp in range(24):
                    row = (sh * 24 + cp) * PITCH
                    out[sh * 2 + jh, cp] = ys[jh, row : row + 32, :].astype(bf16)

    @pl.when((chunk == 2) & (step == place[0] // 8))
    def _():
        for i in range(2):
            at = (place[0] & 7) * 2 + i
            pairs[i, 0:L, :] = load(ts, pl.ds(at, L, stride=TABLE_PITCH)).astype(bf16)
            last = load(ts, pl.ds(L * TABLE_PITCH + at, 1))
            pairs[i, L : L + 16, :] = jnp.broadcast_to(last, (16, NH)).astype(bf16)


def legendre_synthesis(place, orders, velocity, vorticity, magnetic, current, table):
    field = pl.BlockSpec((3, 2, 2, 32, L), lambda g, q, place, low: (0, 0, 0, g, 0))
    return pl.pallas_call(
        synthesis_kernel,
        grid_spec=pltpu.PrefetchScalarGridSpec(
            num_scalar_prefetch=2,
            grid=(2, 3),
            in_specs=[field] * 4
            + [pl.BlockSpec((CHUNK, 16, NH), lambda g, q, place, low: (q, g, 0))],
            out_specs=[
                pl.BlockSpec((8, 24, 32, 128), lambda g, q, place, low: (0, 0, g, 0)),
                pl.BlockSpec((2, L + 16, NH), lambda g, q, place, low: (0, 0, 0)),
            ],
            scratch_shapes=[
                pltpu.VMEM((4, 48 * PITCH, 128), f32),
                pltpu.VMEM((2, 96 * PITCH, 128), f32),
                pltpu.VMEM((2, (L + 1) * TABLE_PITCH + 7, 128), f32),
            ],
        ),
        out_shape=[
            jax.ShapeDtypeStruct((8, 24, 64, 128), bf16),
            jax.ShapeDtypeStruct((2, L + 16, NH), bf16),
        ],
        compiler_params=pltpu.CompilerParams(vmem_limit_bytes=60 * MIB),
        cost_estimate=pl.CostEstimate(flops=int(1.6e9), bytes_accessed=15 * MIB, transcendentals=0),
        name="legendre_synthesis",
    )(place, orders, velocity, vorticity, magnetic, current, table)


def state_kernel(place, kappa, angular, vel, pot, *refs):
    outs, scr = refs[:16], refs[16]
    for f, ref in enumerate((vel, pot)):
        for c in range(3):
            for s in range(2):
                for p in range(2):
                    x = ref[c, s, p].astype(f32)
                    row = s * 48 + ((f * 3 + c) * 2 + p) * 4
                    for d in range(16):
                        scr[d, row : row + 4, :] = x[4 * d : 4 * d + 4]
    lane = lax.broadcasted_iota(jnp.int32, (1, L), 1)
    lines = []
    for ref in (kappa, angular):
        for f in range(2):
            for s in range(2):
                value = jnp.full((1, L), ref[f, s], f32)
                high = value.astype(bf16).astype(f32)
                rest = value - high
                mid = rest.astype(bf16).astype(f32)
                low = rest - mid
                lines.append(jnp.where(lane < 128, high, jnp.where(lane < 256, mid, low)))
    extra = jnp.concatenate(lines + [jnp.zeros((8, L), f32)], axis=0).astype(bf16)
    for r in range(16):
        outs[r][0:96, :] = scr[partner(place, r)].astype(bf16)
        outs[r][96:112, :] = extra


def state_to_send(place, kappa, angular, velocity, potential):
    field = pl.BlockSpec((3, 2, 2, 64, L), lambda g: (0, 0, 0, 0, 0))
    small = pl.BlockSpec(memory_space=pltpu.SMEM)
    return pl.pallas_call(
        state_kernel,
        grid=(1,),
        in_specs=[small, small, small, field, field],
        out_specs=[pl.BlockSpec((112, L), lambda g: (0, 0))] * 16,
        out_shape=[jax.ShapeDtypeStruct((112, L), bf16)] * 16,
        scratch_shapes=[pltpu.VMEM((16, 96, L), f32)],
        compiler_params=pltpu.CompilerParams(vmem_limit_bytes=32 * MIB),
        cost_estimate=pl.CostEstimate(flops=10**6, bytes_accessed=4 * MIB, transcendentals=0),
        name="state_to_send",
    )(place, kappa, angular, velocity, potential)


def grid_kernel(lat, syn, ana, weight, out, wide, prod):
    step = pl.program_id(0)
    rows = 512

    @pl.when(step == 0)
    def _():
        for c in range(12):
            for p in range(2):
                rows_p = lat[:, 2 * c + p].reshape(512, 128)
                wide[p * 512 : p * 512 + 512, c * 128 : c * 128 + 128] = rows_p

    @pl.when(step < 2)
    def _():
        g = jnp.dot(syn[...], wide[...], preferred_element_type=f32)
        x = [g[:, c * 128 : c * 128 + 128] for c in range(12)]
        u, w, b, j = x[0:3], x[3:6], x[6:9], x[9:12]

        def cross(p, q):
            return [
                p[1] * q[2] - p[2] * q[1],
                p[2] * q[0] - p[0] * q[2],
                p[0] * q[1] - p[1] * q[0],
            ]

        uw, jb, ub = cross(u, w), cross(j, b), cross(u, b)
        terms = [uw[0] + jb[0] + 2.0 * u[1], uw[1] + jb[1] - 2.0 * u[0], uw[2] + jb[2]] + ub
        at = pl.ds(pl.multiple_of(step * rows, rows), rows)
        for c in range(6):
            prod[at, c * 128 : c * 128 + 128] = terms[c].astype(bf16)

    @pl.when(step >= 2)
    def _():
        sums = jnp.dot(ana[...], prod[...], preferred_element_type=f32)
        for c in range(6):
            part = sums[:, c * 128 : c * 128 + 128] * weight[...]
            out[:, c * 128 : c * 128 + 128] = part.astype(bf16)


def grid_stage(lat, syn, ana, weight):
    rows = 512
    return pl.pallas_call(
        grid_kernel,
        grid=(4,),
        in_specs=[
            pl.BlockSpec((8, 24, 64, 128), lambda i: (0, 0, 0, 0)),
            pl.BlockSpec((rows, 1024), lambda i: (jnp.minimum(i, 1), 0)),
            pl.BlockSpec((rows, 1024), lambda i: (jnp.maximum(i - 2, 0), 0)),
            pl.BlockSpec((1, 128), lambda i: (0, 0)),
        ],
        out_specs=pl.BlockSpec((rows, 768), lambda i: (jnp.maximum(i - 2, 0), 0)),
        out_shape=jax.ShapeDtypeStruct((1024, 768), bf16),
        scratch_shapes=[pltpu.VMEM((1024, 1536), bf16), pltpu.VMEM((1024, 768), bf16)],
        compiler_params=pltpu.CompilerParams(vmem_limit_bytes=60 * MIB),
        cost_estimate=pl.CostEstimate(flops=int(4.8e9), bytes_accessed=9 * MIB, transcendentals=0),
        name="grid_stage",
    )(lat, syn, ana, weight)


def tables_kernel(place, orders, slots, targets, natural_s, natural_a, pairs, syn, ana, table_out, scr):
    ids = lax.broadcasted_iota(jnp.int32, (L, L), 0)
    pick = jnp.where(ids == slots[...], 1.0, 0.0).astype(bf16)
    for p in range(2):
        at = slice(p * L, p * L + L)
        syn[:, at] = jnp.dot(natural_s[:, at], pick, preferred_element_type=f32).astype(bf16)
    ids = lax.broadcasted_iota(jnp.int32, (2 * L, 2 * L), 0)
    pick = jnp.where(ids == targets[...], 1.0, 0.0).astype(bf16)
    ana[...] = lax.dot_general(
        pick, natural_a[...], (((0,), (0,)), ((), ())), preferred_element_type=f32
    ).astype(bf16)
    l_row = lax.broadcasted_iota(jnp.int32, (1, L), 1)
    for i in range(2):
        m = orders[place[1] * 64 + place[0] * 4 + 2 * i]
        scr[...] = pairs[i].astype(f32)
        a = jnp.transpose(scr[0:L, :])
        a = pltpu.roll(a, m, 1)
        table_out[2 * i] = jnp.where(l_row >= m, a, 0.0).astype(bf16)
        b = jnp.transpose(scr[1 : L + 1, :])
        table_out[2 * i + 1] = jnp.where(l_row >= L - 1 - m, b, 0.0).astype(bf16)


def make_tables(place, order_slots, pairs):
    natural_s, natural_a = natural_tables()
    slots = order_slots.reshape(8, 16, 4).transpose(1, 0, 2)[..., None]
    targets = (slots + jnp.arange(2, dtype=jnp.int32) * L).reshape(1, 2 * L)
    whole = lambda *shape: pl.BlockSpec(shape, lambda g: (0,) * len(shape))
    return pl.pallas_call(
        tables_kernel,
        grid=(1,),
        in_specs=[
            pl.BlockSpec(memory_space=pltpu.SMEM),
            pl.BlockSpec(memory_space=pltpu.SMEM),
            whole(1, L),
            whole(1, 2 * L),
            whole(NPHI, 2 * L),
            whole(2 * L, NPHI),
            whole(2, L + 16, NH),
        ],
        out_specs=[whole(NPHI, 2 * L), whole(2 * L, NPHI), whole(4, NH, L)],
        out_shape=[
            jax.ShapeDtypeStruct((NPHI, 2 * L), bf16),
            jax.ShapeDtypeStruct((2 * L, NPHI), bf16),
            jax.ShapeDtypeStruct((4, NH, L), bf16),
        ],
        scratch_shapes=[pltpu.VMEM((L + 16, NH), f32)],
        compiler_params=pltpu.CompilerParams(vmem_limit_bytes=60 * MIB),
        cost_estimate=pl.CostEstimate(flops=int(4e9), bytes_accessed=12 * MIB, transcendentals=0),
        name="make_tables",
    )(
        place,
        order_slots,
        order_slots.reshape(1, L),
        targets,
        jnp.asarray(natural_s),
        jnp.asarray(natural_a),
        pairs,
    )


def factors_kernel(place, *refs):
    parts, (state, factors, extra) = refs[:16], refs[16:]
    for r in range(16):
        state[partner(place, r)] = parts[r][0:96, :]
        extra[partner(place, r)] = parts[r][96:112, :].astype(f32)
    l_row = lax.broadcasted_iota(jnp.int32, (1, L), 1)
    degree = l_row.astype(f32)
    degree_term = degree * (degree + 1.0)
    below, angle = [[], []], [[], []]
    for d in range(16):
        x = extra[d]
        value = (x[0:8, 0:128] + x[0:8, 128:256]) + x[0:8, 256:384]
        value = jnp.concatenate([value] * 4, axis=1)
        for f in range(2):
            for s in range(2):
                below[f].append(value[f * 2 + s : f * 2 + s + 1])
                angle[f].append(value[4 + f * 2 + s : 4 + f * 2 + s + 1])
    for f in range(2):
        carried = jnp.zeros((1, L), f32)
        for s in range(32):
            under = below[f][s]
            above = below[f][s + 1] if s < 31 else jnp.zeros((1, L), f32)
            diagonal = 1.0 + under + above + angle[f][s] * degree_term
            inverse = 1.0 / (diagonal - under * carried)
            carried = above * inverse
            row = f * 32 + s
            factors[0, row : row + 1, :] = inverse
            factors[1, row : row + 1, :] = under * inverse
            factors[2, row : row + 1, :] = carried


def solve_factors(place, parts):
    return pl.pallas_call(
        factors_kernel,
        grid=(1,),
        in_specs=[pl.BlockSpec(memory_space=pltpu.SMEM)]
        + [pl.BlockSpec((112, L), lambda g: (0, 0))] * 16,
        out_specs=[
            pl.BlockSpec((16, 96, L), lambda g: (0, 0, 0)),
            pl.BlockSpec((3, 64, L), lambda g: (0, 0, 0)),
        ],
        out_shape=[
            jax.ShapeDtypeStruct((16, 96, L), bf16),
            jax.ShapeDtypeStruct((3, 64, L), f32),
        ],
        scratch_shapes=[pltpu.VMEM((16, 16, L), f32)],
        compiler_params=pltpu.CompilerParams(vmem_limit_bytes=16 * MIB),
        cost_estimate=pl.CostEstimate(flops=10**6, bytes_accessed=MIB, transcendentals=0),
        name="solve_factors",
    )(place, *parts)


def solve_kernel(place, orders, coef, table, factors, state, out, cs, lhs, rhs, reduced):
    for c in range(6):
        for ds in range(32):
            piece = coef[ds * 32 : ds * 32 + 32, c * 128 : c * 128 + 128]
            cs[c, ds * 33 : ds * 33 + 32, :] = piece.astype(f32)
    l_row = lax.broadcasted_iota(jnp.int32, (1, L), 1)
    for k in range(4):
        m = orders[place[1] * 64 + place[0] * 4 + k // 2 * 2]
        order = m if k % 2 == 0 else L - 1 - m
        half_sign = 0.5 * (1 - 2 * ((l_row + order) & 1)).astype(f32)
        for h in range(2):
            for c in range(6):
                for p in range(2):
                    row = ((h * 6 + c) * 2 + p) * 32
                    for jh in range(2):
                        start = h * 16 + jh * 8 + k * 2 + p
                        lhs[k % 2, row : row + 32, jh * 128 : jh * 128 + 128] = cs[
                            c, pl.ds(start, 32, stride=33), :
                        ].astype(bf16)
        res = jnp.dot(lhs[k % 2], table[k], preferred_element_type=f32)
        half = 0.5 * res[0:384] + half_sign * res[384:768]
        for cp in range(12):
            store(rhs, pl.ds(cp * 4 + k, 32, stride=49), half[cp * 32 : cp * 32 + 32])

    def factor(kind, f, s):
        return factors[kind, pl.ds(f * 32 + s, 1), :]

    def forward(step, running):
        running = list(running)
        for t in range(8):
            block = state[4 * step + t // 2, pl.ds(t % 2 * 48, 48), :].astype(f32)
            s = 8 * step + t
            for f in range(2):
                at = pl.ds(pl.multiple_of(step * 392, 8) + t * 49 + f * 24, 24)
                value = load(rhs, at) + block[f * 24 : f * 24 + 24]
                running[f] = factor(0, f, s) * value + factor(1, f, s) * running[f]
                store(reduced, pl.ds(s * 48 + f * 24, 24), running[f])
        return tuple(running)

    zero = jnp.zeros((24, L), f32)
    lax.fori_loop(0, 4, forward, (zero, zero))

    def backward(step, carried):
        d = 15 - step
        carried = list(carried)
        pieces = [None] * 4
        for s2 in (1, 0):
            s = 2 * d + s2
            for f in range(2):
                value = load(reduced, pl.ds(s * 48 + f * 24, 24))
                carried[f] = value + factor(2, f, s) * carried[f]
                pieces[s2 * 2 + f] = carried[f]
        out[d] = jnp.concatenate(pieces, axis=0).astype(bf16)
        return tuple(carried)

    lax.fori_loop(0, 16, backward, (zero, zero))


def analysis_and_solve(place, orders, coef, table, factors, state):
    small = pl.BlockSpec(memory_space=pltpu.SMEM)
    return pl.pallas_call(
        solve_kernel,
        grid=(1,),
        in_specs=[
            small,
            small,
            pl.BlockSpec((1024, 768), lambda g: (0, 0)),
            pl.BlockSpec((4, NH, L), lambda g: (0, 0, 0)),
            pl.BlockSpec((3, 64, L), lambda g: (0, 0, 0)),
            pl.BlockSpec((16, 96, L), lambda g: (0, 0, 0)),
        ],
        out_specs=pl.BlockSpec((16, 96, L), lambda g: (0, 0, 0)),
        out_shape=jax.ShapeDtypeStruct((16, 96, L), bf16),
        scratch_shapes=[
            pltpu.VMEM((6, 32 * 33, 128), f32),
            pltpu.VMEM((2, 768, NH), bf16),
            pltpu.VMEM((4, 32 * 49, 128), f32),
            pltpu.VMEM((4, 32 * 48, 128), f32),
        ],
        compiler_params=pltpu.CompilerParams(vmem_limit_bytes=32 * MIB),
        cost_estimate=pl.CostEstimate(flops=int(0.9e9), bytes_accessed=6 * MIB, transcendentals=0),
        name="analysis_and_solve",
    )(place, orders, coef, table, factors, state)


def unpack_kernel(got, out_v, out_p):
    x = got[...].astype(f32)
    low = lax.broadcasted_iota(jnp.int32, (1, 8, 1), 1) < 4
    for f, ref in enumerate((out_v, out_p)):
        for c in range(3):
            row = (f * 3 + c) * 8
            both = x[:, row : row + 8, :].reshape(8, 2, 8, L)
            a, b = both[:, 0], both[:, 1]
            ref[c, 0, 0] = jnp.where(low, a, pltpu.roll(b, 4, 1)).reshape(64, L)
            ref[c, 0, 1] = jnp.where(low, pltpu.roll(a, 4, 1), b).reshape(64, L)


def unpack_solution(got):
    shape = jax.ShapeDtypeStruct((3, 2, 2, 64, L), f32)
    field = pl.BlockSpec((3, 1, 2, 64, L), lambda s: (0, s, 0, 0, 0))
    return pl.pallas_call(
        unpack_kernel,
        grid=(2,),
        in_specs=[pl.BlockSpec((16, 48, L), lambda s: (0, s, 0))],
        out_specs=[field, field],
        out_shape=[shape, shape],
        compiler_params=pltpu.CompilerParams(vmem_limit_bytes=24 * MIB),
        cost_estimate=pl.CostEstimate(flops=10**6, bytes_accessed=5 * MIB, transcendentals=0),
        name="unpack_solution",
    )(got)


def body(
    velocity,
    vorticity,
    magnetic,
    current,
    potential,
    order_slots,
    legendre_values,
    block_lengths,
    coupling,
    angular,
):
    order_rank = lax.axis_index("order")
    shell_rank = lax.axis_index("shell")
    place = jnp.stack([shell_rank, order_rank]).astype(jnp.int32)
    shell_ids = shell_rank * 2 + jnp.arange(2, dtype=jnp.int32)
    starts = jnp.cumsum(block_lengths) - block_lengths
    is_start = jnp.any(shell_ids[:, None] == starts[None, :], axis=1)
    kappa = jnp.where(is_start[None, :], 0.0, coupling)
    rows = (order_rank & 1) * 128 + jnp.arange(128, dtype=jnp.int32)
    colatitude = math.pi * (rows.astype(f32) + 0.5) / NLAT
    weight = (math.sqrt(2.0 * math.pi) * L * math.pi / NLAT * jnp.sin(colatitude))[None, :]

    latitude, pairs = legendre_synthesis(
        place,
        order_slots,
        velocity,
        vorticity,
        magnetic,
        current,
        jnp.transpose(legendre_values, (1, 0, 2)),
    )
    incoming = lax.all_to_all(latitude, "order", 0, 0, tiled=True)

    order_after, vel_after, pot_after, _ = lax.optimization_barrier(
        (order_slots, velocity, potential, latitude)
    )
    parts = state_to_send(place, kappa, angular, vel_after, pot_after)
    received = [parts[0]]
    for r in range(1, 16):
        swapped = (r & 3) * 4 + r // 4
        pairs_r = [
            (i * 8 + o, (i ^ (swapped if o & 1 else r)) * 8 + o) for i in range(16) for o in range(8)
        ]
        received.append(lax.ppermute(parts[r], ("shell", "order"), pairs_r))
    syn, ana, table = make_tables(place, order_after, pairs)
    incoming, table, received = lax.optimization_barrier((incoming, table, received))

    coefs = grid_stage(incoming, syn, ana, weight)
    received, _ = lax.optimization_barrier((received, coefs))
    state, factors = solve_factors(place, received)
    coefs = lax.all_to_all(
        coefs.reshape(128, 8, 768), ("shell", "order"), 0, 0, tiled=True
    ).reshape(1024, 768)
    solved = analysis_and_solve(place, order_slots, coefs, table, factors, state)
    solved = lax.all_to_all(solved, "shell", 0, 0, tiled=True)
    return tuple(unpack_solution(solved))


def solution(mesh):
    spectral = P(None, "shell", None, "order", None)
    in_specs = (
        spectral,
        spectral,
        spectral,
        spectral,
        spectral,
        P(),
        P("order", None, None),
        P(),
        P(None, "shell"),
        P(None, "shell"),
    )
    return jax.shard_map(
        body, mesh=mesh, in_specs=in_specs, out_specs=(spectral, spectral), check_vma=False
    )
```

```python
import math

import jax
import jax.numpy as jnp
import numpy as np
from jax import lax
from jax.experimental import pallas as pl
from jax.experimental.pallas import tpu as pltpu
from jax.sharding import PartitionSpec as P

L = 512
NLAT = 512
NPHI = 1024
NH = 256
f32 = jnp.float32
bf16 = jnp.bfloat16
MIB = 1 << 20


FOLD = NPHI // 2


def natural_tables():
    order = np.arange(L)[None, :]
    angles = 2.0 * np.pi * ((np.arange(FOLD + 16)[:, None] * order) % NPHI) / NPHI
    weight = np.where(order == 0, 1.0, 2.0) * (math.sqrt(2.0 * math.pi) / L)
    syn_cos = np.cos(angles) * weight
    syn_cos[FOLD + 1 :] = 0.0
    syn_sin = (-np.sin(angles) * weight)[:FOLD]
    ana_cos = np.cos(angles)[:FOLD].T / NPHI
    ana_cos[:, 0] *= 0.5
    ana_sin = -np.sin(angles)[:FOLD].T / NPHI
    last = np.repeat(np.cos(np.pi * order).T / NPHI, 128, axis=1)
    return [jnp.asarray(a.astype(jnp.bfloat16)) for a in (syn_cos, syn_sin, ana_cos, ana_sin, last)]


def partner(place, r):
    swapped = (r & 3) * 4 + r // 4
    return place[0] ^ jnp.where((place[1] & 1) == 1, swapped, r)


def load(ref, rows):
    return jnp.concatenate([ref[q, rows, :] for q in range(ref.shape[0])], axis=1)


def store(ref, rows, value):
    for q in range(ref.shape[0]):
        ref[q, rows, :] = value[:, q * 128 : q * 128 + 128]


PITCH = 33
TABLE_PITCH = 17
CHUNK = 171


def synthesis_kernel(place, orders, vel, vor, mag, cur, table, out, pairs, xs, ys, ts):
    step = pl.program_id(0)
    chunk = pl.program_id(1)

    @pl.when(chunk == 0)
    def _():
        for a, ref in enumerate((vel, vor, mag, cur)):
            for c in range(3):
                for s in range(2):
                    for p in range(2):
                        row = (s * 24 + (a * 3 + c) * 2 + p) * PITCH
                        store(xs, pl.ds(row, 32), ref[c, s, p].astype(f32))

    for q in range(3):

        @pl.when(chunk == q)
        def _():
            for d in range(CHUNK):
                store(ts, pl.ds((q * CHUNK + d) * TABLE_PITCH, 16), table[d].astype(f32))

    r = lax.broadcasted_iota(jnp.int32, (1, L), 1)
    sign_a = (1 - 2 * (r & 1)).astype(f32)

    def one_pair(i, _):
        m = orders[place[1] * 64 + step * 32 + 2 * i]
        a = load(xs, pl.ds(2 * i, 48, stride=PITCH))
        b = load(xs, pl.ds(2 * i + 1, 48, stride=PITCH))
        rows = load(ts, pl.ds(i, L, stride=TABLE_PITCH)).astype(bf16)
        a = pltpu.roll(a, (L - m) & (L - 1), 1)
        b_last = b[:, L - 1 : L]
        b = pltpu.roll(b, 1, 1)
        is_a = r < L - m
        sign_b = (1 - 2 * ((r + m) & 1)).astype(f32)
        a = jnp.where(is_a, a, 0.0)
        b = jnp.where(is_a, 0.0, b)
        lhs = jnp.concatenate([a, a * sign_a, b, b * sign_b], axis=0).astype(bf16)
        res = jnp.dot(lhs, rows, preferred_element_type=f32)
        last = b_last * load(ts, pl.ds(L * TABLE_PITCH + i, 1))
        last_sign = (1 - 2 * (m & 1)).astype(f32)
        b_n = res[96:144] + last
        b_s = res[144:192] + last * last_sign
        for k, parts in ((2 * i, (res[0:48], res[48:96])), (2 * i + 1, (b_n, b_s))):
            for h in range(2):
                for s in range(2):
                    at = pl.ds((s * 2 + h) * 24 * PITCH + k, 24, stride=PITCH)
                    store(ys, at, parts[h][s * 24 : s * 24 + 24])
        return 0

    @pl.when(chunk == 2)
    def _():
        lax.fori_loop(0, 16, one_pair, 0, unroll=8)
        for sh in range(4):
            for jh in range(2):
                for cp in range(24):
                    row = (sh * 24 + cp) * PITCH
                    out[sh * 2 + jh, cp] = ys[jh, row : row + 32, :].astype(bf16)

    @pl.when((chunk == 2) & (step == place[0] // 8))
    def _():
        for i in range(2):
            at = (place[0] & 7) * 2 + i
            pairs[i, 0:L, :] = load(ts, pl.ds(at, L, stride=TABLE_PITCH)).astype(bf16)
            last = load(ts, pl.ds(L * TABLE_PITCH + at, 1))
            pairs[i, L : L + 16, :] = jnp.broadcast_to(last, (16, NH)).astype(bf16)


def legendre_synthesis(place, orders, velocity, vorticity, magnetic, current, table):
    field = pl.BlockSpec((3, 2, 2, 32, L), lambda g, q, place, low: (0, 0, 0, g, 0))
    return pl.pallas_call(
        synthesis_kernel,
        grid_spec=pltpu.PrefetchScalarGridSpec(
            num_scalar_prefetch=2,
            grid=(2, 3),
            in_specs=[field] * 4
            + [pl.BlockSpec((CHUNK, 16, NH), lambda g, q, place, low: (q, g, 0))],
            out_specs=[
                pl.BlockSpec((8, 24, 32, 128), lambda g, q, place, low: (0, 0, g, 0)),
                pl.BlockSpec((2, L + 16, NH), lambda g, q, place, low: (0, 0, 0)),
            ],
            scratch_shapes=[
                pltpu.VMEM((4, 48 * PITCH, 128), f32),
                pltpu.VMEM((2, 96 * PITCH, 128), f32),
                pltpu.VMEM((2, (L + 1) * TABLE_PITCH + 7, 128), f32),
            ],
        ),
        out_shape=[
            jax.ShapeDtypeStruct((8, 24, 64, 128), bf16),
            jax.ShapeDtypeStruct((2, L + 16, NH), bf16),
        ],
        compiler_params=pltpu.CompilerParams(vmem_limit_bytes=60 * MIB),
        cost_estimate=pl.CostEstimate(flops=int(1.6e9), bytes_accessed=15 * MIB, transcendentals=0),
        name="legendre_synthesis",
    )(place, orders, velocity, vorticity, magnetic, current, table)


def state_kernel(place, kappa, angular, vel, pot, *refs):
    outs, scr = refs[:16], refs[16]
    for f, ref in enumerate((vel, pot)):
        for c in range(3):
            for s in range(2):
                for p in range(2):
                    x = ref[c, s, p].astype(f32)
                    row = s * 48 + ((f * 3 + c) * 2 + p) * 4
                    for d in range(16):
                        scr[d, row : row + 4, :] = x[4 * d : 4 * d + 4]
    lane = lax.broadcasted_iota(jnp.int32, (1, L), 1)
    lines = []
    for ref in (kappa, angular):
        for f in range(2):
            for s in range(2):
                value = jnp.full((1, L), ref[f, s], f32)
                high = value.astype(bf16).astype(f32)
                rest = value - high
                mid = rest.astype(bf16).astype(f32)
                low = rest - mid
                lines.append(jnp.where(lane < 128, high, jnp.where(lane < 256, mid, low)))
    extra = jnp.concatenate(lines + [jnp.zeros((8, L), f32)], axis=0).astype(bf16)
    for r in range(16):
        outs[r][0:96, :] = scr[partner(place, r)].astype(bf16)
        outs[r][96:112, :] = extra


def state_to_send(place, kappa, angular, velocity, potential):
    field = pl.BlockSpec((3, 2, 2, 64, L), lambda g: (0, 0, 0, 0, 0))
    small = pl.BlockSpec(memory_space=pltpu.SMEM)
    return pl.pallas_call(
        state_kernel,
        grid=(1,),
        in_specs=[small, small, small, field, field],
        out_specs=[pl.BlockSpec((112, L), lambda g: (0, 0))] * 16,
        out_shape=[jax.ShapeDtypeStruct((112, L), bf16)] * 16,
        scratch_shapes=[pltpu.VMEM((16, 96, L), f32)],
        compiler_params=pltpu.CompilerParams(vmem_limit_bytes=32 * MIB),
        cost_estimate=pl.CostEstimate(flops=10**6, bytes_accessed=4 * MIB, transcendentals=0),
        name="state_to_send",
    )(place, kappa, angular, velocity, potential)


def products(x):
    u, w, b, j = x[0:3], x[3:6], x[6:9], x[9:12]

    def cross(p, q):
        return [
            p[1] * q[2] - p[2] * q[1],
            p[2] * q[0] - p[0] * q[2],
            p[0] * q[1] - p[1] * q[0],
        ]

    uw, jb, ub = cross(u, w), cross(j, b), cross(u, b)
    return [uw[0] + jb[0] + 2.0 * u[1], uw[1] + jb[1] - 2.0 * u[0], uw[2] + jb[2]] + ub


def grid_kernel(lat, syn_cos, syn_sin, ana_cos, ana_sin, ana_last, weight, out, wide, even, odd, middle):
    step = pl.program_id(0)

    @pl.when(step == 0)
    def _():
        for c in range(12):
            for p in range(2):
                rows_p = lat[:, 2 * c + p].reshape(512, 128)
                wide[p * 512 : p * 512 + 512, c * 128 : c * 128 + 128] = rows_p
        g = jnp.dot(syn_cos[...], wide[0:512, :], preferred_element_type=f32)
        d = jnp.dot(syn_sin[...], wide[512:1024, :], preferred_element_type=f32)
        cols = [slice(c * 128, c * 128 + 128) for c in range(12)]
        here = products([g[0:FOLD, at] + d[:, at] for at in cols])
        mirror = products([g[0:FOLD, at] - d[:, at] for at in cols])
        edge = products([g[FOLD : FOLD + 8, at] for at in cols])
        for c in range(6):
            even[:, cols[c]] = (here[c] + mirror[c]).astype(bf16)
            odd[:, cols[c]] = (here[c] - mirror[c]).astype(bf16)
            middle[:, cols[c]] = edge[c]

    @pl.when(step > 0)
    def _():
        real = jnp.dot(ana_cos[...], even[...], preferred_element_type=f32)
        imag = jnp.dot(ana_sin[...], odd[...], preferred_element_type=f32)
        sign = ana_last[...]
        low = lax.broadcasted_iota(jnp.int32, (1, 8, 1), 1) < 4
        for c in range(6):
            at = slice(c * 128, c * 128 + 128)
            a = (real[:, at] + sign * middle[0:1, at]) * weight[...]
            b = imag[:, at] * weight[...]
            a, b = a.reshape(32, 8, 128), b.reshape(32, 8, 128)
            first = jnp.where(low, a, pltpu.roll(b, 4, 1))
            second = jnp.where(low, pltpu.roll(a, 4, 1), b)
            both = jnp.stack([first, second], axis=1).reshape(512, 128)
            out[:, at] = both.astype(bf16)


def grid_stage(lat, tables, weight):
    rows = 256
    by_slots = pl.BlockSpec((rows, FOLD), lambda i: (jnp.maximum(i - 1, 0), 0))
    return pl.pallas_call(
        grid_kernel,
        grid=(3,),
        in_specs=[
            pl.BlockSpec((8, 24, 64, 128), lambda i: (0, 0, 0, 0)),
            pl.BlockSpec((FOLD + 16, L), lambda i: (0, 0)),
            pl.BlockSpec((FOLD, L), lambda i: (0, 0)),
            by_slots,
            by_slots,
            pl.BlockSpec((rows, 128), lambda i: (jnp.maximum(i - 1, 0), 0)),
            pl.BlockSpec((1, 128), lambda i: (0, 0)),
        ],
        out_specs=pl.BlockSpec((2 * rows, 768), lambda i: (jnp.maximum(i - 1, 0), 0)),
        out_shape=jax.ShapeDtypeStruct((1024, 768), bf16),
        scratch_shapes=[
            pltpu.VMEM((1024, 1536), bf16),
            pltpu.VMEM((FOLD, 768), bf16),
            pltpu.VMEM((FOLD, 768), bf16),
            pltpu.VMEM((8, 768), f32),
        ],
        compiler_params=pltpu.CompilerParams(vmem_limit_bytes=60 * MIB),
        cost_estimate=pl.CostEstimate(flops=int(2.4e9), bytes_accessed=7 * MIB, transcendentals=0),
        name="grid_stage",
    )(lat, *tables, weight)


def tables_kernel(slots, targets, *refs):
    natural, made = refs[:5], refs[5:]
    ids = lax.broadcasted_iota(jnp.int32, (L, L), 0)
    pick = jnp.where(ids == slots[...], 1.0, 0.0).astype(bf16)
    for at in range(2):
        made[at][...] = jnp.dot(natural[at][...], pick, preferred_element_type=f32).astype(bf16)
    pick = jnp.where(ids == targets[...], 1.0, 0.0).astype(bf16)
    for at in range(2, 5):
        made[at][...] = lax.dot_general(
            pick, natural[at][...], (((0,), (0,)), ((), ())), preferred_element_type=f32
        ).astype(made[at].dtype)


def make_tables(order_slots):
    natural = natural_tables()
    targets = order_slots.reshape(8, 16, 4).transpose(1, 0, 2).reshape(1, L)
    whole = lambda shape: pl.BlockSpec(shape, lambda g: (0, 0))
    made = [jax.ShapeDtypeStruct(a.shape, bf16) for a in natural[:4]]
    made.append(jax.ShapeDtypeStruct((L, 128), f32))
    return pl.pallas_call(
        tables_kernel,
        grid=(1,),
        in_specs=[whole((1, L)), whole((1, L))] + [whole(a.shape) for a in natural],
        out_specs=[whole(a.shape) for a in made],
        out_shape=made,
        compiler_params=pltpu.CompilerParams(vmem_limit_bytes=60 * MIB),
        cost_estimate=pl.CostEstimate(flops=int(1e9), bytes_accessed=5 * MIB, transcendentals=0),
        name="make_tables",
    )(order_slots.reshape(1, L), targets, *natural)


def factors_kernel(place, orders, pairs, *refs):
    parts, (state, factors, table_out, extra, scr) = refs[:16], refs[16:]
    for r in range(16):
        state[partner(place, r)] = parts[r][0:96, :]
        extra[partner(place, r)] = parts[r][96:112, :].astype(f32)
    l_row = lax.broadcasted_iota(jnp.int32, (1, L), 1)
    for i in range(2):
        m = orders[place[1] * 64 + place[0] * 4 + 2 * i]
        scr[...] = pairs[i].astype(f32)
        a = jnp.transpose(scr[0:L, :])
        a = pltpu.roll(a, m, 1)
        table_out[2 * i] = jnp.where(l_row >= m, a, 0.0).astype(bf16)
        b = jnp.transpose(scr[1 : L + 1, :])
        table_out[2 * i + 1] = jnp.where(l_row >= L - 1 - m, b, 0.0).astype(bf16)
    degree = l_row.astype(f32)
    degree_term = degree * (degree + 1.0)
    below, angle = [[], []], [[], []]
    for d in range(16):
        x = extra[d]
        value = (x[0:8, 0:128] + x[0:8, 128:256]) + x[0:8, 256:384]
        value = jnp.concatenate([value] * 4, axis=1)
        for f in range(2):
            for s in range(2):
                below[f].append(value[f * 2 + s : f * 2 + s + 1])
                angle[f].append(value[4 + f * 2 + s : 4 + f * 2 + s + 1])
    for f in range(2):
        carried = jnp.zeros((1, L), f32)
        for s in range(32):
            under = below[f][s]
            above = below[f][s + 1] if s < 31 else jnp.zeros((1, L), f32)
            diagonal = 1.0 + under + above + angle[f][s] * degree_term
            inverse = 1.0 / (diagonal - under * carried)
            carried = above * inverse
            row = f * 32 + s
            factors[0, row : row + 1, :] = inverse
            factors[1, row : row + 1, :] = under * inverse
            factors[2, row : row + 1, :] = carried


def solve_factors(place, orders, pairs, parts):
    return pl.pallas_call(
        factors_kernel,
        grid=(1,),
        in_specs=[
            pl.BlockSpec(memory_space=pltpu.SMEM),
            pl.BlockSpec(memory_space=pltpu.SMEM),
            pl.BlockSpec((2, L + 16, NH), lambda g: (0, 0, 0)),
        ]
        + [pl.BlockSpec((112, L), lambda g: (0, 0))] * 16,
        out_specs=[
            pl.BlockSpec((16, 96, L), lambda g: (0, 0, 0)),
            pl.BlockSpec((3, 64, L), lambda g: (0, 0, 0)),
            pl.BlockSpec((4, NH, L), lambda g: (0, 0, 0)),
        ],
        out_shape=[
            jax.ShapeDtypeStruct((16, 96, L), bf16),
            jax.ShapeDtypeStruct((3, 64, L), f32),
            jax.ShapeDtypeStruct((4, NH, L), bf16),
        ],
        scratch_shapes=[pltpu.VMEM((16, 16, L), f32), pltpu.VMEM((L + 16, NH), f32)],
        compiler_params=pltpu.CompilerParams(vmem_limit_bytes=16 * MIB),
        cost_estimate=pl.CostEstimate(flops=10**6, bytes_accessed=MIB, transcendentals=0),
        name="solve_factors",
    )(place, orders, pairs, *parts)


def solve_kernel(place, orders, coef, table, factors, state, out, cs, lhs, rhs, reduced):
    for c in range(6):
        for ds in range(32):
            piece = coef[ds * 32 : ds * 32 + 32, c * 128 : c * 128 + 128]
            cs[c, ds * 33 : ds * 33 + 32, :] = piece.astype(f32)
    l_row = lax.broadcasted_iota(jnp.int32, (1, L), 1)
    for k in range(4):
        m = orders[place[1] * 64 + place[0] * 4 + k // 2 * 2]
        order = m if k % 2 == 0 else L - 1 - m
        half_sign = 0.5 * (1 - 2 * ((l_row + order) & 1)).astype(f32)
        for h in range(2):
            for c in range(6):
                for p in range(2):
                    row = ((h * 6 + c) * 2 + p) * 32
                    for jh in range(2):
                        start = h * 16 + jh * 8 + p * 4 + k
                        lhs[k % 2, row : row + 32, jh * 128 : jh * 128 + 128] = cs[
                            c, pl.ds(start, 32, stride=33), :
                        ].astype(bf16)
        res = jnp.dot(lhs[k % 2], table[k], preferred_element_type=f32)
        half = 0.5 * res[0:384] + half_sign * res[384:768]
        for cp in range(12):
            store(rhs, pl.ds(cp * 4 + k, 32, stride=49), half[cp * 32 : cp * 32 + 32])

    def factor(kind, f, s):
        return factors[kind, pl.ds(f * 32 + s, 1), :]

    def forward(step, running):
        running = list(running)
        for t in range(8):
            block = state[4 * step + t // 2, pl.ds(t % 2 * 48, 48), :].astype(f32)
            s = 8 * step + t
            for f in range(2):
                at = pl.ds(pl.multiple_of(step * 392, 8) + t * 49 + f * 24, 24)
                value = load(rhs, at) + block[f * 24 : f * 24 + 24]
                running[f] = factor(0, f, s) * value + factor(1, f, s) * running[f]
                store(reduced, pl.ds(s * 48 + f * 24, 24), running[f])
        return tuple(running)

    zero = jnp.zeros((24, L), f32)
    lax.fori_loop(0, 4, forward, (zero, zero))

    def backward(step, carried):
        d = 15 - step
        carried = list(carried)
        pieces = [None] * 4
        for s2 in (1, 0):
            s = 2 * d + s2
            for f in range(2):
                value = load(reduced, pl.ds(s * 48 + f * 24, 24))
                carried[f] = value + factor(2, f, s) * carried[f]
                pieces[s2 * 2 + f] = carried[f]
        out[d] = jnp.concatenate(pieces, axis=0).astype(bf16)
        return tuple(carried)

    lax.fori_loop(0, 16, backward, (zero, zero))


def analysis_and_solve(place, orders, coef, table, factors, state):
    small = pl.BlockSpec(memory_space=pltpu.SMEM)
    return pl.pallas_call(
        solve_kernel,
        grid=(1,),
        in_specs=[
            small,
            small,
            pl.BlockSpec((1024, 768), lambda g: (0, 0)),
            pl.BlockSpec((4, NH, L), lambda g: (0, 0, 0)),
            pl.BlockSpec((3, 64, L), lambda g: (0, 0, 0)),
            pl.BlockSpec((16, 96, L), lambda g: (0, 0, 0)),
        ],
        out_specs=pl.BlockSpec((16, 96, L), lambda g: (0, 0, 0)),
        out_shape=jax.ShapeDtypeStruct((16, 96, L), bf16),
        scratch_shapes=[
            pltpu.VMEM((6, 32 * 33, 128), f32),
            pltpu.VMEM((2, 768, NH), bf16),
            pltpu.VMEM((4, 32 * 49, 128), f32),
            pltpu.VMEM((4, 32 * 48, 128), f32),
        ],
        compiler_params=pltpu.CompilerParams(vmem_limit_bytes=32 * MIB),
        cost_estimate=pl.CostEstimate(flops=int(0.9e9), bytes_accessed=6 * MIB, transcendentals=0),
        name="analysis_and_solve",
    )(place, orders, coef, table, factors, state)


def unpack_kernel(got, out_v, out_p):
    x = got[...].astype(f32)
    low = lax.broadcasted_iota(jnp.int32, (1, 8, 1), 1) < 4
    for f, ref in enumerate((out_v, out_p)):
        for c in range(3):
            row = (f * 3 + c) * 8
            both = x[:, row : row + 8, :].reshape(8, 2, 8, L)
            a, b = both[:, 0], both[:, 1]
            ref[c, 0, 0] = jnp.where(low, a, pltpu.roll(b, 4, 1)).reshape(64, L)
            ref[c, 0, 1] = jnp.where(low, pltpu.roll(a, 4, 1), b).reshape(64, L)


def unpack_solution(got):
    shape = jax.ShapeDtypeStruct((3, 2, 2, 64, L), f32)
    field = pl.BlockSpec((3, 1, 2, 64, L), lambda s: (0, s, 0, 0, 0))
    return pl.pallas_call(
        unpack_kernel,
        grid=(2,),
        in_specs=[pl.BlockSpec((16, 48, L), lambda s: (0, s, 0))],
        out_specs=[field, field],
        out_shape=[shape, shape],
        compiler_params=pltpu.CompilerParams(vmem_limit_bytes=24 * MIB),
        cost_estimate=pl.CostEstimate(flops=10**6, bytes_accessed=5 * MIB, transcendentals=0),
        name="unpack_solution",
    )(got)


def body(
    velocity,
    vorticity,
    magnetic,
    current,
    potential,
    order_slots,
    legendre_values,
    block_lengths,
    coupling,
    angular,
):
    order_rank = lax.axis_index("order")
    shell_rank = lax.axis_index("shell")
    place = jnp.stack([shell_rank, order_rank]).astype(jnp.int32)
    shell_ids = shell_rank * 2 + jnp.arange(2, dtype=jnp.int32)
    starts = jnp.cumsum(block_lengths) - block_lengths
    is_start = jnp.any(shell_ids[:, None] == starts[None, :], axis=1)
    kappa = jnp.where(is_start[None, :], 0.0, coupling)
    rows = (order_rank & 1) * 128 + jnp.arange(128, dtype=jnp.int32)
    colatitude = math.pi * (rows.astype(f32) + 0.5) / NLAT
    weight = (math.sqrt(2.0 * math.pi) * L * math.pi / NLAT * jnp.sin(colatitude))[None, :]

    latitude, pairs = legendre_synthesis(
        place,
        order_slots,
        velocity,
        vorticity,
        magnetic,
        current,
        jnp.transpose(legendre_values, (1, 0, 2)),
    )
    incoming = lax.all_to_all(latitude, "order", 0, 0, tiled=True)

    order_after, vel_after, pot_after, _ = lax.optimization_barrier(
        (order_slots, velocity, potential, latitude)
    )
    parts = state_to_send(place, kappa, angular, vel_after, pot_after)
    received = [parts[0]]
    for r in range(1, 16):
        swapped = (r & 3) * 4 + r // 4
        pairs_r = [
            (i * 8 + o, (i ^ (swapped if o & 1 else r)) * 8 + o) for i in range(16) for o in range(8)
        ]
        received.append(lax.ppermute(parts[r], ("shell", "order"), pairs_r))
    tables = make_tables(order_after)
    incoming, received = lax.optimization_barrier((incoming, received))

    coefs = grid_stage(incoming, tables, weight)
    received, _ = lax.optimization_barrier((received, coefs))
    state, factors, table = solve_factors(place, order_slots, pairs, received)
    coefs = lax.all_to_all(
        coefs.reshape(128, 8, 768), ("shell", "order"), 0, 0, tiled=True
    ).reshape(1024, 768)
    solved = analysis_and_solve(place, order_slots, coefs, table, factors, state)
    solved = lax.all_to_all(solved, "shell", 0, 0, tiled=True)
    return tuple(unpack_solution(solved))


def solution(mesh):
    spectral = P(None, "shell", None, "order", None)
    in_specs = (
        spectral,
        spectral,
        spectral,
        spectral,
        spectral,
        P(),
        P("order", None, None),
        P(),
        P(None, "shell"),
        P(None, "shell"),
    )
    return jax.shard_map(
        body, mesh=mesh, in_specs=in_specs, out_specs=(spectral, spectral), check_vma=False
    )
```

```python
import math

import jax
import jax.numpy as jnp
import numpy as np
from jax import lax
from jax.experimental import pallas as pl
from jax.experimental.pallas import tpu as pltpu
from jax.sharding import PartitionSpec as P

L = 512
NLAT = 512
NPHI = 1024
NH = 256
f32 = jnp.float32
bf16 = jnp.bfloat16
MIB = 1 << 20


FOLD = NPHI // 2


def natural_tables():
    order = np.arange(L)[None, :]
    angles = 2.0 * np.pi * ((np.arange(FOLD + 16)[:, None] * order) % NPHI) / NPHI
    weight = np.where(order == 0, 1.0, 2.0) * (math.sqrt(2.0 * math.pi) / L)
    syn_cos = np.cos(angles) * weight
    syn_cos[FOLD + 1 :] = 0.0
    syn_sin = (-np.sin(angles) * weight)[:FOLD]
    ana_cos = np.cos(angles)[:FOLD].T / NPHI
    ana_cos[:, 0] *= 0.5
    ana_sin = -np.sin(angles)[:FOLD].T / NPHI
    last = np.repeat(np.cos(np.pi * order).T / NPHI, 128, axis=1)
    return [jnp.asarray(a.astype(jnp.bfloat16)) for a in (syn_cos, syn_sin, ana_cos, ana_sin, last)]


def partner(place, r):
    swapped = (r & 3) * 4 + r // 4
    return place[0] ^ jnp.where((place[1] & 1) == 1, swapped, r)


def load(ref, rows):
    return jnp.concatenate([ref[q, rows, :] for q in range(ref.shape[0])], axis=1)


def store(ref, rows, value):
    for q in range(ref.shape[0]):
        ref[q, rows, :] = value[:, q * 128 : q * 128 + 128]


PITCH = 33
TABLE_PITCH = 17
CHUNK = 171


def synthesis_kernel(place, orders, vel, vor, mag, cur, table, out, pairs, xs, ys, ts, packed, sems):
    step = pl.program_id(0)

    def arrival(g, q):
        source = table.at[pl.ds(q * CHUNK, CHUNK), pl.ds(g * 16, 16)]
        return pltpu.make_async_copy(source, packed.at[g, q], sems.at[g, q])

    @pl.when(step == 0)
    def _():
        for g in range(2):
            for q in range(3):
                arrival(g, q).start()

    for a, ref in enumerate((vel, vor, mag, cur)):
        for c in range(3):
            for s in range(2):
                for p in range(2):
                    row = (s * 24 + (a * 3 + c) * 2 + p) * PITCH
                    store(xs, pl.ds(row, 32), ref[c, s, p].astype(f32))

    for g in range(2):

        @pl.when(step == g)
        def _():
            for q in range(3):
                arrival(g, q).wait()
                for d in range(CHUNK):
                    at = pl.ds((q * CHUNK + d) * TABLE_PITCH, 16)
                    store(ts, at, packed[g, q, d].astype(f32))

    r = lax.broadcasted_iota(jnp.int32, (1, L), 1)
    sign_a = (1 - 2 * (r & 1)).astype(f32)

    def one_pair(i, _):
        m = orders[place[1] * 64 + step * 32 + 2 * i]
        a = load(xs, pl.ds(2 * i, 48, stride=PITCH))
        b = load(xs, pl.ds(2 * i + 1, 48, stride=PITCH))
        rows = load(ts, pl.ds(i, L, stride=TABLE_PITCH)).astype(bf16)
        a = pltpu.roll(a, (L - m) & (L - 1), 1)
        b_last = b[:, L - 1 : L]
        b = pltpu.roll(b, 1, 1)
        is_a = r < L - m
        sign_b = (1 - 2 * ((r + m) & 1)).astype(f32)
        a = jnp.where(is_a, a, 0.0)
        b = jnp.where(is_a, 0.0, b)
        lhs = jnp.concatenate([a, a * sign_a, b, b * sign_b], axis=0).astype(bf16)
        res = jnp.dot(lhs, rows, preferred_element_type=f32)
        last = b_last * load(ts, pl.ds(L * TABLE_PITCH + i, 1))
        last_sign = (1 - 2 * (m & 1)).astype(f32)
        b_n = res[96:144] + last
        b_s = res[144:192] + last * last_sign
        for k, parts in ((2 * i, (res[0:48], res[48:96])), (2 * i + 1, (b_n, b_s))):
            for h in range(2):
                for s in range(2):
                    at = pl.ds((s * 2 + h) * 24 * PITCH + k, 24, stride=PITCH)
                    store(ys, at, parts[h][s * 24 : s * 24 + 24])
        return 0

    lax.fori_loop(0, 16, one_pair, 0, unroll=16)
    for sh in range(4):
        for jh in range(2):
            for cp in range(24):
                row = (sh * 24 + cp) * PITCH
                out[sh * 2 + jh, cp] = ys[jh, row : row + 32, :].astype(bf16)

    @pl.when(step == place[0] // 8)
    def _():
        for i in range(2):
            at = (place[0] & 7) * 2 + i
            pairs[i, 0:L, :] = load(ts, pl.ds(at, L, stride=TABLE_PITCH)).astype(bf16)
            last = load(ts, pl.ds(L * TABLE_PITCH + at, 1))
            pairs[i, L : L + 16, :] = jnp.broadcast_to(last, (16, NH)).astype(bf16)


def legendre_synthesis(place, orders, velocity, vorticity, magnetic, current, table):
    field = pl.BlockSpec((3, 2, 2, 32, L), lambda g, place, low: (0, 0, 0, g, 0))
    return pl.pallas_call(
        synthesis_kernel,
        grid_spec=pltpu.PrefetchScalarGridSpec(
            num_scalar_prefetch=2,
            grid=(2,),
            in_specs=[field] * 4 + [pl.BlockSpec(memory_space=pl.ANY)],
            out_specs=[
                pl.BlockSpec((8, 24, 32, 128), lambda g, place, low: (0, 0, g, 0)),
                pl.BlockSpec((2, L + 16, NH), lambda g, place, low: (0, 0, 0)),
            ],
            scratch_shapes=[
                pltpu.VMEM((4, 48 * PITCH, 128), f32),
                pltpu.VMEM((2, 96 * PITCH, 128), f32),
                pltpu.VMEM((2, (L + 1) * TABLE_PITCH + 7, 128), f32),
                pltpu.VMEM((2, 3, CHUNK, 16, NH), bf16),
                pltpu.SemaphoreType.DMA((2, 3)),
            ],
        ),
        out_shape=[
            jax.ShapeDtypeStruct((8, 24, 64, 128), bf16),
            jax.ShapeDtypeStruct((2, L + 16, NH), bf16),
        ],
        compiler_params=pltpu.CompilerParams(vmem_limit_bytes=60 * MIB),
        cost_estimate=pl.CostEstimate(flops=int(1.6e9), bytes_accessed=15 * MIB, transcendentals=0),
        name="legendre_synthesis",
    )(place, orders, velocity, vorticity, magnetic, current, table)


def state_kernel(place, kappa, angular, vel, pot, *refs):
    outs, scr = refs[:16], refs[16]
    for f, ref in enumerate((vel, pot)):
        for c in range(3):
            for s in range(2):
                for p in range(2):
                    x = ref[c, s, p].astype(f32)
                    row = s * 48 + ((f * 3 + c) * 2 + p) * 4
                    for d in range(16):
                        scr[d, row : row + 4, :] = x[4 * d : 4 * d + 4]
    lane = lax.broadcasted_iota(jnp.int32, (1, L), 1)
    lines = []
    for ref in (kappa, angular):
        for f in range(2):
            for s in range(2):
                value = jnp.full((1, L), ref[f, s], f32)
                high = value.astype(bf16).astype(f32)
                rest = value - high
                mid = rest.astype(bf16).astype(f32)
                low = rest - mid
                lines.append(jnp.where(lane < 128, high, jnp.where(lane < 256, mid, low)))
    extra = jnp.concatenate(lines + [jnp.zeros((8, L), f32)], axis=0).astype(bf16)
    for r in range(16):
        outs[r][0:96, :] = scr[partner(place, r)].astype(bf16)
        outs[r][96:112, :] = extra


def state_to_send(place, kappa, angular, velocity, potential):
    field = pl.BlockSpec((3, 2, 2, 64, L), lambda g: (0, 0, 0, 0, 0))
    small = pl.BlockSpec(memory_space=pltpu.SMEM)
    return pl.pallas_call(
        state_kernel,
        grid=(1,),
        in_specs=[small, small, small, field, field],
        out_specs=[pl.BlockSpec((112, L), lambda g: (0, 0))] * 16,
        out_shape=[jax.ShapeDtypeStruct((112, L), bf16)] * 16,
        scratch_shapes=[pltpu.VMEM((16, 96, L), f32)],
        compiler_params=pltpu.CompilerParams(vmem_limit_bytes=60 * MIB),
        cost_estimate=pl.CostEstimate(flops=10**6, bytes_accessed=4 * MIB, transcendentals=0),
        name="state_to_send",
    )(place, kappa, angular, velocity, potential)


def products(x):
    u, w, b, j = x[0:3], x[3:6], x[6:9], x[9:12]

    def cross(p, q):
        return [
            p[1] * q[2] - p[2] * q[1],
            p[2] * q[0] - p[0] * q[2],
            p[0] * q[1] - p[1] * q[0],
        ]

    uw, jb, ub = cross(u, w), cross(j, b), cross(u, b)
    return [uw[0] + jb[0] + 2.0 * u[1], uw[1] + jb[1] - 2.0 * u[0], uw[2] + jb[2]] + ub


def grid_kernel(lat, syn_cos, syn_sin, ana_cos, ana_sin, ana_last, weight, out, wide, even, odd, middle):
    step = pl.program_id(0)

    @pl.when(step == 0)
    def _():
        for c in range(12):
            for p in range(2):
                rows_p = lat[:, 2 * c + p].reshape(512, 128)
                wide[p * 512 : p * 512 + 512, c * 128 : c * 128 + 128] = rows_p
        g = jnp.dot(syn_cos[...], wide[0:512, :], preferred_element_type=f32)
        d = jnp.dot(syn_sin[...], wide[512:1024, :], preferred_element_type=f32)
        cols = [slice(c * 128, c * 128 + 128) for c in range(12)]
        here = products([g[0:FOLD, at] + d[:, at] for at in cols])
        mirror = products([g[0:FOLD, at] - d[:, at] for at in cols])
        edge = products([g[FOLD : FOLD + 8, at] for at in cols])
        for c in range(6):
            even[:, cols[c]] = (here[c] + mirror[c]).astype(bf16)
            odd[:, cols[c]] = (here[c] - mirror[c]).astype(bf16)
            middle[:, cols[c]] = edge[c]

    @pl.when(step > 0)
    def _():
        real = jnp.dot(ana_cos[...], even[...], preferred_element_type=f32)
        imag = jnp.dot(ana_sin[...], odd[...], preferred_element_type=f32)
        sign = ana_last[...]
        low = lax.broadcasted_iota(jnp.int32, (1, 8, 1), 1) < 4
        for c in range(6):
            at = slice(c * 128, c * 128 + 128)
            a = (real[:, at] + sign * middle[0:1, at]) * weight[...]
            b = imag[:, at] * weight[...]
            a, b = a.reshape(32, 8, 128), b.reshape(32, 8, 128)
            first = jnp.where(low, a, pltpu.roll(b, 4, 1))
            second = jnp.where(low, pltpu.roll(a, 4, 1), b)
            both = jnp.stack([first, second], axis=1).reshape(512, 128)
            out[:, at] = both.astype(bf16)


def grid_stage(lat, tables, weight):
    rows = 256
    by_slots = pl.BlockSpec((rows, FOLD), lambda i: (jnp.maximum(i - 1, 0), 0))
    return pl.pallas_call(
        grid_kernel,
        grid=(3,),
        in_specs=[
            pl.BlockSpec((8, 24, 64, 128), lambda i: (0, 0, 0, 0)),
            pl.BlockSpec((FOLD + 16, L), lambda i: (0, 0)),
            pl.BlockSpec((FOLD, L), lambda i: (0, 0)),
            by_slots,
            by_slots,
            pl.BlockSpec((rows, 128), lambda i: (jnp.maximum(i - 1, 0), 0)),
            pl.BlockSpec((1, 128), lambda i: (0, 0)),
        ],
        out_specs=pl.BlockSpec((2 * rows, 768), lambda i: (jnp.maximum(i - 1, 0), 0)),
        out_shape=jax.ShapeDtypeStruct((1024, 768), bf16),
        scratch_shapes=[
            pltpu.VMEM((1024, 1536), bf16),
            pltpu.VMEM((FOLD, 768), bf16),
            pltpu.VMEM((FOLD, 768), bf16),
            pltpu.VMEM((8, 768), f32),
        ],
        compiler_params=pltpu.CompilerParams(vmem_limit_bytes=60 * MIB),
        cost_estimate=pl.CostEstimate(flops=int(2.4e9), bytes_accessed=7 * MIB, transcendentals=0),
        name="grid_stage",
    )(lat, *tables, weight)


def tables_kernel(slots, targets, *refs):
    natural, made = refs[:5], refs[5:]
    ids = lax.broadcasted_iota(jnp.int32, (L, L), 0)
    pick = jnp.where(ids == slots[...], 1.0, 0.0).astype(bf16)
    for at in range(2):
        made[at][...] = jnp.dot(natural[at][...], pick, preferred_element_type=f32).astype(bf16)
    pick = jnp.where(ids == targets[...], 1.0, 0.0).astype(bf16)
    for at in range(2, 5):
        made[at][...] = lax.dot_general(
            pick, natural[at][...], (((0,), (0,)), ((), ())), preferred_element_type=f32
        ).astype(made[at].dtype)


def make_tables(order_slots):
    natural = natural_tables()
    targets = order_slots.reshape(8, 16, 4).transpose(1, 0, 2).reshape(1, L)
    whole = lambda shape: pl.BlockSpec(shape, lambda g: (0, 0))
    made = [jax.ShapeDtypeStruct(a.shape, bf16) for a in natural[:4]]
    made.append(jax.ShapeDtypeStruct((L, 128), f32))
    return pl.pallas_call(
        tables_kernel,
        grid=(1,),
        in_specs=[whole((1, L)), whole((1, L))] + [whole(a.shape) for a in natural],
        out_specs=[whole(a.shape) for a in made],
        out_shape=made,
        compiler_params=pltpu.CompilerParams(vmem_limit_bytes=60 * MIB),
        cost_estimate=pl.CostEstimate(flops=int(1e9), bytes_accessed=5 * MIB, transcendentals=0),
        name="make_tables",
    )(order_slots.reshape(1, L), targets, *natural)


def factors_kernel(place, orders, pairs, *refs):
    parts, (state, factors, table_out, extra, scr) = refs[:16], refs[16:]
    for r in range(16):
        state[partner(place, r)] = parts[r][0:96, :]
        extra[partner(place, r)] = parts[r][96:112, :].astype(f32)
    l_row = lax.broadcasted_iota(jnp.int32, (1, L), 1)
    for i in range(2):
        m = orders[place[1] * 64 + place[0] * 4 + 2 * i]
        scr[...] = pairs[i].astype(f32)
        a = jnp.transpose(scr[0:L, :])
        a = pltpu.roll(a, m, 1)
        table_out[2 * i] = jnp.where(l_row >= m, a, 0.0).astype(bf16)
        b = jnp.transpose(scr[1 : L + 1, :])
        table_out[2 * i + 1] = jnp.where(l_row >= L - 1 - m, b, 0.0).astype(bf16)
    degree = l_row.astype(f32)
    degree_term = degree * (degree + 1.0)
    below, angle = [[], []], [[], []]
    for d in range(16):
        x = extra[d]
        value = (x[0:8, 0:128] + x[0:8, 128:256]) + x[0:8, 256:384]
        value = jnp.concatenate([value] * 4, axis=1)
        for f in range(2):
            for s in range(2):
                below[f].append(value[f * 2 + s : f * 2 + s + 1])
                angle[f].append(value[4 + f * 2 + s : 4 + f * 2 + s + 1])
    for f in range(2):
        carried = jnp.zeros((1, L), f32)
        for s in range(32):
            under = below[f][s]
            above = below[f][s + 1] if s < 31 else jnp.zeros((1, L), f32)
            diagonal = 1.0 + under + above + angle[f][s] * degree_term
            inverse = 1.0 / (diagonal - under * carried)
            carried = above * inverse
            row = f * 32 + s
            factors[0, row : row + 1, :] = inverse
            factors[1, row : row + 1, :] = under * inverse
            factors[2, row : row + 1, :] = carried


def solve_factors(place, orders, pairs, parts):
    return pl.pallas_call(
        factors_kernel,
        grid=(1,),
        in_specs=[
            pl.BlockSpec(memory_space=pltpu.SMEM),
            pl.BlockSpec(memory_space=pltpu.SMEM),
            pl.BlockSpec((2, L + 16, NH), lambda g: (0, 0, 0)),
        ]
        + [pl.BlockSpec((112, L), lambda g: (0, 0))] * 16,
        out_specs=[
            pl.BlockSpec((16, 96, L), lambda g: (0, 0, 0)),
            pl.BlockSpec((3, 64, L), lambda g: (0, 0, 0)),
            pl.BlockSpec((4, NH, L), lambda g: (0, 0, 0)),
        ],
        out_shape=[
            jax.ShapeDtypeStruct((16, 96, L), bf16),
            jax.ShapeDtypeStruct((3, 64, L), f32),
            jax.ShapeDtypeStruct((4, NH, L), bf16),
        ],
        scratch_shapes=[pltpu.VMEM((16, 16, L), f32), pltpu.VMEM((L + 16, NH), f32)],
        compiler_params=pltpu.CompilerParams(vmem_limit_bytes=16 * MIB),
        cost_estimate=pl.CostEstimate(flops=10**6, bytes_accessed=MIB, transcendentals=0),
        name="solve_factors",
    )(place, orders, pairs, *parts)


def solve_kernel(place, orders, coef, table, factors, state, out, cs, lhs, rhs, reduced):
    for c in range(6):
        for ds in range(32):
            piece = coef[ds * 32 : ds * 32 + 32, c * 128 : c * 128 + 128]
            cs[c, ds * 33 : ds * 33 + 32, :] = piece.astype(f32)
    l_row = lax.broadcasted_iota(jnp.int32, (1, L), 1)
    for k in range(4):
        m = orders[place[1] * 64 + place[0] * 4 + k // 2 * 2]
        order = m if k % 2 == 0 else L - 1 - m
        half_sign = 0.5 * (1 - 2 * ((l_row + order) & 1)).astype(f32)
        for h in range(2):
            for c in range(6):
                for p in range(2):
                    row = ((h * 6 + c) * 2 + p) * 32
                    for jh in range(2):
                        start = h * 16 + jh * 8 + p * 4 + k
                        lhs[k % 2, row : row + 32, jh * 128 : jh * 128 + 128] = cs[
                            c, pl.ds(start, 32, stride=33), :
                        ].astype(bf16)
        res = jnp.dot(lhs[k % 2], table[k], preferred_element_type=f32)
        half = 0.5 * res[0:384] + half_sign * res[384:768]
        for cp in range(12):
            store(rhs, pl.ds(cp * 4 + k, 32, stride=49), half[cp * 32 : cp * 32 + 32])

    def factor(kind, f, s):
        return factors[kind, pl.ds(f * 32 + s, 1), :]

    def forward(step, running):
        running = list(running)
        for t in range(8):
            block = state[4 * step + t // 2, pl.ds(t % 2 * 48, 48), :].astype(f32)
            s = 8 * step + t
            for f in range(2):
                at = pl.ds(pl.multiple_of(step * 392, 8) + t * 49 + f * 24, 24)
                value = load(rhs, at) + block[f * 24 : f * 24 + 24]
                running[f] = factor(0, f, s) * value + factor(1, f, s) * running[f]
                store(reduced, pl.ds(s * 48 + f * 24, 24), running[f])
        return tuple(running)

    zero = jnp.zeros((24, L), f32)
    lax.fori_loop(0, 4, forward, (zero, zero))

    def backward(step, carried):
        d = 15 - step
        carried = list(carried)
        pieces = [None] * 4
        for s2 in (1, 0):
            s = 2 * d + s2
            for f in range(2):
                value = load(reduced, pl.ds(s * 48 + f * 24, 24))
                carried[f] = value + factor(2, f, s) * carried[f]
                pieces[s2 * 2 + f] = carried[f]
        out[d] = jnp.concatenate(pieces, axis=0).astype(bf16)
        return tuple(carried)

    lax.fori_loop(0, 16, backward, (zero, zero))


def analysis_and_solve(place, orders, coef, table, factors, state):
    small = pl.BlockSpec(memory_space=pltpu.SMEM)
    return pl.pallas_call(
        solve_kernel,
        grid=(1,),
        in_specs=[
            small,
            small,
            pl.BlockSpec((1024, 768), lambda g: (0, 0)),
            pl.BlockSpec((4, NH, L), lambda g: (0, 0, 0)),
            pl.BlockSpec((3, 64, L), lambda g: (0, 0, 0)),
            pl.BlockSpec((16, 96, L), lambda g: (0, 0, 0)),
        ],
        out_specs=pl.BlockSpec((16, 96, L), lambda g: (0, 0, 0)),
        out_shape=jax.ShapeDtypeStruct((16, 96, L), bf16),
        scratch_shapes=[
            pltpu.VMEM((6, 32 * 33, 128), f32),
            pltpu.VMEM((2, 768, NH), bf16),
            pltpu.VMEM((4, 32 * 49, 128), f32),
            pltpu.VMEM((4, 32 * 48, 128), f32),
        ],
        compiler_params=pltpu.CompilerParams(vmem_limit_bytes=32 * MIB),
        cost_estimate=pl.CostEstimate(flops=int(0.9e9), bytes_accessed=6 * MIB, transcendentals=0),
        name="analysis_and_solve",
    )(place, orders, coef, table, factors, state)


def unpack_kernel(got, out_v, out_p):
    x = got[...].astype(f32)
    low = lax.broadcasted_iota(jnp.int32, (1, 8, 1), 1) < 4
    for f, ref in enumerate((out_v, out_p)):
        for c in range(3):
            row = (f * 3 + c) * 8
            both = x[:, row : row + 8, :].reshape(8, 2, 8, L)
            a, b = both[:, 0], both[:, 1]
            ref[c, 0, 0] = jnp.where(low, a, pltpu.roll(b, 4, 1)).reshape(64, L)
            ref[c, 0, 1] = jnp.where(low, pltpu.roll(a, 4, 1), b).reshape(64, L)


def unpack_solution(got):
    shape = jax.ShapeDtypeStruct((3, 2, 2, 64, L), f32)
    field = pl.BlockSpec((3, 1, 2, 64, L), lambda s: (0, s, 0, 0, 0))
    return pl.pallas_call(
        unpack_kernel,
        grid=(2,),
        in_specs=[pl.BlockSpec((16, 48, L), lambda s: (0, s, 0))],
        out_specs=[field, field],
        out_shape=[shape, shape],
        compiler_params=pltpu.CompilerParams(vmem_limit_bytes=24 * MIB),
        cost_estimate=pl.CostEstimate(flops=10**6, bytes_accessed=5 * MIB, transcendentals=0),
        name="unpack_solution",
    )(got)


def body(
    velocity,
    vorticity,
    magnetic,
    current,
    potential,
    order_slots,
    legendre_values,
    block_lengths,
    coupling,
    angular,
):
    order_rank = lax.axis_index("order")
    shell_rank = lax.axis_index("shell")
    place = jnp.stack([shell_rank, order_rank]).astype(jnp.int32)
    shell_ids = shell_rank * 2 + jnp.arange(2, dtype=jnp.int32)
    starts = jnp.cumsum(block_lengths) - block_lengths
    is_start = jnp.any(shell_ids[:, None] == starts[None, :], axis=1)
    kappa = jnp.where(is_start[None, :], 0.0, coupling)
    rows = (order_rank & 1) * 128 + jnp.arange(128, dtype=jnp.int32)
    colatitude = math.pi * (rows.astype(f32) + 0.5) / NLAT
    weight = (math.sqrt(2.0 * math.pi) * L * math.pi / NLAT * jnp.sin(colatitude))[None, :]

    latitude, pairs = legendre_synthesis(
        place,
        order_slots,
        velocity,
        vorticity,
        magnetic,
        current,
        jnp.transpose(legendre_values, (1, 0, 2)),
    )
    incoming = lax.all_to_all(latitude, "order", 0, 0, tiled=True)

    order_after, vel_after, pot_after, _ = lax.optimization_barrier(
        (order_slots, velocity, potential, latitude)
    )
    parts = state_to_send(place, kappa, angular, vel_after, pot_after)
    received = [parts[0]]
    for r in range(1, 16):
        swapped = (r & 3) * 4 + r // 4
        pairs_r = [
            (i * 8 + o, (i ^ (swapped if o & 1 else r)) * 8 + o) for i in range(16) for o in range(8)
        ]
        received.append(lax.ppermute(parts[r], ("shell", "order"), pairs_r))
    tables = make_tables(order_after)
    incoming, received = lax.optimization_barrier((incoming, received))

    coefs = grid_stage(incoming, tables, weight)
    received, _ = lax.optimization_barrier((received, coefs))
    state, factors, table = solve_factors(place, order_slots, pairs, received)
    coefs = lax.all_to_all(
        coefs.reshape(128, 8, 768), ("shell", "order"), 0, 0, tiled=True
    ).reshape(1024, 768)
    solved = analysis_and_solve(place, order_slots, coefs, table, factors, state)
    solved = lax.all_to_all(solved, "shell", 0, 0, tiled=True)
    return tuple(unpack_solution(solved))


def solution(mesh):
    spectral = P(None, "shell", None, "order", None)
    in_specs = (
        spectral,
        spectral,
        spectral,
        spectral,
        spectral,
        P(),
        P("order", None, None),
        P(),
        P(None, "shell"),
        P(None, "shell"),
    )
    return jax.shard_map(
        body, mesh=mesh, in_specs=in_specs, out_specs=(spectral, spectral), check_vma=False
    )
```

```python
import math

import jax
import jax.numpy as jnp
import numpy as np
from jax import lax
from jax.experimental import pallas as pl
from jax.experimental.pallas import tpu as pltpu
from jax.sharding import PartitionSpec as P

L = 512
NLAT = 512
NPHI = 1024
NH = 256
f32 = jnp.float32
bf16 = jnp.bfloat16
MIB = 1 << 20


FOLD = NPHI // 2


def natural_tables():
    order = np.arange(L)[None, :]
    angles = 2.0 * np.pi * ((np.arange(FOLD + 16)[:, None] * order) % NPHI) / NPHI
    weight = np.where(order == 0, 1.0, 2.0) * (math.sqrt(2.0 * math.pi) / L)
    syn_cos = np.cos(angles) * weight
    syn_cos[FOLD + 1 :] = 0.0
    syn_sin = (-np.sin(angles) * weight)[:FOLD]
    ana_cos = np.cos(angles)[:FOLD].T / NPHI
    ana_cos[:, 0] *= 0.5
    ana_sin = -np.sin(angles)[:FOLD].T / NPHI
    last = np.repeat(np.cos(np.pi * order).T / NPHI, 128, axis=1)
    return [jnp.asarray(a.astype(jnp.bfloat16)) for a in (syn_cos, syn_sin, ana_cos, ana_sin, last)]


def partner(place, r):
    swapped = (r & 3) * 4 + r // 4
    return place[0] ^ jnp.where((place[1] & 1) == 1, swapped, r)


def load(ref, rows):
    return jnp.concatenate([ref[q, rows, :] for q in range(ref.shape[0])], axis=1)


def store(ref, rows, value):
    for q in range(ref.shape[0]):
        ref[q, rows, :] = value[:, q * 128 : q * 128 + 128]


PITCH = 33
TABLE_PITCH = 17
CHUNK = 171


def synthesis_kernel(place, orders, vel, vor, mag, cur, table, out, pairs, xs, ys, ts, packed, sems):
    step = pl.program_id(0)

    def arrival(g, q):
        source = table.at[pl.ds(q * CHUNK, CHUNK), pl.ds(g * 16, 16)]
        return pltpu.make_async_copy(source, packed.at[g, q], sems.at[g, q])

    @pl.when(step == 0)
    def _():
        for g in range(2):
            for q in range(3):
                arrival(g, q).start()

    for a, ref in enumerate((vel, vor, mag, cur)):
        for c in range(3):
            for s in range(2):
                for p in range(2):
                    row = (s * 24 + (a * 3 + c) * 2 + p) * PITCH
                    store(xs, pl.ds(row, 32), ref[c, s, p].astype(f32))

    for g in range(2):

        @pl.when(step == g)
        def _():
            for q in range(3):
                arrival(g, q).wait()
                for d in range(CHUNK):
                    at = pl.ds((q * CHUNK + d) * TABLE_PITCH, 16)
                    store(ts, at, packed[g, q, d].astype(f32))

    r = lax.broadcasted_iota(jnp.int32, (1, L), 1)
    sign_a = (1 - 2 * (r & 1)).astype(f32)

    def one_pair(i, _):
        m = orders[place[1] * 64 + step * 32 + 2 * i]
        a = load(xs, pl.ds(2 * i, 48, stride=PITCH))
        b = load(xs, pl.ds(2 * i + 1, 48, stride=PITCH))
        rows = load(ts, pl.ds(i, L, stride=TABLE_PITCH)).astype(bf16)
        a = pltpu.roll(a, (L - m) & (L - 1), 1)
        b_last = b[:, L - 1 : L]
        b = pltpu.roll(b, 1, 1)
        is_a = r < L - m
        sign_b = (1 - 2 * ((r + m) & 1)).astype(f32)
        a = jnp.where(is_a, a, 0.0)
        b = jnp.where(is_a, 0.0, b)
        lhs = jnp.concatenate([a, a * sign_a, b, b * sign_b], axis=0).astype(bf16)
        res = jnp.dot(lhs, rows, preferred_element_type=f32)
        last = b_last * load(ts, pl.ds(L * TABLE_PITCH + i, 1))
        last_sign = (1 - 2 * (m & 1)).astype(f32)
        b_n = res[96:144] + last
        b_s = res[144:192] + last * last_sign
        for k, parts in ((2 * i, (res[0:48], res[48:96])), (2 * i + 1, (b_n, b_s))):
            for h in range(2):
                for s in range(2):
                    at = pl.ds((s * 2 + h) * 24 * PITCH + k, 24, stride=PITCH)
                    store(ys, at, parts[h][s * 24 : s * 24 + 24])
        return 0

    lax.fori_loop(0, 16, one_pair, 0, unroll=16)
    for sh in range(4):
        for jh in range(2):
            for cp in range(24):
                row = (sh * 24 + cp) * PITCH
                out[sh * 2 + jh, cp] = ys[jh, row : row + 32, :].astype(bf16)

    @pl.when(step == place[0] // 8)
    def _():
        for i in range(2):
            at = (place[0] & 7) * 2 + i
            pairs[i, 0:L, :] = load(ts, pl.ds(at, L, stride=TABLE_PITCH)).astype(bf16)
            last = load(ts, pl.ds(L * TABLE_PITCH + at, 1))
            pairs[i, L : L + 16, :] = jnp.broadcast_to(last, (16, NH)).astype(bf16)


def legendre_synthesis(place, orders, velocity, vorticity, magnetic, current, table):
    field = pl.BlockSpec((3, 2, 2, 32, L), lambda g, place, low: (0, 0, 0, g, 0))
    return pl.pallas_call(
        synthesis_kernel,
        grid_spec=pltpu.PrefetchScalarGridSpec(
            num_scalar_prefetch=2,
            grid=(2,),
            in_specs=[field] * 4 + [pl.BlockSpec(memory_space=pl.ANY)],
            out_specs=[
                pl.BlockSpec((8, 24, 32, 128), lambda g, place, low: (0, 0, g, 0)),
                pl.BlockSpec((2, L + 16, NH), lambda g, place, low: (0, 0, 0)),
            ],
            scratch_shapes=[
                pltpu.VMEM((4, 48 * PITCH, 128), f32),
                pltpu.VMEM((2, 96 * PITCH, 128), f32),
                pltpu.VMEM((2, (L + 1) * TABLE_PITCH + 7, 128), f32),
                pltpu.VMEM((2, 3, CHUNK, 16, NH), bf16),
                pltpu.SemaphoreType.DMA((2, 3)),
            ],
        ),
        out_shape=[
            jax.ShapeDtypeStruct((8, 24, 64, 128), bf16),
            jax.ShapeDtypeStruct((2, L + 16, NH), bf16),
        ],
        compiler_params=pltpu.CompilerParams(vmem_limit_bytes=60 * MIB),
        cost_estimate=pl.CostEstimate(flops=int(1.6e9), bytes_accessed=15 * MIB, transcendentals=0),
        name="legendre_synthesis",
    )(place, orders, velocity, vorticity, magnetic, current, table)


def state_kernel(place, kappa, angular, vel, pot, *refs):
    outs, scr = refs[:16], refs[16]
    for f, ref in enumerate((vel, pot)):
        for c in range(3):
            for s in range(2):
                for p in range(2):
                    x = ref[c, s, p].astype(f32)
                    row = s * 48 + ((f * 3 + c) * 2 + p) * 4
                    for d in range(16):
                        scr[d, row : row + 4, :] = x[4 * d : 4 * d + 4]
    lane = lax.broadcasted_iota(jnp.int32, (1, L), 1)
    lines = []
    for ref in (kappa, angular):
        for f in range(2):
            for s in range(2):
                value = jnp.full((1, L), ref[f, s], f32)
                high = value.astype(bf16).astype(f32)
                rest = value - high
                mid = rest.astype(bf16).astype(f32)
                low = rest - mid
                lines.append(jnp.where(lane < 128, high, jnp.where(lane < 256, mid, low)))
    extra = jnp.concatenate(lines + [jnp.zeros((8, L), f32)], axis=0).astype(bf16)
    for r in range(16):
        outs[r][0:96, :] = scr[partner(place, r)].astype(bf16)
        outs[r][96:112, :] = extra


def state_to_send(place, kappa, angular, velocity, potential):
    field = pl.BlockSpec((3, 2, 2, 64, L), lambda g: (0, 0, 0, 0, 0))
    small = pl.BlockSpec(memory_space=pltpu.SMEM)
    return pl.pallas_call(
        state_kernel,
        grid=(1,),
        in_specs=[small, small, small, field, field],
        out_specs=[pl.BlockSpec((112, L), lambda g: (0, 0))] * 16,
        out_shape=[jax.ShapeDtypeStruct((112, L), bf16)] * 16,
        scratch_shapes=[pltpu.VMEM((16, 96, L), f32)],
        compiler_params=pltpu.CompilerParams(vmem_limit_bytes=60 * MIB),
        cost_estimate=pl.CostEstimate(flops=10**6, bytes_accessed=4 * MIB, transcendentals=0),
        name="state_to_send",
    )(place, kappa, angular, velocity, potential)


def products(x):
    u, w, b, j = x[0:3], x[3:6], x[6:9], x[9:12]

    def cross(p, q):
        return [
            p[1] * q[2] - p[2] * q[1],
            p[2] * q[0] - p[0] * q[2],
            p[0] * q[1] - p[1] * q[0],
        ]

    uw, jb, ub = cross(u, w), cross(j, b), cross(u, b)
    return [uw[0] + jb[0] + 2.0 * u[1], uw[1] + jb[1] - 2.0 * u[0], uw[2] + jb[2]] + ub


def grid_kernel(lat, syn_cos, syn_sin, ana_cos, ana_sin, ana_last, weight, out, wide, even, odd, middle):
    step = pl.program_id(0)

    @pl.when(step == 0)
    def _():
        for c in range(12):
            for p in range(2):
                rows_p = lat[:, 2 * c + p].reshape(512, 128)
                wide[p * 512 : p * 512 + 512, c * 128 : c * 128 + 128] = rows_p
        g = jnp.dot(syn_cos[...], wide[0:512, :], preferred_element_type=f32)
        d = jnp.dot(syn_sin[...], wide[512:1024, :], preferred_element_type=f32)
        cols = [slice(c * 128, c * 128 + 128) for c in range(12)]
        here = products([g[0:FOLD, at] + d[:, at] for at in cols])
        mirror = products([g[0:FOLD, at] - d[:, at] for at in cols])
        edge = products([g[FOLD : FOLD + 8, at] for at in cols])
        for c in range(6):
            even[:, cols[c]] = (here[c] + mirror[c]).astype(bf16)
            odd[:, cols[c]] = (here[c] - mirror[c]).astype(bf16)
            middle[:, cols[c]] = edge[c]

    @pl.when(step > 0)
    def _():
        real = jnp.dot(ana_cos[...], even[...], preferred_element_type=f32)
        imag = jnp.dot(ana_sin[...], odd[...], preferred_element_type=f32)
        sign = ana_last[...]
        low = lax.broadcasted_iota(jnp.int32, (1, 8, 1), 1) < 4
        for c in range(6):
            at = slice(c * 128, c * 128 + 128)
            a = (real[:, at] + sign * middle[0:1, at]) * weight[...]
            b = imag[:, at] * weight[...]
            a, b = a.reshape(32, 8, 128), b.reshape(32, 8, 128)
            first = jnp.where(low, a, pltpu.roll(b, 4, 1))
            second = jnp.where(low, pltpu.roll(a, 4, 1), b)
            both = jnp.stack([first, second], axis=1).reshape(512, 128)
            out[:, at] = both.astype(bf16)


def grid_stage(lat, tables, weight):
    rows = 256
    by_slots = pl.BlockSpec((rows, FOLD), lambda i: (jnp.maximum(i - 1, 0), 0))
    return pl.pallas_call(
        grid_kernel,
        grid=(3,),
        in_specs=[
            pl.BlockSpec((8, 24, 64, 128), lambda i: (0, 0, 0, 0)),
            pl.BlockSpec((FOLD + 16, L), lambda i: (0, 0)),
            pl.BlockSpec((FOLD, L), lambda i: (0, 0)),
            by_slots,
            by_slots,
            pl.BlockSpec((rows, 128), lambda i: (jnp.maximum(i - 1, 0), 0)),
            pl.BlockSpec((1, 128), lambda i: (0, 0)),
        ],
        out_specs=pl.BlockSpec((2 * rows, 768), lambda i: (jnp.maximum(i - 1, 0), 0)),
        out_shape=jax.ShapeDtypeStruct((1024, 768), bf16),
        scratch_shapes=[
            pltpu.VMEM((1024, 1536), bf16),
            pltpu.VMEM((FOLD, 768), bf16),
            pltpu.VMEM((FOLD, 768), bf16),
            pltpu.VMEM((8, 768), f32),
        ],
        compiler_params=pltpu.CompilerParams(vmem_limit_bytes=60 * MIB),
        cost_estimate=pl.CostEstimate(flops=int(2.4e9), bytes_accessed=7 * MIB, transcendentals=0),
        name="grid_stage",
    )(lat, *tables, weight)


def tables_kernel(slots, targets, *refs):
    natural, made = refs[:5], refs[5:]
    ids = lax.broadcasted_iota(jnp.int32, (L, L), 0)
    pick = jnp.where(ids == slots[...], 1.0, 0.0).astype(bf16)
    for at in range(2):
        made[at][...] = jnp.dot(natural[at][...], pick, preferred_element_type=f32).astype(bf16)
    pick = jnp.where(ids == targets[...], 1.0, 0.0).astype(bf16)
    for at in range(2, 5):
        made[at][...] = lax.dot_general(
            pick, natural[at][...], (((0,), (0,)), ((), ())), preferred_element_type=f32
        ).astype(made[at].dtype)


def make_tables(order_slots):
    natural = natural_tables()
    targets = order_slots.reshape(8, 16, 4).transpose(1, 0, 2).reshape(1, L)
    whole = lambda shape: pl.BlockSpec(shape, lambda g: (0, 0))
    made = [jax.ShapeDtypeStruct(a.shape, bf16) for a in natural[:4]]
    made.append(jax.ShapeDtypeStruct((L, 128), f32))
    return pl.pallas_call(
        tables_kernel,
        grid=(1,),
        in_specs=[whole((1, L)), whole((1, L))] + [whole(a.shape) for a in natural],
        out_specs=[whole(a.shape) for a in made],
        out_shape=made,
        compiler_params=pltpu.CompilerParams(vmem_limit_bytes=60 * MIB),
        cost_estimate=pl.CostEstimate(flops=int(1e9), bytes_accessed=5 * MIB, transcendentals=0),
        name="make_tables",
    )(order_slots.reshape(1, L), targets, *natural)


def factors_kernel(place, orders, pairs, *refs):
    parts, (state, factors, table_out, extra, scr) = refs[:16], refs[16:]
    for r in range(16):
        state[partner(place, r)] = parts[r][0:96, :]
        extra[partner(place, r)] = parts[r][96:112, :].astype(f32)
    l_row = lax.broadcasted_iota(jnp.int32, (1, L), 1)
    for i in range(2):
        m = orders[place[1] * 64 + place[0] * 4 + 2 * i]
        scr[...] = pairs[i].astype(f32)
        a = jnp.transpose(scr[0:L, :])
        a = pltpu.roll(a, m, 1)
        table_out[2 * i] = jnp.where(l_row >= m, a, 0.0).astype(bf16)
        b = jnp.transpose(scr[1 : L + 1, :])
        table_out[2 * i + 1] = jnp.where(l_row >= L - 1 - m, b, 0.0).astype(bf16)
    degree = l_row.astype(f32)
    degree_term = degree * (degree + 1.0)
    below, angle = [[], []], [[], []]
    for d in range(16):
        x = extra[d]
        value = (x[0:8, 0:128] + x[0:8, 128:256]) + x[0:8, 256:384]
        value = jnp.concatenate([value] * 4, axis=1)
        for f in range(2):
            for s in range(2):
                below[f].append(value[f * 2 + s : f * 2 + s + 1])
                angle[f].append(value[4 + f * 2 + s : 4 + f * 2 + s + 1])
    for f in range(2):
        carried = jnp.zeros((1, L), f32)
        for s in range(32):
            under = below[f][s]
            above = below[f][s + 1] if s < 31 else jnp.zeros((1, L), f32)
            diagonal = 1.0 + under + above + angle[f][s] * degree_term
            inverse = 1.0 / (diagonal - under * carried)
            carried = above * inverse
            row = f * 32 + s
            factors[0, row : row + 1, :] = inverse
            factors[1, row : row + 1, :] = under * inverse
            factors[2, row : row + 1, :] = carried


def solve_factors(place, orders, pairs, parts):
    return pl.pallas_call(
        factors_kernel,
        grid=(1,),
        in_specs=[
            pl.BlockSpec(memory_space=pltpu.SMEM),
            pl.BlockSpec(memory_space=pltpu.SMEM),
            pl.BlockSpec((2, L + 16, NH), lambda g: (0, 0, 0)),
        ]
        + [pl.BlockSpec((112, L), lambda g: (0, 0))] * 16,
        out_specs=[
            pl.BlockSpec((16, 96, L), lambda g: (0, 0, 0)),
            pl.BlockSpec((3, 64, L), lambda g: (0, 0, 0)),
            pl.BlockSpec((4, NH, L), lambda g: (0, 0, 0)),
        ],
        out_shape=[
            jax.ShapeDtypeStruct((16, 96, L), bf16),
            jax.ShapeDtypeStruct((3, 64, L), f32),
            jax.ShapeDtypeStruct((4, NH, L), bf16),
        ],
        scratch_shapes=[pltpu.VMEM((16, 16, L), f32), pltpu.VMEM((L + 16, NH), f32)],
        compiler_params=pltpu.CompilerParams(vmem_limit_bytes=16 * MIB),
        cost_estimate=pl.CostEstimate(flops=10**6, bytes_accessed=MIB, transcendentals=0),
        name="solve_factors",
    )(place, orders, pairs, *parts)


def solve_kernel(place, orders, coef, table, factors, state, out, cs, lhs, rhs, reduced):
    for c in range(6):
        for ds in range(32):
            piece = coef[ds * 32 : ds * 32 + 32, c * 128 : c * 128 + 128]
            cs[c, ds * 33 : ds * 33 + 32, :] = piece.astype(f32)
    l_row = lax.broadcasted_iota(jnp.int32, (1, L), 1)
    for k in range(4):
        m = orders[place[1] * 64 + place[0] * 4 + k // 2 * 2]
        order = m if k % 2 == 0 else L - 1 - m
        half_sign = 0.5 * (1 - 2 * ((l_row + order) & 1)).astype(f32)
        for h in range(2):
            for c in range(6):
                for p in range(2):
                    row = ((h * 6 + c) * 2 + p) * 32
                    for jh in range(2):
                        start = h * 16 + jh * 8 + p * 4 + k
                        lhs[k % 2, row : row + 32, jh * 128 : jh * 128 + 128] = cs[
                            c, pl.ds(start, 32, stride=33), :
                        ].astype(bf16)
        res = jnp.dot(lhs[k % 2], table[k], preferred_element_type=f32)
        half = 0.5 * res[0:384] + half_sign * res[384:768]
        for cp in range(12):
            store(rhs, pl.ds(cp * 4 + k, 32, stride=49), half[cp * 32 : cp * 32 + 32])

    def factor(kind, f, s):
        return factors[kind, pl.ds(f * 32 + s, 1), :]

    def forward(step, running):
        running = list(running)
        for t in range(8):
            block = state[4 * step + t // 2, pl.ds(t % 2 * 48, 48), :].astype(f32)
            s = 8 * step + t
            for f in range(2):
                at = pl.ds(pl.multiple_of(step * 392, 8) + t * 49 + f * 24, 24)
                value = load(rhs, at) + block[f * 24 : f * 24 + 24]
                running[f] = factor(0, f, s) * value + factor(1, f, s) * running[f]
                store(reduced, pl.ds(s * 48 + f * 24, 24), running[f])
        return tuple(running)

    zero = jnp.zeros((24, L), f32)
    lax.fori_loop(0, 4, forward, (zero, zero))

    def backward(step, carried):
        d = 15 - step
        carried = list(carried)
        pieces = [None] * 4
        for s2 in (1, 0):
            s = 2 * d + s2
            for f in range(2):
                value = load(reduced, pl.ds(s * 48 + f * 24, 24))
                carried[f] = value + factor(2, f, s) * carried[f]
                pieces[s2 * 2 + f] = carried[f]
        out[d] = jnp.concatenate(pieces, axis=0).astype(bf16)
        return tuple(carried)

    lax.fori_loop(0, 16, backward, (zero, zero))


def analysis_and_solve(place, orders, coef, table, factors, state):
    small = pl.BlockSpec(memory_space=pltpu.SMEM)
    return pl.pallas_call(
        solve_kernel,
        grid=(1,),
        in_specs=[
            small,
            small,
            pl.BlockSpec((1024, 768), lambda g: (0, 0)),
            pl.BlockSpec((4, NH, L), lambda g: (0, 0, 0)),
            pl.BlockSpec((3, 64, L), lambda g: (0, 0, 0)),
            pl.BlockSpec((16, 96, L), lambda g: (0, 0, 0)),
        ],
        out_specs=pl.BlockSpec((16, 96, L), lambda g: (0, 0, 0)),
        out_shape=jax.ShapeDtypeStruct((16, 96, L), bf16),
        scratch_shapes=[
            pltpu.VMEM((6, 32 * 33, 128), f32),
            pltpu.VMEM((2, 768, NH), bf16),
            pltpu.VMEM((4, 32 * 49, 128), f32),
            pltpu.VMEM((4, 32 * 48, 128), f32),
        ],
        compiler_params=pltpu.CompilerParams(vmem_limit_bytes=32 * MIB),
        cost_estimate=pl.CostEstimate(flops=int(0.9e9), bytes_accessed=6 * MIB, transcendentals=0),
        name="analysis_and_solve",
    )(place, orders, coef, table, factors, state)


def unpack_kernel(got, out_v, out_p):
    x = got[...].astype(f32)
    low = lax.broadcasted_iota(jnp.int32, (1, 8, 1), 1) < 4
    for f, ref in enumerate((out_v, out_p)):
        for c in range(3):
            row = (f * 3 + c) * 8
            both = x[:, row : row + 8, :].reshape(8, 2, 8, L)
            a, b = both[:, 0], both[:, 1]
            ref[c, 0, 0] = jnp.where(low, a, pltpu.roll(b, 4, 1)).reshape(64, L)
            ref[c, 0, 1] = jnp.where(low, pltpu.roll(a, 4, 1), b).reshape(64, L)


def unpack_solution(got):
    shape = jax.ShapeDtypeStruct((3, 2, 2, 64, L), f32)
    field = pl.BlockSpec((3, 1, 2, 64, L), lambda s: (0, s, 0, 0, 0))
    return pl.pallas_call(
        unpack_kernel,
        grid=(2,),
        in_specs=[pl.BlockSpec((16, 48, L), lambda s: (0, s, 0))],
        out_specs=[field, field],
        out_shape=[shape, shape],
        compiler_params=pltpu.CompilerParams(vmem_limit_bytes=24 * MIB),
        cost_estimate=pl.CostEstimate(flops=10**6, bytes_accessed=5 * MIB, transcendentals=0),
        name="unpack_solution",
    )(got)


def body(
    velocity,
    vorticity,
    magnetic,
    current,
    potential,
    order_slots,
    legendre_values,
    block_lengths,
    coupling,
    angular,
):
    order_rank = lax.axis_index("order")
    shell_rank = lax.axis_index("shell")
    place = jnp.stack([shell_rank, order_rank]).astype(jnp.int32)
    shell_ids = shell_rank * 2 + jnp.arange(2, dtype=jnp.int32)
    starts = jnp.cumsum(block_lengths) - block_lengths
    is_start = jnp.any(shell_ids[:, None] == starts[None, :], axis=1)
    kappa = jnp.where(is_start[None, :], 0.0, coupling)
    rows = (order_rank & 1) * 128 + jnp.arange(128, dtype=jnp.int32)
    colatitude = math.pi * (rows.astype(f32) + 0.5) / NLAT
    weight = (math.sqrt(2.0 * math.pi) * L * math.pi / NLAT * jnp.sin(colatitude))[None, :]

    latitude, pairs = legendre_synthesis(
        place,
        order_slots,
        velocity,
        vorticity,
        magnetic,
        current,
        jnp.transpose(legendre_values, (1, 0, 2)),
    )
    incoming = lax.all_to_all(latitude, "order", 0, 0, tiled=True)

    order_after, vel_after, pot_after, _ = lax.optimization_barrier(
        (order_slots, velocity, potential, latitude)
    )
    parts = state_to_send(place, kappa, angular, vel_after, pot_after)
    tables = make_tables(order_after)
    parts = list(parts)
    parts[6:], tables = lax.optimization_barrier((parts[6:], tables))
    received = [parts[0]]
    for r in range(1, 16):
        swapped = (r & 3) * 4 + r // 4
        pairs_r = [
            (i * 8 + o, (i ^ (swapped if o & 1 else r)) * 8 + o) for i in range(16) for o in range(8)
        ]
        received.append(lax.ppermute(parts[r], ("shell", "order"), pairs_r))
    early = 12
    incoming, received[:early] = lax.optimization_barrier((incoming, received[:early]))

    coefs = grid_stage(incoming, tables, weight)
    received, coefs = lax.optimization_barrier((received, coefs))
    state, factors, table = solve_factors(place, order_slots, pairs, received)
    coefs = lax.all_to_all(
        coefs.reshape(128, 8, 768), ("shell", "order"), 0, 0, tiled=True
    ).reshape(1024, 768)
    solved = analysis_and_solve(place, order_slots, coefs, table, factors, state)
    solved = lax.all_to_all(solved, "shell", 0, 0, tiled=True)
    return tuple(unpack_solution(solved))


def solution(mesh):
    spectral = P(None, "shell", None, "order", None)
    in_specs = (
        spectral,
        spectral,
        spectral,
        spectral,
        spectral,
        P(),
        P("order", None, None),
        P(),
        P(None, "shell"),
        P(None, "shell"),
    )
    return jax.shard_map(
        body, mesh=mesh, in_specs=in_specs, out_specs=(spectral, spectral), check_vma=False
    )
```

```python
import math

import jax
import jax.numpy as jnp
import numpy as np
from jax import lax
from jax.experimental import pallas as pl
from jax.experimental.pallas import tpu as pltpu
from jax.sharding import PartitionSpec as P

L = 512
NLAT = 512
NPHI = 1024
NH = 256
f32 = jnp.float32
bf16 = jnp.bfloat16
MIB = 1 << 20


FOLD = NPHI // 2


def natural_tables():
    order = np.arange(L)[None, :]
    angles = 2.0 * np.pi * ((np.arange(FOLD + 16)[:, None] * order) % NPHI) / NPHI
    weight = np.where(order == 0, 1.0, 2.0) * (math.sqrt(2.0 * math.pi) / L)
    syn_cos = np.cos(angles) * weight
    syn_cos[FOLD + 1 :] = 0.0
    syn_sin = (-np.sin(angles) * weight)[:FOLD]
    ana_cos = np.cos(angles)[:FOLD].T / NPHI
    ana_cos[:, 0] *= 0.5
    ana_sin = -np.sin(angles)[:FOLD].T / NPHI
    last = np.repeat(np.cos(np.pi * order).T / NPHI, 128, axis=1)
    return [jnp.asarray(a.astype(jnp.bfloat16)) for a in (syn_cos, syn_sin, ana_cos, ana_sin, last)]


def partner(place, r):
    swapped = (r & 3) * 4 + r // 4
    return place[0] ^ jnp.where((place[1] & 1) == 1, swapped, r)


def load(ref, rows):
    return jnp.concatenate([ref[q, rows, :] for q in range(ref.shape[0])], axis=1)


def store(ref, rows, value):
    for q in range(ref.shape[0]):
        ref[q, rows, :] = value[:, q * 128 : q * 128 + 128]


PITCH = 33
TABLE_PITCH = 17
CHUNK = 171


def synthesis_kernel(place, orders, vel, vor, mag, cur, table, out, pairs, xs, ys, ts, packed, sems):
    step = pl.program_id(0)

    def arrival(g, q):
        source = table.at[pl.ds(q * CHUNK, CHUNK), pl.ds(g * 16, 16)]
        return pltpu.make_async_copy(source, packed.at[g, q], sems.at[g, q])

    @pl.when(step == 0)
    def _():
        for g in range(2):
            for q in range(3):
                arrival(g, q).start()

    for a, ref in enumerate((vel, vor, mag, cur)):
        for c in range(3):
            for s in range(2):
                for p in range(2):
                    row = (s * 24 + (a * 3 + c) * 2 + p) * PITCH
                    store(xs, pl.ds(row, 32), ref[c, s, p].astype(f32))

    for g in range(2):

        @pl.when(step == g)
        def _():
            for q in range(3):
                arrival(g, q).wait()
                for d in range(CHUNK):
                    at = pl.ds((q * CHUNK + d) * TABLE_PITCH, 16)
                    store(ts, at, packed[g, q, d].astype(f32))

    r = lax.broadcasted_iota(jnp.int32, (1, L), 1)
    sign_a = (1 - 2 * (r & 1)).astype(f32)

    def one_pair(i, _):
        m = orders[place[1] * 64 + step * 32 + 2 * i]
        a = load(xs, pl.ds(2 * i, 48, stride=PITCH))
        b = load(xs, pl.ds(2 * i + 1, 48, stride=PITCH))
        rows = load(ts, pl.ds(i, L, stride=TABLE_PITCH)).astype(bf16)
        a = pltpu.roll(a, (L - m) & (L - 1), 1)
        b_last = b[:, L - 1 : L]
        b = pltpu.roll(b, 1, 1)
        is_a = r < L - m
        sign_b = (1 - 2 * ((r + m) & 1)).astype(f32)
        a = jnp.where(is_a, a, 0.0)
        b = jnp.where(is_a, 0.0, b)
        lhs = jnp.concatenate([a, a * sign_a, b, b * sign_b], axis=0).astype(bf16)
        res = jnp.dot(lhs, rows, preferred_element_type=f32)
        last = b_last * load(ts, pl.ds(L * TABLE_PITCH + i, 1))
        last_sign = (1 - 2 * (m & 1)).astype(f32)
        b_n = res[96:144] + last
        b_s = res[144:192] + last * last_sign
        for k, parts in ((2 * i, (res[0:48], res[48:96])), (2 * i + 1, (b_n, b_s))):
            for h in range(2):
                for s in range(2):
                    at = pl.ds((s * 2 + h) * 24 * PITCH + k, 24, stride=PITCH)
                    store(ys, at, parts[h][s * 24 : s * 24 + 24])
        return 0

    lax.fori_loop(0, 16, one_pair, 0, unroll=16)
    for sh in range(4):
        for jh in range(2):
            for cp in range(24):
                row = (sh * 24 + cp) * PITCH
                out[sh * 2 + jh, cp] = ys[jh, row : row + 32, :].astype(bf16)

    @pl.when(step == place[0] // 8)
    def _():
        for i in range(2):
            at = (place[0] & 7) * 2 + i
            pairs[i, 0:L, :] = load(ts, pl.ds(at, L, stride=TABLE_PITCH)).astype(bf16)
            last = load(ts, pl.ds(L * TABLE_PITCH + at, 1))
            pairs[i, L : L + 16, :] = jnp.broadcast_to(last, (16, NH)).astype(bf16)


def legendre_synthesis(place, orders, velocity, vorticity, magnetic, current, table):
    field = pl.BlockSpec((3, 2, 2, 32, L), lambda g, place, low: (0, 0, 0, g, 0))
    return pl.pallas_call(
        synthesis_kernel,
        grid_spec=pltpu.PrefetchScalarGridSpec(
            num_scalar_prefetch=2,
            grid=(2,),
            in_specs=[field] * 4 + [pl.BlockSpec(memory_space=pl.ANY)],
            out_specs=[
                pl.BlockSpec((8, 24, 32, 128), lambda g, place, low: (0, 0, g, 0)),
                pl.BlockSpec((2, L + 16, NH), lambda g, place, low: (0, 0, 0)),
            ],
            scratch_shapes=[
                pltpu.VMEM((4, 48 * PITCH, 128), f32),
                pltpu.VMEM((2, 96 * PITCH, 128), f32),
                pltpu.VMEM((2, (L + 1) * TABLE_PITCH + 7, 128), f32),
                pltpu.VMEM((2, 3, CHUNK, 16, NH), bf16),
                pltpu.SemaphoreType.DMA((2, 3)),
            ],
        ),
        out_shape=[
            jax.ShapeDtypeStruct((8, 24, 64, 128), bf16),
            jax.ShapeDtypeStruct((2, L + 16, NH), bf16),
        ],
        compiler_params=pltpu.CompilerParams(vmem_limit_bytes=60 * MIB),
        cost_estimate=pl.CostEstimate(flops=int(1.6e9), bytes_accessed=15 * MIB, transcendentals=0),
        name="legendre_synthesis",
    )(place, orders, velocity, vorticity, magnetic, current, table)


def state_kernel(place, kappa, angular, vel, pot, *refs):
    outs, scr = refs[:16], refs[16]
    for f, ref in enumerate((vel, pot)):
        for c in range(3):
            for s in range(2):
                for p in range(2):
                    x = ref[c, s, p].astype(f32)
                    row = s * 48 + ((f * 3 + c) * 2 + p) * 4
                    for d in range(16):
                        scr[d, row : row + 4, :] = x[4 * d : 4 * d + 4]
    lane = lax.broadcasted_iota(jnp.int32, (1, L), 1)
    lines = []
    for ref in (kappa, angular):
        for f in range(2):
            for s in range(2):
                value = jnp.full((1, L), ref[f, s], f32)
                high = value.astype(bf16).astype(f32)
                rest = value - high
                mid = rest.astype(bf16).astype(f32)
                low = rest - mid
                lines.append(jnp.where(lane < 128, high, jnp.where(lane < 256, mid, low)))
    extra = jnp.concatenate(lines + [jnp.zeros((8, L), f32)], axis=0).astype(bf16)
    for r in range(16):
        outs[r][0:96, :] = scr[partner(place, r)].astype(bf16)
        outs[r][96:112, :] = extra


def state_to_send(place, kappa, angular, velocity, potential):
    field = pl.BlockSpec((3, 2, 2, 64, L), lambda g: (0, 0, 0, 0, 0))
    small = pl.BlockSpec(memory_space=pltpu.SMEM)
    return pl.pallas_call(
        state_kernel,
        grid=(1,),
        in_specs=[small, small, small, field, field],
        out_specs=[pl.BlockSpec((112, L), lambda g: (0, 0))] * 16,
        out_shape=[jax.ShapeDtypeStruct((112, L), bf16)] * 16,
        scratch_shapes=[pltpu.VMEM((16, 96, L), f32)],
        compiler_params=pltpu.CompilerParams(vmem_limit_bytes=60 * MIB),
        cost_estimate=pl.CostEstimate(flops=10**6, bytes_accessed=4 * MIB, transcendentals=0),
        name="state_to_send",
    )(place, kappa, angular, velocity, potential)


def products(x):
    u, w, b, j = x[0:3], x[3:6], x[6:9], x[9:12]

    def cross(p, q):
        return [
            p[1] * q[2] - p[2] * q[1],
            p[2] * q[0] - p[0] * q[2],
            p[0] * q[1] - p[1] * q[0],
        ]

    uw, jb, ub = cross(u, w), cross(j, b), cross(u, b)
    return [uw[0] + jb[0] + 2.0 * u[1], uw[1] + jb[1] - 2.0 * u[0], uw[2] + jb[2]] + ub


def grid_kernel(lat, syn_cos, syn_sin, ana_cos, ana_sin, ana_last, weight, out, wide, even, odd, middle):
    step = pl.program_id(0)

    @pl.when(step == 0)
    def _():
        for c in range(12):
            for p in range(2):
                rows_p = lat[:, 2 * c + p].reshape(512, 128)
                wide[p * 512 : p * 512 + 512, c * 128 : c * 128 + 128] = rows_p
        g = jnp.dot(syn_cos[...], wide[0:512, :], preferred_element_type=f32)
        d = jnp.dot(syn_sin[...], wide[512:1024, :], preferred_element_type=f32)
        cols = [slice(c * 128, c * 128 + 128) for c in range(12)]
        here = products([g[0:FOLD, at] + d[:, at] for at in cols])
        mirror = products([g[0:FOLD, at] - d[:, at] for at in cols])
        edge = products([g[FOLD : FOLD + 8, at] for at in cols])
        for c in range(6):
            even[:, cols[c]] = (here[c] + mirror[c]).astype(bf16)
            odd[:, cols[c]] = (here[c] - mirror[c]).astype(bf16)
            middle[:, cols[c]] = edge[c]

    @pl.when(step > 0)
    def _():
        real = jnp.dot(ana_cos[...], even[...], preferred_element_type=f32)
        imag = jnp.dot(ana_sin[...], odd[...], preferred_element_type=f32)
        sign = ana_last[...]
        low = lax.broadcasted_iota(jnp.int32, (1, 8, 1), 1) < 4
        for c in range(6):
            at = slice(c * 128, c * 128 + 128)
            a = (real[:, at] + sign * middle[0:1, at]) * weight[...]
            b = imag[:, at] * weight[...]
            a, b = a.reshape(32, 8, 128), b.reshape(32, 8, 128)
            first = jnp.where(low, a, pltpu.roll(b, 4, 1))
            second = jnp.where(low, pltpu.roll(a, 4, 1), b)
            both = jnp.stack([first, second], axis=1).reshape(512, 128)
            out[:, at] = both.astype(bf16)


def grid_stage(lat, tables, weight):
    rows = 256
    by_slots = pl.BlockSpec((rows, FOLD), lambda i: (jnp.maximum(i - 1, 0), 0))
    return pl.pallas_call(
        grid_kernel,
        grid=(3,),
        in_specs=[
            pl.BlockSpec((8, 24, 64, 128), lambda i: (0, 0, 0, 0)),
            pl.BlockSpec((FOLD + 16, L), lambda i: (0, 0)),
            pl.BlockSpec((FOLD, L), lambda i: (0, 0)),
            by_slots,
            by_slots,
            pl.BlockSpec((rows, 128), lambda i: (jnp.maximum(i - 1, 0), 0)),
            pl.BlockSpec((1, 128), lambda i: (0, 0)),
        ],
        out_specs=pl.BlockSpec((2 * rows, 768), lambda i: (jnp.maximum(i - 1, 0), 0)),
        out_shape=jax.ShapeDtypeStruct((1024, 768), bf16),
        scratch_shapes=[
            pltpu.VMEM((1024, 1536), bf16),
            pltpu.VMEM((FOLD, 768), bf16),
            pltpu.VMEM((FOLD, 768), bf16),
            pltpu.VMEM((8, 768), f32),
        ],
        compiler_params=pltpu.CompilerParams(vmem_limit_bytes=60 * MIB),
        cost_estimate=pl.CostEstimate(flops=int(2.4e9), bytes_accessed=7 * MIB, transcendentals=0),
        name="grid_stage",
    )(lat, *tables, weight)


def tables_kernel(slots, targets, *refs):
    natural, made = refs[:5], refs[5:]
    ids = lax.broadcasted_iota(jnp.int32, (L, L), 0)
    pick = jnp.where(ids == slots[...], 1.0, 0.0).astype(bf16)
    for at in range(2):
        made[at][...] = jnp.dot(natural[at][...], pick, preferred_element_type=f32).astype(bf16)
    pick = jnp.where(ids == targets[...], 1.0, 0.0).astype(bf16)
    for at in range(2, 5):
        made[at][...] = lax.dot_general(
            pick, natural[at][...], (((0,), (0,)), ((), ())), preferred_element_type=f32
        ).astype(made[at].dtype)


def make_tables(order_slots):
    natural = natural_tables()
    targets = order_slots.reshape(8, 16, 4).transpose(1, 0, 2).reshape(1, L)
    whole = lambda shape: pl.BlockSpec(shape, lambda g: (0, 0))
    made = [jax.ShapeDtypeStruct(a.shape, bf16) for a in natural[:4]]
    made.append(jax.ShapeDtypeStruct((L, 128), f32))
    return pl.pallas_call(
        tables_kernel,
        grid=(1,),
        in_specs=[whole((1, L)), whole((1, L))] + [whole(a.shape) for a in natural],
        out_specs=[whole(a.shape) for a in made],
        out_shape=made,
        compiler_params=pltpu.CompilerParams(vmem_limit_bytes=60 * MIB),
        cost_estimate=pl.CostEstimate(flops=int(1e9), bytes_accessed=5 * MIB, transcendentals=0),
        name="make_tables",
    )(order_slots.reshape(1, L), targets, *natural)


def factors_kernel(place, orders, pairs, *refs):
    parts, (state, factors, table_out, extra, scr) = refs[:16], refs[16:]
    for r in range(16):
        state[partner(place, r)] = parts[r][0:96, :]
        extra[partner(place, r)] = parts[r][96:112, :].astype(f32)
    l_row = lax.broadcasted_iota(jnp.int32, (1, L), 1)
    for i in range(2):
        m = orders[place[1] * 64 + place[0] * 4 + 2 * i]
        scr[...] = pairs[i].astype(f32)
        a = jnp.transpose(scr[0:L, :])
        a = pltpu.roll(a, m, 1)
        table_out[2 * i] = jnp.where(l_row >= m, a, 0.0).astype(bf16)
        b = jnp.transpose(scr[1 : L + 1, :])
        table_out[2 * i + 1] = jnp.where(l_row >= L - 1 - m, b, 0.0).astype(bf16)
    degree = l_row.astype(f32)
    degree_term = degree * (degree + 1.0)
    below, angle = [[], []], [[], []]
    for d in range(16):
        x = extra[d]
        value = (x[0:8, 0:128] + x[0:8, 128:256]) + x[0:8, 256:384]
        value = jnp.concatenate([value] * 4, axis=1)
        for f in range(2):
            for s in range(2):
                below[f].append(value[f * 2 + s : f * 2 + s + 1])
                angle[f].append(value[4 + f * 2 + s : 4 + f * 2 + s + 1])
    for f in range(2):
        carried = jnp.zeros((1, L), f32)
        for s in range(32):
            under = below[f][s]
            above = below[f][s + 1] if s < 31 else jnp.zeros((1, L), f32)
            diagonal = 1.0 + under + above + angle[f][s] * degree_term
            inverse = 1.0 / (diagonal - under * carried)
            carried = above * inverse
            row = f * 32 + s
            factors[0, row : row + 1, :] = inverse
            factors[1, row : row + 1, :] = under * inverse
            factors[2, row : row + 1, :] = carried


def solve_factors(place, orders, pairs, parts):
    return pl.pallas_call(
        factors_kernel,
        grid=(1,),
        in_specs=[
            pl.BlockSpec(memory_space=pltpu.SMEM),
            pl.BlockSpec(memory_space=pltpu.SMEM),
            pl.BlockSpec((2, L + 16, NH), lambda g: (0, 0, 0)),
        ]
        + [pl.BlockSpec((112, L), lambda g: (0, 0))] * 16,
        out_specs=[
            pl.BlockSpec((16, 96, L), lambda g: (0, 0, 0)),
            pl.BlockSpec((3, 64, L), lambda g: (0, 0, 0)),
            pl.BlockSpec((4, NH, L), lambda g: (0, 0, 0)),
        ],
        out_shape=[
            jax.ShapeDtypeStruct((16, 96, L), bf16),
            jax.ShapeDtypeStruct((3, 64, L), f32),
            jax.ShapeDtypeStruct((4, NH, L), bf16),
        ],
        scratch_shapes=[pltpu.VMEM((16, 16, L), f32), pltpu.VMEM((L + 16, NH), f32)],
        compiler_params=pltpu.CompilerParams(vmem_limit_bytes=16 * MIB),
        cost_estimate=pl.CostEstimate(flops=10**6, bytes_accessed=MIB, transcendentals=0),
        name="solve_factors",
    )(place, orders, pairs, *parts)


def solve_kernel(place, orders, coef, table, factors, state, out, cs, lhs, rhs, reduced):
    for c in range(6):
        for ds in range(32):
            piece = coef[ds * 32 : ds * 32 + 32, c * 128 : c * 128 + 128]
            cs[c, ds * 33 : ds * 33 + 32, :] = piece.astype(f32)
    l_row = lax.broadcasted_iota(jnp.int32, (1, L), 1)
    for k in range(4):
        m = orders[place[1] * 64 + place[0] * 4 + k // 2 * 2]
        order = m if k % 2 == 0 else L - 1 - m
        half_sign = 0.5 * (1 - 2 * ((l_row + order) & 1)).astype(f32)
        for h in range(2):
            for c in range(6):
                for p in range(2):
                    row = ((h * 6 + c) * 2 + p) * 32
                    for jh in range(2):
                        start = h * 16 + jh * 8 + p * 4 + k
                        lhs[k % 2, row : row + 32, jh * 128 : jh * 128 + 128] = cs[
                            c, pl.ds(start, 32, stride=33), :
                        ].astype(bf16)
        res = jnp.dot(lhs[k % 2], table[k], preferred_element_type=f32)
        half = 0.5 * res[0:384] + half_sign * res[384:768]
        for cp in range(12):
            store(rhs, pl.ds(cp * 4 + k, 32, stride=49), half[cp * 32 : cp * 32 + 32])

    def factor(kind, f, s):
        return factors[kind, pl.ds(f * 32 + s, 1), :]

    def forward(step, running):
        running = list(running)
        for t in range(8):
            block = state[4 * step + t // 2, pl.ds(t % 2 * 48, 48), :].astype(f32)
            s = 8 * step + t
            for f in range(2):
                at = pl.ds(pl.multiple_of(step * 392, 8) + t * 49 + f * 24, 24)
                value = load(rhs, at) + block[f * 24 : f * 24 + 24]
                running[f] = factor(0, f, s) * value + factor(1, f, s) * running[f]
                store(reduced, pl.ds(s * 48 + f * 24, 24), running[f])
        return tuple(running)

    zero = jnp.zeros((24, L), f32)
    lax.fori_loop(0, 4, forward, (zero, zero))

    def backward(step, carried):
        d = 15 - step
        carried = list(carried)
        pieces = [None] * 4
        for s2 in (1, 0):
            s = 2 * d + s2
            for f in range(2):
                value = load(reduced, pl.ds(s * 48 + f * 24, 24))
                carried[f] = value + factor(2, f, s) * carried[f]
                pieces[s2 * 2 + f] = carried[f]
        out[d] = jnp.concatenate(pieces, axis=0).astype(bf16)
        return tuple(carried)

    lax.fori_loop(0, 16, backward, (zero, zero))


def analysis_and_solve(place, orders, coef, table, factors, state):
    small = pl.BlockSpec(memory_space=pltpu.SMEM)
    return pl.pallas_call(
        solve_kernel,
        grid=(1,),
        in_specs=[
            small,
            small,
            pl.BlockSpec((1024, 768), lambda g: (0, 0)),
            pl.BlockSpec((4, NH, L), lambda g: (0, 0, 0)),
            pl.BlockSpec((3, 64, L), lambda g: (0, 0, 0)),
            pl.BlockSpec((16, 96, L), lambda g: (0, 0, 0)),
        ],
        out_specs=pl.BlockSpec((16, 96, L), lambda g: (0, 0, 0)),
        out_shape=jax.ShapeDtypeStruct((16, 96, L), bf16),
        scratch_shapes=[
            pltpu.VMEM((6, 32 * 33, 128), f32),
            pltpu.VMEM((2, 768, NH), bf16),
            pltpu.VMEM((4, 32 * 49, 128), f32),
            pltpu.VMEM((4, 32 * 48, 128), f32),
        ],
        compiler_params=pltpu.CompilerParams(vmem_limit_bytes=32 * MIB),
        cost_estimate=pl.CostEstimate(flops=int(0.9e9), bytes_accessed=6 * MIB, transcendentals=0),
        name="analysis_and_solve",
    )(place, orders, coef, table, factors, state)


def unpack_kernel(got, out_v, out_p):
    x = got[...].astype(f32)
    low = lax.broadcasted_iota(jnp.int32, (1, 8, 1), 1) < 4
    for f, ref in enumerate((out_v, out_p)):
        for c in range(3):
            row = (f * 3 + c) * 8
            both = x[:, row : row + 8, :].reshape(8, 2, 8, L)
            a, b = both[:, 0], both[:, 1]
            ref[c, 0, 0] = jnp.where(low, a, pltpu.roll(b, 4, 1)).reshape(64, L)
            ref[c, 0, 1] = jnp.where(low, pltpu.roll(a, 4, 1), b).reshape(64, L)


def unpack_solution(got):
    shape = jax.ShapeDtypeStruct((3, 2, 2, 64, L), f32)
    field = pl.BlockSpec((3, 1, 2, 64, L), lambda s: (0, s, 0, 0, 0))
    return pl.pallas_call(
        unpack_kernel,
        grid=(2,),
        in_specs=[pl.BlockSpec((16, 48, L), lambda s: (0, s, 0))],
        out_specs=[field, field],
        out_shape=[shape, shape],
        compiler_params=pltpu.CompilerParams(vmem_limit_bytes=24 * MIB),
        cost_estimate=pl.CostEstimate(flops=10**6, bytes_accessed=5 * MIB, transcendentals=0),
        name="unpack_solution",
    )(got)


def body(
    velocity,
    vorticity,
    magnetic,
    current,
    potential,
    order_slots,
    legendre_values,
    block_lengths,
    coupling,
    angular,
):
    order_rank = lax.axis_index("order")
    shell_rank = lax.axis_index("shell")
    place = jnp.stack([shell_rank, order_rank]).astype(jnp.int32)
    shell_ids = shell_rank * 2 + jnp.arange(2, dtype=jnp.int32)
    starts = jnp.cumsum(block_lengths) - block_lengths
    is_start = jnp.any(shell_ids[:, None] == starts[None, :], axis=1)
    kappa = jnp.where(is_start[None, :], 0.0, coupling)
    rows = (order_rank & 1) * 128 + jnp.arange(128, dtype=jnp.int32)
    colatitude = math.pi * (rows.astype(f32) + 0.5) / NLAT
    weight = (math.sqrt(2.0 * math.pi) * L * math.pi / NLAT * jnp.sin(colatitude))[None, :]

    latitude, pairs = legendre_synthesis(
        place,
        order_slots,
        velocity,
        vorticity,
        magnetic,
        current,
        jnp.transpose(legendre_values, (1, 0, 2)),
    )
    incoming = lax.all_to_all(latitude, "order", 0, 0, tiled=True)

    order_after, vel_after, pot_after, _ = lax.optimization_barrier(
        (order_slots, velocity, potential, latitude)
    )
    parts = state_to_send(place, kappa, angular, vel_after, pot_after)
    tables = make_tables(order_after)
    parts = list(parts)
    parts[6:], tables = lax.optimization_barrier((parts[6:], tables))
    received = [parts[0]]
    for r in range(1, 16):
        swapped = (r & 3) * 4 + r // 4
        pairs_r = [
            (i * 8 + o, (i ^ (swapped if o & 1 else r)) * 8 + o) for i in range(16) for o in range(8)
        ]
        received.append(lax.ppermute(parts[r], ("shell", "order"), pairs_r))
    early = 15
    incoming, received[:early] = lax.optimization_barrier((incoming, received[:early]))

    coefs = grid_stage(incoming, tables, weight)
    received, coefs = lax.optimization_barrier((received, coefs))
    state, factors, table = solve_factors(place, order_slots, pairs, received)
    coefs = lax.all_to_all(
        coefs.reshape(128, 8, 768), ("shell", "order"), 0, 0, tiled=True
    ).reshape(1024, 768)
    solved = analysis_and_solve(place, order_slots, coefs, table, factors, state)
    solved = lax.all_to_all(solved, "shell", 0, 0, tiled=True)
    return tuple(unpack_solution(solved))


def solution(mesh):
    spectral = P(None, "shell", None, "order", None)
    in_specs = (
        spectral,
        spectral,
        spectral,
        spectral,
        spectral,
        P(),
        P("order", None, None),
        P(),
        P(None, "shell"),
        P(None, "shell"),
    )
    return jax.shard_map(
        body, mesh=mesh, in_specs=in_specs, out_specs=(spectral, spectral), check_vma=False
    )
```
